128 devices in a mesh: gx: 8 (over x, core), gy: 16 (over z, y).
Axes of the slice: x: 4, y: 4, z: 4, core: 2. Of those that a mesh axis runs over, the one named last changes fastest.
Arguments:
- sources: float32 [3, 2, 2, 64, 512, 128], P(None, None, None, 'gx', 'gy'), may hold values from -15 to 15
- masks: int32 [3, 64, 512, 128], P(None, 'gx', 'gy'), may hold values 0 or 1
- absorption: float32 [64, 512, 128], P('gx', 'gy'), may hold values from 4 to 8
- plane_basis: float32 [8, 64, 512], P(None, 'gx', 'gy'), may hold values from -0.625 to 0.625
- depth_basis: float32 [8, 128], replicated, may hold values from -0.75 to 0.75
- coupling_blocks: bfloat16 [8, 16, 5, 128, 128], P('gx', 'gy'), may hold values from -0.125 to 0.125
- coupling_index: int32 [8, 16, 5], replicated, may hold values from 0 to 127
Outputs:
- solution: float32 [3, 2, 2, 64, 512, 128], P(None, None, None, 'gx', 'gy')
- residual: float32 [3, 2, 2, 64, 512, 128], P(None, None, None, 'gx', 'gy')
The draws below stay inside these ranges and needn't reach their ends.
Inputs may be any that keep to these rules, and one draw needn't show every extreme that they name: `coupling_index`: tile numbers are p 16 + q for tile (p, q); entries may repeat.
All inputs are finite; a program needn't handle non-finite values. No bound on the sum of `masks` on one device may be relied on, other than what follows from the above.
Results may differ from the reference program's by a relative error of at most 0.0034.
Values may be sent and summed in bfloat16 or wider, within the bound.
No kernel may reach another device: no remote copies, remote signals or barrier semaphores. Data moves between devices by JAX's collectives and lax.ppermute only.
A program may use at most 128 MiB of HBM per device.

```python
import math
import jax
import jax.numpy as jnp
from jax import lax

VARIANTS = 3
RHS = 2
CX = 8
CY = 32
NZ = 128
OV = 2
LSTEPS = 3
SWEEPS = 3
ITERS = 2
PLANE_MODES = 8
DEPTH_MODES = 8
NNZ = 5
COARSE = 128
TILES = 128
NX = 64
NY = 512
N_GX = 8
N_GY = 16


def draw_sources(key, part):
    key = jax.random.fold_in(key, 11)
    shape = (VARIANTS, RHS, 2, NX, NY, NZ)
    across = 1.0 + 2.0 * jnp.arange(NX, dtype=jnp.float32) / max(NX - 1, 1)
    along = 1.0 + 2.0 * jnp.arange(NY, dtype=jnp.float32) / max(NY - 1, 1)
    ramp = across[:, None, None] * along[None, :, None] / 3.0
    values = jnp.clip(jax.random.normal(key, shape, jnp.float32), -5.0, 5.0)
    return values * ramp


def set_ends(drawn, rng, smallest, largest):
    index_at = [jax.random.randint(jax.random.fold_in(rng, axis), (), 0, length) for axis, length in enumerate(drawn.shape)]
    widest = drawn.shape.index(max(drawn.shape))
    neighbour = index_at[:widest] + [(index_at[widest] + 1) % drawn.shape[widest]] + index_at[widest + 1:]
    return drawn.at[tuple(index_at)].set(smallest).at[tuple(neighbour)].set(largest)


def levels(stream_key, dims, cuts, least, largest):
    def one(dim, shards_of):
        steps = jax.random.uniform(jax.random.fold_in(jax.random.fold_in(stream_key, 6), dim), (shards_of,), jnp.float32, least / len(cuts), largest / len(cuts))
        return jnp.repeat(jnp.exp(steps), dims[dim] // shards_of).reshape((-1,) + (1,) * (len(dims) - dim - 1))

    gain = one(*cuts[0])
    for cut in cuts[1:]:
        gain = gain * one(*cut)
    return gain


def scatter_about(rng, dims, width, most, shards=(), kind=jnp.bfloat16):
    values = width * jax.random.normal(rng, dims, jnp.float32)
    if shards:
        values = values * levels(rng, dims, shards, -0.22, 0.18)
    return jnp.clip(values, -most, most).astype(kind)


def setup_inputs(seed: int = 0) -> dict:
    splits = jax.random.split(jax.random.key(seed), 8)
    sources = draw_sources(jax.random.fold_in(splits[7], 71), 0)
    masks = set_ends((jax.random.randint(splits[1], (VARIANTS, NX, NY, NZ), 0, 2) < 1).astype(jnp.int32), jax.random.fold_in(splits[1], 1), 0, 1)
    absorption = jnp.clip(jnp.exp(math.log(8.0) - 0.6931472 * jax.random.uniform(splits[2], (NX, NY, NZ), jnp.float32) ** levels(splits[2], (NX, NY, NZ), ((0, 8), (1, 16)), -0.2, 0.2)), 4.0, 8.0)
    plane_basis = scatter_about(splits[3], (PLANE_MODES, NX, NY), (6 * (CX * CY) ** 0.5) ** -0.5, 0.625, ((1, 8), (2, 16)), jnp.float32)
    depth_basis = scatter_about(splits[4], (DEPTH_MODES, NZ), (5 * NZ ** 0.5) ** -0.5, 0.75, (), jnp.float32)
    coupling_blocks = scatter_about(splits[5], (N_GX, N_GY, NNZ, COARSE, COARSE), (4 * NNZ * COARSE) ** -0.5, 0.125, ((0, 8), (1, 16)))
    coupling_index = set_ends(jax.random.randint(splits[6], (N_GX, N_GY, NNZ), 0, TILES), jax.random.fold_in(splits[6], 1), 0, TILES - 1).astype(jnp.int32)
    return {"sources": sources, "masks": masks, "absorption": absorption, "plane_basis": plane_basis, "depth_basis": depth_basis, "coupling_blocks": coupling_blocks, "coupling_index": coupling_index}


HIGH = lax.Precision.HIGHEST
wave_sq = 0.5
background = 1.0
contrast = 2.0


def neighbours(field):
    widths = [(0, 0)] * (field.ndim - 3) + [(1, 1)] * 3
    padded = jnp.pad(field, widths)
    total = padded[..., 2:, 1:-1, 1:-1] + padded[..., :-2, 1:-1, 1:-1]
    total = total + padded[..., 1:-1, 2:, 1:-1] + padded[..., 1:-1, :-2, 1:-1]
    total = total + padded[..., 1:-1, 1:-1, 2:] + padded[..., 1:-1, 1:-1, :-2]
    return total


def apply_operator(field, diag_re, diag_im):
    near = neighbours(field)
    part_re = diag_re[:, None] * field[:, :, 0] - diag_im * field[:, :, 1] - near[:, :, 0]
    part_im = diag_re[:, None] * field[:, :, 1] + diag_im * field[:, :, 0] - near[:, :, 1]
    return jnp.stack([part_re, part_im], axis=2)


def inverses(diag_re, diag_im):
    inside = jnp.broadcast_to(diag_im > 1.0, diag_re.shape)
    modulus = jnp.where(inside, diag_re * diag_re + diag_im * diag_im, 1.0)
    inv_re = jnp.where(inside, diag_re / modulus, 0.0)
    inv_im = jnp.where(inside, -diag_im / modulus, 0.0)
    return inv_re, inv_im


def jacobi(source, inv_re, inv_im):
    field = jnp.zeros_like(source)
    for step in range(LSTEPS):
        total = source + neighbours(field)
        new_re = inv_re[:, None] * total[:, :, 0] - inv_im[:, None] * total[:, :, 1]
        new_im = inv_re[:, None] * total[:, :, 1] + inv_im[:, None] * total[:, :, 0]
        field = jnp.stack([new_re, new_im], axis=2)
    return field


def local_solves(residual, diag_re, diag_im):
    tile_x = NX // N_GX
    tile_y = NY // N_GY
    res_pad = jnp.pad(residual, [(0, 0)] * 3 + [(OV, OV), (OV, OV), (0, 0)])
    re_pad = jnp.pad(diag_re, [(0, 0), (OV, OV), (OV, OV), (0, 0)])
    im_pad = jnp.pad(diag_im, [(OV, OV), (OV, OV), (0, 0)])
    zero = jnp.zeros((), jnp.int32)

    def one_tile(tile):
        start_x = ((tile // N_GY) * tile_x).astype(jnp.int32)
        start_y = ((tile % N_GY) * tile_y).astype(jnp.int32)
        ext_x = tile_x + 2 * OV
        ext_y = tile_y + 2 * OV
        source = lax.dynamic_slice(res_pad, (zero, zero, zero, start_x, start_y, zero), (VARIANTS, RHS, 2, ext_x, ext_y, NZ))
        part_re = lax.dynamic_slice(re_pad, (zero, start_x, start_y, zero), (VARIANTS, ext_x, ext_y, NZ))
        part_im = lax.dynamic_slice(im_pad, (start_x, start_y, zero), (ext_x, ext_y, NZ))
        inv_re, inv_im = inverses(part_re, part_im)
        field = jacobi(source, inv_re, inv_im)
        return field[:, :, :, OV:OV + tile_x, OV:OV + tile_y]

    tiles = lax.map(one_tile, jnp.arange(N_GX * N_GY, dtype=jnp.int32))
    tiles = tiles.reshape(N_GX, N_GY, VARIANTS, RHS, 2, tile_x, tile_y, NZ)
    return tiles.transpose(2, 3, 4, 0, 5, 1, 6, 7).reshape(VARIANTS, RHS, 2, NX, NY, NZ)


def restrict(field, plane_basis, depth_basis):
    tile_x = NX // N_GX
    tile_y = NY // N_GY
    split = field.reshape(VARIANTS, RHS, 2, N_GX, tile_x, N_GY, tile_y, NZ)
    plane = plane_basis.reshape(PLANE_MODES, N_GX, tile_x, N_GY, tile_y)
    depthwise = jnp.einsum("vrcpxqyz,bz->vrcpxqyb", split, depth_basis, precision=HIGH)
    coarse = jnp.einsum("vrcpxqyb,apxqy->pqvrcab", depthwise, plane, precision=HIGH)
    return coarse.reshape(N_GX * N_GY, VARIANTS * RHS, COARSE)


def prolong(coarse, plane_basis, depth_basis):
    tile_x = NX // N_GX
    tile_y = NY // N_GY
    split = coarse.reshape(N_GX, N_GY, VARIANTS, RHS, 2, PLANE_MODES, DEPTH_MODES)
    plane = plane_basis.reshape(PLANE_MODES, N_GX, tile_x, N_GY, tile_y)
    planar = jnp.einsum("pqvrcab,apxqy->vrcpxqyb", split, plane, precision=HIGH)
    field = jnp.einsum("vrcpxqyb,bz->vrcpxqyz", planar, depth_basis, precision=HIGH)
    return field.reshape(VARIANTS, RHS, 2, NX, NY, NZ)


def coarse_solve(coarse_residual, coupling_blocks, coupling_index):
    blocks = coupling_blocks.reshape(TILES, NNZ, COARSE, COARSE).astype(jnp.float32)
    index = coupling_index.reshape(TILES, NNZ).astype(jnp.int32)
    iterate = coarse_residual
    for sweep in range(SWEEPS):
        rounded = lax.optimization_barrier(iterate.astype(jnp.bfloat16)).astype(jnp.float32)
        chosen = rounded[index]
        iterate = coarse_residual - jnp.einsum("tjfi,tjoi->tfo", chosen, blocks, precision=HIGH)
    return iterate


def reference(sources, masks, absorption, plane_basis, depth_basis, coupling_blocks, coupling_index):
    diag_re = 6.0 - wave_sq * (background + contrast * masks.astype(jnp.float32))
    diag_im = absorption
    solution = jnp.zeros_like(sources)
    residual = sources
    for outer in range(ITERS):
        local = local_solves(residual, diag_re, diag_im)
        coarse = coarse_solve(restrict(residual, plane_basis, depth_basis), coupling_blocks, coupling_index)
        direction = local + prolong(coarse, plane_basis, depth_basis)
        image = apply_operator(direction, diag_re, diag_im)
        img_re, img_im = image[:, :, 0], image[:, :, 1]
        res_re, res_im = residual[:, :, 0], residual[:, :, 1]
        dot_re = jnp.sum(img_re * res_re + img_im * res_im, axis=(2, 3, 4))
        dot_im = jnp.sum(img_re * res_im - img_im * res_re, axis=(2, 3, 4))
        energy = jnp.sum(img_re * img_re + img_im * img_im, axis=(2, 3, 4))
        alpha_re = (dot_re / energy)[:, :, None, None, None]
        alpha_im = (dot_im / energy)[:, :, None, None, None]
        dir_re, dir_im = direction[:, :, 0], direction[:, :, 1]
        solution = solution + jnp.stack([alpha_re * dir_re - alpha_im * dir_im, alpha_re * dir_im + alpha_im * dir_re], axis=2)
        residual = residual - jnp.stack([alpha_re * img_re - alpha_im * img_im, alpha_re * img_im + alpha_im * img_re], axis=2)
    return solution, residual
```

```python
import functools

import jax
import jax.numpy as jnp
from jax import lax
from jax.experimental import pallas as pl
from jax.experimental.pallas import tpu as pltpu
from jax.sharding import PartitionSpec as P

F32 = jnp.float32
BF16 = jnp.bfloat16
TX, TY, NZ = 8, 32, 128
CELLS = TX * TY
TILES = 128
NNZ = 5
FIELDS = 6
VMEM = 60 * 1024 * 1024
BOTH = ("gx", "gy")


def params(**more):
    return pltpu.CompilerParams(vmem_limit_bytes=VMEM, **more)


def iota(shape, dim):
    return lax.broadcasted_iota(jnp.int32, shape, dim)


def split(x):
    hi = x.astype(BF16)
    return hi, (x - hi.astype(F32)).astype(BF16)


def mm(a, b):
    return lax.dot_general(a, b, (((1,), (0,)), ((), ())), preferred_element_type=F32)


def mm_nt(a, b):
    return lax.dot_general(a, b, (((1,), (1,)), ((), ())), preferred_element_type=F32)


def depth_matrix(depth):
    tall = jnp.concatenate([depth] * 8, axis=0)
    none = jnp.zeros_like(tall)
    return jnp.concatenate(
        [jnp.concatenate([tall, none], axis=1), jnp.concatenate([none, tall], axis=1)], axis=0
    )


def restrict_rows(re, im, pe, rows):
    cells = jnp.concatenate([re.reshape(CELLS, NZ), im.reshape(CELLS, NZ)], axis=1)
    hi, lo = split(cells)
    both = mm_nt(hi, rows)
    part = both[:, :128] + both[:, 128:] + mm_nt(lo, rows[:128])
    return jnp.sum(pe * part, axis=0, keepdims=True)


def pack_low(cells):
    sub = iota((4, 8, NZ), 1)
    return jnp.where(sub < 4, cells[0:4, 0:8], pltpu.roll(cells[4:8, 0:8], 4, 1))


def pack_high(cells):
    sub = iota((4, 8, NZ), 1)
    return jnp.where(sub >= 4, cells[0:4, 24:32], pltpu.roll(cells[4:8, 24:32], 4, 1))


def halo_rows(low, high, x):
    sub = iota((8, NZ), 0)
    if x < 4:
        return jnp.where(sub < 4, low[x], high[x])
    return jnp.where(sub < 4, pltpu.roll(low[x - 4], 4, 0), pltpu.roll(high[x - 4], 4, 0))


def wide_plane(cells, low, high, x):
    return jnp.concatenate([cells[x], halo_rows(low, high, x)], axis=0)


def first_kernel(src, masks, absorb, plane, depth, y0b, y0, pe, ylo, yhi, rows):
    f = pl.program_id(0)

    @pl.when(f == 0)
    def _():
        pick = (iota((8, 128), 1) // 8) % 8 == iota((8, 128), 0)
        pick = jnp.where(pick, 1.0, 0.0)
        p = plane[...]
        hi = p.astype(BF16).astype(F32)
        mid = (p - hi).astype(BF16).astype(F32)
        low = p - hi - mid
        parts = jnp.concatenate([hi, mid, low], axis=0).astype(BF16)
        picks = jnp.concatenate([pick] * 3, axis=0).astype(BF16)
        pe[...] = lax.dot_general(parts, picks, (((0,), (0,)), ((), ())), preferred_element_type=F32)
        hi, lo = split(depth_matrix(depth[...]))
        rows[...] = jnp.concatenate([hi, lo], axis=0)
        y0[...] = jnp.zeros_like(y0)
        for v in range(3):
            m = masks[v].astype(F32)
            ylo[12 + v] = pack_low(m)
            yhi[12 + v] = pack_high(m)
        ylo[15] = pack_low(absorb[...])
        yhi[15] = pack_high(absorb[...])
        ylo[16] = jnp.zeros((4, 8, NZ), F32)
        yhi[16] = jnp.zeros((4, 8, NZ), F32)
        ylo[16, 0] = pe[pl.ds(0, TX, stride=TY), :]
        yhi[16, 0] = pe[pl.ds(TY - 1, TX, stride=TY), :]

    y0[pl.ds(f, 1), :] = restrict_rows(src[0], src[1], pe[...], rows[...])
    for c in range(2):
        ylo[2 * f + c] = pack_low(src[c])
        yhi[2 * f + c] = pack_high(src[c])

    @pl.when(f == FIELDS - 1)
    def _():
        y0b[...] = jnp.broadcast_to(y0[...][None], y0b.shape)


def fixed(*shape):
    return pl.BlockSpec(shape, lambda f: (0,) * len(shape))


def fields(*shape):
    return pl.BlockSpec((2,) + shape, lambda f: (f,) + (0,) * len(shape))


def whole():
    return pl.BlockSpec(memory_space=pltpu.VMEM)


def shape(*dims, dtype=F32):
    return jax.ShapeDtypeStruct(dims, dtype)


def first(src, masks, absorb, plane, depth):
    return pl.pallas_call(
        first_kernel,
        grid=(FIELDS,),
        in_specs=[fields(TX, TY, NZ), fixed(3, TX, TY, NZ), fixed(TX, TY, NZ), fixed(8, CELLS), fixed(8, NZ)],
        out_specs=[fixed(TILES, 8, 128), fixed(8, 128), fixed(CELLS, 128), fixed(17, 4, 8, NZ), fixed(17, 4, 8, NZ)],
        out_shape=[shape(TILES, 8, 128), shape(8, 128), shape(CELLS, 128), shape(17, 4, 8, NZ), shape(17, 4, 8, NZ)],
        scratch_shapes=[pltpu.VMEM((256, 256), BF16)],
        compiler_params=params(),
        name="first",
    )(src, masks, absorb, plane, depth)


def slabs_kernel(src, masks, absorb, pe, low, high, left, right):
    for out, start in ((left, 0), (right, TX - 3)):
        for i in range(3):
            x = start + i
            for ch in range(16):
                if ch < 12:
                    mid = src[ch, x]
                elif ch < 15:
                    mid = masks[ch - 12, x].astype(F32)
                else:
                    mid = absorb[x]
                out[ch, i, :TY] = mid
                out[ch, i, TY:] = halo_rows(low[ch], high[ch], x)
        out[16] = jnp.zeros((3, TY + 8, NZ), F32)
    left[16, 0, :TY] = pe[:TY]
    right[16, 0, :TY] = pe[CELLS - TY :]


def slabs(src, masks, absorb, pe, low, high):
    return pl.pallas_call(
        slabs_kernel,
        in_specs=[whole()] * 6,
        out_specs=[whole()] * 2,
        out_shape=[shape(17, 3, TY + 8, NZ)] * 2,
        compiler_params=params(),
        name="slabs",
    )(src, masks, absorb, pe, low, high)


def complex_times(are, aim, re, im):
    return are * re - aim * im, are * im + aim * re


def update_kernel(res, img, alpha, low0, high0, low1, high1, out, low, high, left, right):
    for f in range(FIELDS):
        are = alpha[f : f + 1, :]
        aim = alpha[8 + f : 9 + f, :]
        a, b = 2 * f, 2 * f + 1
        pre, pim = complex_times(are, aim, img[a], img[b])
        out[a] = res[a] - pre
        out[b] = res[b] - pim
        pre, pim = complex_times(are, aim, low1[a], low1[b])
        low[a] = low0[a] - pre
        low[b] = low0[b] - pim
        pre, pim = complex_times(are, aim, high1[a], high1[b])
        high[a] = high0[a] - pre
        high[b] = high0[b] - pim
        for ch in (a, b):
            for slab, start in ((left, 0), (right, TX - 3)):
                for i in range(3):
                    x = start + i
                    slab[ch, i, :TY] = out[ch, x]
                    slab[ch, i, TY:] = halo_rows(low[ch], high[ch], x)


def update(res, img, alpha, low0, high0, low1, high1):
    return pl.pallas_call(
        update_kernel,
        in_specs=[whole()] * 7,
        out_specs=[whole()] * 5,
        out_shape=[
            shape(12, TX, TY, NZ),
            shape(12, 4, 8, NZ),
            shape(12, 4, 8, NZ),
            shape(12, 3, TY + 8, NZ),
            shape(12, 3, TY + 8, NZ),
        ],
        compiler_params=params(),
        name="update",
    )(res, img, alpha, low0, high0, low1, high1)


def local_kernel(src, low, high, left, right, mask, mlow, mhigh, mleft, mright, absorb, alow, ahigh, aleft, aright,
                 local, image, inv, r, z1, z2, z3):
    lane = iota((TY + 8, NZ), 1)

    def plane(cells, lo, hi, lft, rgt, p):
        if p < 0:
            return lft[p + 3]
        if p >= TX:
            return rgt[p - TX]
        return wide_plane(cells, lo, hi, p)

    for p in range(-3, TX + 3):
        i = p + 3
        if 0 <= p < TX:
            m = jnp.concatenate([mask[0, p].astype(F32), halo_rows(mlow[0], mhigh[0], p)], axis=0)
        else:
            m = plane(None, None, None, mleft[0], mright[0], p)
        dim = plane(absorb, alow[0], ahigh[0], aleft[0], aright[0], p)
        dre = 5.5 - m
        inside = dim > 1.0
        scale = 1.0 / jnp.where(inside, dre * dre + dim * dim, 1.0)
        ire = jnp.where(inside, dre * scale, 0.0)
        iim = jnp.where(inside, -dim * scale, 0.0)
        inv[0, i] = ire
        inv[1, i] = iim
        re = plane(src[0], low[0], high[0], left[0], right[0], p)
        im = plane(src[1], low[1], high[1], left[1], right[1], p)
        r[0, i] = re
        r[1, i] = im
        z1[0, i], z1[1, i] = complex_times(ire, iim, re, im)

    def near(z, c, i):
        mid = z[c, i]
        total = z[c, i - 1] + z[c, i + 1]
        total = total + pltpu.roll(mid, 1, 0) + pltpu.roll(mid, TY + 7, 0)
        total = total + jnp.where(lane == 0, 0.0, pltpu.roll(mid, 1, 1))
        return total + jnp.where(lane == NZ - 1, 0.0, pltpu.roll(mid, NZ - 1, 1))

    for i in range(1, TX + 5):
        re = r[0, i] + near(z1, 0, i)
        im = r[1, i] + near(z1, 1, i)
        z2[0, i], z2[1, i] = complex_times(inv[0, i], inv[1, i], re, im)
    for i in range(2, TX + 4):
        re = r[0, i] + near(z2, 0, i)
        im = r[1, i] + near(z2, 1, i)
        zre, zim = complex_times(inv[0, i], inv[1, i], re, im)
        z3[0, i], z3[1, i] = zre, zim
        if 3 <= i < TX + 3:
            local[0, i - 3], local[1, i - 3] = zre[:TY], zim[:TY]
            image[0, i - 3], image[1, i - 3] = re[:TY], im[:TY]
    for i in range(3, TX + 3):
        for c in range(2):
            image[c, i - 3] = image[c, i - 3] - near(z3, c, i)[:TY]


def channel(offset, *dims):
    return pl.BlockSpec((1,) + dims, lambda f: (offset(f),) + (0,) * len(dims))


def local_solve(res, low, high, left, right, masks, absorb, dlow, dhigh, dleft, dright):
    of_mask = lambda f: 12 + f // 2
    of_absorb = lambda f: 15
    y = (4, 8, NZ)
    x = (3, TY + 8, NZ)
    planes = pltpu.VMEM((2, TX + 6, TY + 8, NZ), F32)
    return pl.pallas_call(
        local_kernel,
        grid=(FIELDS,),
        in_specs=[
            fields(TX, TY, NZ), fields(*y), fields(*y), fields(*x), fields(*x),
            channel(lambda f: f // 2, TX, TY, NZ),
            channel(of_mask, *y), channel(of_mask, *y), channel(of_mask, *x), channel(of_mask, *x),
            fixed(TX, TY, NZ),
            channel(of_absorb, *y), channel(of_absorb, *y), channel(of_absorb, *x), channel(of_absorb, *x),
        ],
        out_specs=[fields(TX, TY, NZ)] * 2,
        out_shape=[shape(12, TX, TY, NZ)] * 2,
        scratch_shapes=[planes] * 5,
        compiler_params=params(),
        name="local",
    )(res, low, high, left, right, masks, dlow, dhigh, dleft, dright, absorb, dlow, dhigh, dleft, dright)


def own_tile():
    return lax.axis_index("gx") * 16 + lax.axis_index("gy")


def sweep(index, tile, blocks, chosen):
    total = None
    for j in range(NNZ):
        part = mm_nt(chosen(index[tile * NNZ + j]), blocks[j])
        total = part if total is None else total + part
    return total


def sweep_kernel(index, every, y0, blocks, out):
    y = y0[...] - sweep(index, own_tile(), blocks, lambda t: every[t].astype(BF16))
    if len(out.shape) == 3:
        out[...] = jnp.broadcast_to(y.astype(BF16)[None], out.shape)
    else:
        out[...] = y


def sweep_call(index, every, y0, blocks, last):
    return pl.pallas_call(
        sweep_kernel,
        in_specs=[pl.BlockSpec(memory_space=pltpu.SMEM)] + [whole()] * 3,
        out_specs=whole(),
        out_shape=shape(8, 128) if last else shape(TILES, 8, 128, dtype=BF16),
        compiler_params=params(),
        name="sweep",
    )(index, every, y0, blocks)


def alphas(every):
    total = jnp.sum(every[...], axis=0)
    row = jnp.broadcast_to(total[6:7, :], (8, 128))
    sub, lane = iota((8, 128), 0), iota((8, 128), 1)

    def take(first_lane):
        return jnp.sum(jnp.where(lane == sub + first_lane, row, 0.0), axis=1, keepdims=True)

    energy = jnp.where(sub[:, :1] < FIELDS, take(16), 1.0)
    are = jnp.broadcast_to(take(0) / energy, (8, 128))
    aim = jnp.broadcast_to(take(8) / energy, (8, 128))
    return are, aim


def restart_kernel(index, every, before, y0, blocks, out, y0_out, alpha):
    are, aim = alphas(every)
    alpha[:8] = are
    alpha[8:] = aim
    sub, lane = iota((8, 128), 0), iota((8, 128), 1)
    turned = jnp.where(lane < 64, -aim, aim)

    def coarse(y, part):
        part = jnp.where(sub < FIELDS, part, 0.0)
        return y - (are * part + turned * pltpu.roll(part, 64, 1))

    tile = own_tile()
    own = coarse(y0[...], every[tile])
    y0_out[...] = own
    y = own - sweep(index, tile, blocks, lambda t: coarse(before[t], every[t]).astype(BF16))
    out[...] = jnp.broadcast_to(y.astype(BF16)[None], out.shape)


def restart(index, every, before, y0, blocks):
    return pl.pallas_call(
        restart_kernel,
        in_specs=[pl.BlockSpec(memory_space=pltpu.SMEM)] + [whole()] * 4,
        out_specs=[whole()] * 3,
        out_shape=[shape(TILES, 8, 128, dtype=BF16), shape(8, 128), shape(16, 128)],
        compiler_params=params(),
        name="restart",
    )(index, every, before, y0, blocks)


def image_kernel(last, y3, yw, ye, yl, yr, pe, elow, ehigh, eleft, eright, depth, masks, absorb, res, local, part,
                 *refs):
    if last:
        direction, image, pay, mats, rows, edge, acc = refs
    else:
        direction, image, pay, ylo, yhi, mats, rows, edge, acc = refs
    f = pl.program_id(0)
    sub8 = iota((8, NZ), 0)

    @pl.when(f == 0)
    def _():
        d = depth[...]
        lane = iota((8, NZ), 1)
        beside = jnp.where(lane == 0, 0.0, pltpu.roll(d, 1, 1))
        beside = beside + jnp.where(lane == NZ - 1, 0.0, pltpu.roll(d, NZ - 1, 1))
        hi, lo = split(depth_matrix(d))
        nhi, nlo = split(depth_matrix(beside))
        mats[0] = jnp.concatenate([hi, hi], axis=0)
        mats[1] = jnp.concatenate([nhi, nhi], axis=0)
        mats[2] = jnp.concatenate([lo, nlo], axis=0)
        rows[...] = jnp.concatenate([hi, lo], axis=0)
        acc[...] = jnp.zeros_like(acc)
        for x in range(TX):
            low = jnp.broadcast_to(ehigh[0, 0, x : x + 1, :], (8, 128))
            high = jnp.broadcast_to(elow[0, 0, x : x + 1, :], (8, 128))
            edge[0, x] = jnp.where(sub8 == 0, low, 0.0)
            edge[1, x] = jnp.where(sub8 == 7, high, 0.0)

    row = pl.ds(f, 1)
    one = pe[...] * y3[row, :]
    three = one.reshape(TX, TY, 128)
    west = (eleft[0, 0, :TY] * yw[row, :])[None]
    east = (eright[0, 0, :TY] * ye[row, :])[None]
    sub = iota((TX, TY, 128), 1)
    near = jnp.concatenate([west, three[:-1]], axis=0) + jnp.concatenate([three[1:], east], axis=0)
    near = near + jnp.where(sub == 0, 0.0, pltpu.roll(three, 1, 1))
    near = near + jnp.where(sub == TY - 1, 0.0, pltpu.roll(three, TY - 1, 1))
    first_rows = near[:, :8] + edge[0] * yl[row, :]
    last_rows = near[:, TY - 8 :] + edge[1] * yr[row, :]
    near = jnp.concatenate([first_rows, near[:, 8 : TY - 8], last_rows], axis=1).reshape(CELLS, 128)
    ohi, olo = split(one)
    nhi, nlo = split(near)
    o = jnp.concatenate([ohi, olo], axis=1)
    n = jnp.concatenate([nhi, nlo], axis=1)
    fine = mm(o, mats[0]) + mm(ohi, mats[2, :128])
    beside = mm(n, mats[0]) + mm(o, mats[1]) + mm(jnp.concatenate([nhi, ohi], axis=1), mats[2])
    cre, cim = fine[:, :NZ].reshape(TX, TY, NZ), fine[:, NZ:].reshape(TX, TY, NZ)
    bre, bim = beside[:, :NZ].reshape(TX, TY, NZ), beside[:, NZ:].reshape(TX, TY, NZ)
    direction[0] = local[0] + cre
    direction[1] = local[1] + cim
    dre = 5.5 - masks[0].astype(F32)
    dim = absorb[...]
    ire = part[0] + (dre * cre - dim * cim - bre)
    iim = part[1] + (dre * cim + dim * cre - bim)
    image[0] = ire
    image[1] = iim
    rre, rim = res[0], res[1]

    def total(v):
        return jnp.sum(jnp.sum(v, axis=(0, 1)).reshape(1, NZ), axis=1, keepdims=True)

    lane1 = iota((1, 128), 1)
    dots = jnp.where(lane1 == f, total(ire * rre + iim * rim), 0.0)
    dots = dots + jnp.where(lane1 == f + 8, total(ire * rim - iim * rre), 0.0)
    dots = dots + jnp.where(lane1 == f + 16, total(ire * ire + iim * iim), 0.0)
    acc[6:7, :] = acc[6:7, :] + dots
    if not last:
        acc[row, :] = restrict_rows(ire, iim, pe[...], rows[...])
        for c, value in ((0, ire), (1, iim)):
            ylo[c] = pack_low(value)
            yhi[c] = pack_high(value)

    @pl.when(f == FIELDS - 1)
    def _():
        pay[...] = jnp.broadcast_to(acc[...][None], pay.shape)


def image_call(last, y3, sides, pe, dlow, dhigh, dleft, dright, depth, masks, absorb, res, local, part):
    edge_y = channel(lambda f: 16, 4, 8, NZ)
    edge_x = channel(lambda f: 16, 3, TY + 8, NZ)
    cells = fields(TX, TY, NZ)
    out_specs = [cells, cells, fixed(TILES, 8, 128)]
    out_shape = [shape(12, TX, TY, NZ)] * 2 + [shape(TILES, 8, 128)]
    if not last:
        out_specs += [fields(4, 8, NZ)] * 2
        out_shape += [shape(12, 4, 8, NZ)] * 2
    return pl.pallas_call(
        functools.partial(image_kernel, last),
        grid=(FIELDS,),
        in_specs=[fixed(8, 128)] * 5
        + [fixed(CELLS, 128), edge_y, edge_y, edge_x, edge_x, fixed(8, NZ)]
        + [channel(lambda f: f // 2, TX, TY, NZ), fixed(TX, TY, NZ), cells, cells, cells],
        out_specs=out_specs,
        out_shape=out_shape,
        scratch_shapes=[
            pltpu.VMEM((3, 256, 256), BF16),
            pltpu.VMEM((256, 256), BF16),
            pltpu.VMEM((2, TX, 8, 128), F32),
            pltpu.VMEM((8, 128), F32),
        ],
        compiler_params=params(),
        name="image",
    )(y3, *sides, pe, dlow, dhigh, dleft, dright, depth, masks, absorb, res, local, part)


def finish_kernel(every, alpha, dir1, dir2, res, img, solution, residual, two):
    f = pl.program_id(0)

    @pl.when(f == 0)
    def _():
        are, aim = alphas(every)
        two[:8] = are
        two[8:] = aim

    are, aim = alpha[pl.ds(f, 1), :], alpha[pl.ds(f + 8, 1), :]
    bre, bim = two[pl.ds(f, 1), :], two[pl.ds(f + 8, 1), :]
    sre, sim = complex_times(are, aim, dir1[0], dir1[1])
    tre, tim = complex_times(bre, bim, dir2[0], dir2[1])
    solution[0] = sre + tre
    solution[1] = sim + tim
    pre, pim = complex_times(bre, bim, img[0], img[1])
    residual[0] = res[0] - pre
    residual[1] = res[1] - pim


def finish(every, alpha, dir1, dir2, res, img):
    cells = fields(TX, TY, NZ)
    return pl.pallas_call(
        finish_kernel,
        grid=(FIELDS,),
        in_specs=[fixed(TILES, 8, 128), fixed(16, 128), cells, cells, cells, cells],
        out_specs=[cells, cells],
        out_shape=[shape(12, TX, TY, NZ)] * 2,
        scratch_shapes=[pltpu.VMEM((16, 128), F32)],
        compiler_params=params(),
        name="finish",
    )(every, alpha, dir1, dir2, res, img)


def down(value, axis):
    count = lax.axis_size(axis)
    return lax.ppermute(value, axis, [(i + 1, i) for i in range(count - 1)])


def up(value, axis):
    count = lax.axis_size(axis)
    return lax.ppermute(value, axis, [(i, i + 1) for i in range(count - 1)])


def gather(copies):
    return lax.all_to_all(copies, BOTH, 0, 0, tiled=True)


def neighbours_of(y3):
    return up(y3, "gx"), down(y3, "gx"), up(y3, "gy"), down(y3, "gy")


def on_device(sources, masks, absorption, plane_basis, depth_basis, coupling_blocks, coupling_index):
    src = sources.reshape(12, TX, TY, NZ)
    blocks = coupling_blocks.reshape(NNZ, 128, 128)
    index = coupling_index.reshape(-1)
    plane = plane_basis.reshape(8, CELLS)

    y0b, y0, pe, ylo, yhi = first(src, masks, absorption, plane, depth_basis)
    low0, high0 = down(ylo, "gy"), up(yhi, "gy")
    all0 = gather(y0b)
    to_left, to_right = slabs(src, masks, absorption, pe, low0, high0)
    left0, right0 = up(to_right, "gx"), down(to_left, "gx")
    all1 = gather(sweep_call(index, all0, y0, blocks, False))
    all2 = gather(sweep_call(index, all1, y0, blocks, False))
    local, part = local_solve(
        src, low0, high0, left0, right0, masks, absorption, low0, high0, left0, right0
    )
    y3 = sweep_call(index, all2, y0, blocks, True)
    dir1, img1, pay, ylo, yhi = image_call(
        False, y3, neighbours_of(y3), pe, low0, high0, left0, right0, depth_basis, masks, absorption, src, local, part
    )

    low1, high1 = down(ylo, "gy"), up(yhi, "gy")
    all3 = gather(pay)
    y1b, y0, alpha = restart(index, all3, all0, y0, blocks)
    res, low, high, to_left, to_right = update(src, img1, alpha, low0, high0, low1, high1)
    left, right = up(to_right, "gx"), down(to_left, "gx")
    all1 = gather(y1b)
    all2 = gather(sweep_call(index, all1, y0, blocks, False))
    local, part = local_solve(res, low, high, left, right, masks, absorption, low0, high0, left0, right0)
    y3 = sweep_call(index, all2, y0, blocks, True)
    dir2, img2, pay = image_call(
        True, y3, neighbours_of(y3), pe, low0, high0, left0, right0, depth_basis, masks, absorption, res, local, part
    )
    all3 = gather(pay)
    solution, residual = finish(all3, alpha, dir1, dir2, res, img2)
    return solution.reshape(sources.shape), residual.reshape(sources.shape)


def solution(mesh):
    return jax.shard_map(
        on_device,
        mesh=mesh,
        in_specs=(
            P(None, None, None, "gx", "gy", None),
            P(None, "gx", "gy", None),
            P("gx", "gy", None),
            P(None, "gx", "gy"),
            P(),
            P("gx", "gy", None, None, None),
            P(),
        ),
        out_specs=(P(None, None, None, "gx", "gy", None), P(None, None, None, "gx", "gy", None)),
        check_vma=False,
    )
```

```python
import functools

import jax
import jax.numpy as jnp
from jax import lax
from jax.experimental import pallas as pl
from jax.experimental.pallas import tpu as pltpu
from jax.sharding import PartitionSpec as P

F32 = jnp.float32
BF16 = jnp.bfloat16
TX, TY, NZ = 8, 32, 128
CELLS = TX * TY
GX, GY = 8, 16
TILES = GX * GY
NNZ = 5
FIELDS = 6
VMEM = 12 * 1024 * 1024
BOTH = ("gx", "gy")


def params(**more):
    return pltpu.CompilerParams(vmem_limit_bytes=VMEM, **more)


def iota(shape, dim):
    return lax.broadcasted_iota(jnp.int32, shape, dim)


def split(x):
    hi = x.astype(BF16)
    return hi, (x - hi.astype(F32)).astype(BF16)


def mm(a, b):
    return lax.dot_general(a, b, (((1,), (0,)), ((), ())), preferred_element_type=F32)


def mm_nt(a, b):
    return lax.dot_general(a, b, (((1,), (1,)), ((), ())), preferred_element_type=F32)


def depth_matrix(depth):
    tall = jnp.concatenate([depth] * 8, axis=0)
    none = jnp.zeros_like(tall)
    return jnp.concatenate(
        [jnp.concatenate([tall, none], axis=1), jnp.concatenate([none, tall], axis=1)], axis=0
    )


def restrict_rows(re, im, pe, rows):
    cells = jnp.concatenate([re.reshape(CELLS, NZ), im.reshape(CELLS, NZ)], axis=1)
    hi, lo = split(cells)
    both = mm_nt(hi, rows)
    part = both[:, :128] + both[:, 128:] + mm_nt(lo, rows[:128])
    return jnp.sum(pe * part, axis=0, keepdims=True)


def pack_low(cells):
    sub = iota((4, 8, NZ), 1)
    return jnp.where(sub < 4, cells[0:4, 0:8], pltpu.roll(cells[4:8, 0:8], 4, 1))


def pack_high(cells):
    sub = iota((4, 8, NZ), 1)
    return jnp.where(sub >= 4, cells[0:4, 24:32], pltpu.roll(cells[4:8, 24:32], 4, 1))


def halo_rows(low, high, x):
    sub = iota((8, NZ), 0)
    if x < 4:
        return jnp.where(sub < 4, low[x], high[x])
    return jnp.where(sub < 4, pltpu.roll(low[x - 4], 4, 0), pltpu.roll(high[x - 4], 4, 0))


def wide_plane(cells, low, high, x):
    return jnp.concatenate([cells[x], halo_rows(low, high, x)], axis=0)


def first_kernel(
    src_far, masks_far, absorb_far, plane_far, depth_far, y0b_far, pe, ylo_far, yhi_far,
    src, masks, absorb, plane, depth, y0b, ylo, yhi, rows, y0, sems,
):
    copies = []
    for f in range(FIELDS):
        two = pl.ds(2 * f, 2)
        copies.append(pltpu.make_async_copy(src_far.at[two], src.at[two], sems.at[f]))
    copies.append(pltpu.make_async_copy(masks_far, masks, sems.at[FIELDS]))
    copies.append(pltpu.make_async_copy(absorb_far, absorb, sems.at[FIELDS + 1]))
    copies.append(pltpu.make_async_copy(plane_far, plane, sems.at[FIELDS + 2]))
    copies.append(pltpu.make_async_copy(depth_far, depth, sems.at[FIELDS + 3]))
    for copy in copies[::-1]:
        copy.start()
    copies[FIELDS + 2].wait()
    copies[FIELDS + 3].wait()

    pick = (iota((8, 128), 1) // 8) % 8 == iota((8, 128), 0)
    pick = jnp.where(pick, 1.0, 0.0)
    picks = jnp.concatenate([pick] * 3, axis=0).astype(BF16)
    for x in range(TX):
        p = plane[:, x, :]
        hi = p.astype(BF16).astype(F32)
        mid = (p - hi).astype(BF16).astype(F32)
        low = p - hi - mid
        parts = jnp.concatenate([hi, mid, low], axis=0).astype(BF16)
        pe[x * TY : (x + 1) * TY, :] = lax.dot_general(
            parts, picks, (((0,), (0,)), ((), ())), preferred_element_type=F32
        )
    hi, lo = split(depth_matrix(depth[...]))
    rows[...] = jnp.concatenate([hi, lo], axis=0)
    y0[...] = jnp.zeros_like(y0)
    ylo[16] = jnp.zeros((4, 8, NZ), F32)
    yhi[16] = jnp.zeros((4, 8, NZ), F32)
    ylo[16, 0] = pe[pl.ds(0, TX, stride=TY), :]
    yhi[16, 0] = pe[pl.ds(TY - 1, TX, stride=TY), :]

    for f in range(FIELDS):
        copies[f].wait()
        y0[f : f + 1, :] = restrict_rows(src[2 * f], src[2 * f + 1], pe[...], rows[...])
        for ch in (2 * f, 2 * f + 1):
            ylo[ch] = pack_low(src[ch])
            yhi[ch] = pack_high(src[ch])
    y0b[...] = jnp.broadcast_to(y0[...][None], y0b.shape)
    results = [pltpu.make_async_copy(y0b, y0b_far, sems.at[FIELDS + 4])]
    results[0].start()
    copies[FIELDS].wait()
    copies[FIELDS + 1].wait()
    for v in range(3):
        m = masks[v].astype(F32)
        ylo[12 + v] = pack_low(m)
        yhi[12 + v] = pack_high(m)
    ylo[15] = pack_low(absorb[...])
    yhi[15] = pack_high(absorb[...])
    results.append(pltpu.make_async_copy(ylo, ylo_far, sems.at[FIELDS + 5]))
    results.append(pltpu.make_async_copy(yhi, yhi_far, sems.at[FIELDS + 6]))
    results[1].start()
    results[2].start()
    for copy in results:
        copy.wait()


def fixed(*shape):
    return pl.BlockSpec(shape, lambda f: (0,) * len(shape))


def fields(*shape):
    return pl.BlockSpec((2,) + shape, lambda f: (f,) + (0,) * len(shape))


def whole():
    return pl.BlockSpec(memory_space=pltpu.VMEM)


def shape(*dims, dtype=F32):
    return jax.ShapeDtypeStruct(dims, dtype)


def far_shape(*dims, dtype=F32):
    return pltpu.HBM(dims, dtype)


def far(value):
    return pltpu.with_memory_space_constraint(value, pltpu.HBM)


def anywhere():
    return pl.BlockSpec(memory_space=pl.ANY)


def first(src, masks, absorb, plane, depth):
    return pl.pallas_call(
        first_kernel,
        in_specs=[anywhere()] * 5,
        out_specs=[anywhere(), whole(), anywhere(), anywhere()],
        out_shape=[far_shape(TILES, 8, 128), shape(CELLS, 128), far_shape(17, 4, 8, NZ), far_shape(17, 4, 8, NZ)],
        scratch_shapes=[
            pltpu.VMEM((12, TX, TY, NZ), F32),
            pltpu.VMEM((3, TX, TY, NZ), jnp.int32),
            pltpu.VMEM((TX, TY, NZ), F32),
            pltpu.VMEM((8, TX, TY), F32),
            pltpu.VMEM((8, NZ), F32),
            pltpu.VMEM((TILES, 8, 128), F32),
            pltpu.VMEM((17, 4, 8, NZ), F32),
            pltpu.VMEM((17, 4, 8, NZ), F32),
            pltpu.VMEM((256, 256), BF16),
            pltpu.VMEM((8, 128), F32),
            pltpu.SemaphoreType.DMA((FIELDS + 7,)),
        ],
        compiler_params=params(),
        name="first",
    )(far(src), far(masks), far(absorb), far(plane), far(depth))


SLAB = 2 * (TY + 8)


def slab_plane(re, im, re_halo, im_halo):
    return jnp.concatenate([re, im, re_halo, im_halo], axis=0).astype(BF16)


def slab_part(slab, i, c):
    start = c * TY if isinstance(c, int) else pl.multiple_of(c * TY, TY)
    own = slab[i, pl.ds(start, TY), :].astype(F32)
    halo = slab[i, 2 * TY :, :].astype(F32)
    return jnp.concatenate([own, jnp.where(c == 1, halo[8:], halo[:8])], axis=0)


def slabs_kernel(src, masks, absorb, pe, low, high, left, right):
    def halo(ch, x):
        return halo_rows(low[ch], high[ch], x)

    for out, start in ((left, 0), (right, TX - 3)):
        for i in range(3):
            x = start + i
            for f in range(FIELDS):
                a, b = 2 * f, 2 * f + 1
                out[f, i] = slab_plane(src[a, x], src[b, x], halo(a, x), halo(b, x))
            out[6, i] = slab_plane(masks[0, x].astype(F32), masks[1, x].astype(F32), halo(12, x), halo(13, x))
            out[7, i] = slab_plane(masks[2, x].astype(F32), absorb[x], halo(14, x), halo(15, x))
        none = jnp.zeros((8, 128), F32)
        edge = pe[:TY] if start == 0 else pe[CELLS - TY :]
        hi = edge.astype(BF16).astype(F32)
        out[8, 0] = slab_plane(hi, edge - hi, none, none)
        out[8, 1] = jnp.zeros((SLAB, 128), BF16)
        out[8, 2] = jnp.zeros((SLAB, 128), BF16)


def slabs(src, masks, absorb, pe, low, high):
    return pl.pallas_call(
        slabs_kernel,
        in_specs=[whole()] * 6,
        out_specs=[whole()] * 2,
        out_shape=[shape(9, 3, SLAB, NZ, dtype=BF16)] * 2,
        compiler_params=params(),
        name="slabs",
    )(src, masks, absorb, pe, low, high)


def complex_times(are, aim, re, im):
    return are * re - aim * im, are * im + aim * re


def update_kernel(res, img, alpha, low0, high0, low1, high1, out, low, high, left, right):
    for f in range(FIELDS):
        are = alpha[f : f + 1, :]
        aim = alpha[8 + f : 9 + f, :]
        a, b = 2 * f, 2 * f + 1
        pre, pim = complex_times(are, aim, img[a], img[b])
        out[a] = res[a] - pre
        out[b] = res[b] - pim
        pre, pim = complex_times(are, aim, low1[a], low1[b])
        low[a] = low0[a] - pre
        low[b] = low0[b] - pim
        pre, pim = complex_times(are, aim, high1[a], high1[b])
        high[a] = high0[a] - pre
        high[b] = high0[b] - pim
        for slab, start in ((left, 0), (right, TX - 3)):
            for i in range(3):
                x = start + i
                halos = [halo_rows(low[ch], high[ch], x) for ch in (a, b)]
                slab[f, i] = slab_plane(out[a, x], out[b, x], *halos)


def update(res, img, alpha, low0, high0, low1, high1):
    return pl.pallas_call(
        update_kernel,
        in_specs=[whole()] * 7,
        out_specs=[whole()] * 5,
        out_shape=[
            shape(12, TX, TY, NZ),
            shape(12, 4, 8, NZ),
            shape(12, 4, 8, NZ),
            shape(FIELDS, 3, SLAB, NZ, dtype=BF16),
            shape(FIELDS, 3, SLAB, NZ, dtype=BF16),
        ],
        compiler_params=params(),
        name="update",
    )(res, img, alpha, low0, high0, low1, high1)


def local_kernel(src, low, high, left, right, mask, mlow, mhigh, mleft, mright, absorb, alow, ahigh, aleft, aright,
                 local, image, inv, r, z1, z2, z3):
    lane = iota((TY + 8, NZ), 1)

    def plane(cells, lo, hi, lft, rgt, c, p):
        if p < 0:
            return slab_part(lft, p + 3, c)
        if p >= TX:
            return slab_part(rgt, p - TX, c)
        return wide_plane(cells, lo, hi, p)

    which = (pl.program_id(0) // 2) % 2
    for p in range(-3, TX + 3):
        i = p + 3
        if 0 <= p < TX:
            m = jnp.concatenate([mask[0, p].astype(F32), halo_rows(mlow[0], mhigh[0], p)], axis=0)
        else:
            m = plane(None, None, None, mleft.at[0], mright.at[0], which, p)
        dim = plane(absorb, alow[0], ahigh[0], aleft.at[0], aright.at[0], 1, p)
        dre = 5.5 - m
        inside = dim > 1.0
        scale = 1.0 / jnp.where(inside, dre * dre + dim * dim, 1.0)
        ire = jnp.where(inside, dre * scale, 0.0)
        iim = jnp.where(inside, -dim * scale, 0.0)
        inv[0, i] = ire
        inv[1, i] = iim
        re = plane(src[0], low[0], high[0], left.at[0], right.at[0], 0, p)
        im = plane(src[1], low[1], high[1], left.at[0], right.at[0], 1, p)
        r[0, i] = re
        r[1, i] = im
        z1[0, i], z1[1, i] = complex_times(ire, iim, re, im)

    def near(z, c, i):
        mid = z[c, i]
        total = z[c, i - 1] + z[c, i + 1]
        total = total + pltpu.roll(mid, 1, 0) + pltpu.roll(mid, TY + 7, 0)
        total = total + jnp.where(lane == 0, 0.0, pltpu.roll(mid, 1, 1))
        return total + jnp.where(lane == NZ - 1, 0.0, pltpu.roll(mid, NZ - 1, 1))

    for i in range(1, TX + 5):
        re = r[0, i] + near(z1, 0, i)
        im = r[1, i] + near(z1, 1, i)
        z2[0, i], z2[1, i] = complex_times(inv[0, i], inv[1, i], re, im)
    for i in range(2, TX + 4):
        re = r[0, i] + near(z2, 0, i)
        im = r[1, i] + near(z2, 1, i)
        zre, zim = complex_times(inv[0, i], inv[1, i], re, im)
        z3[0, i], z3[1, i] = zre, zim
        if 3 <= i < TX + 3:
            local[0, i - 3], local[1, i - 3] = zre[:TY], zim[:TY]
            image[0, i - 3], image[1, i - 3] = re[:TY], im[:TY]
    for i in range(3, TX + 3):
        for c in range(2):
            image[c, i - 3] = image[c, i - 3] - near(z3, c, i)[:TY]


def channel(offset, *dims):
    return pl.BlockSpec((1,) + dims, lambda f: (offset(f),) + (0,) * len(dims))


def local_solve(res, low, high, left, right, masks, absorb, dlow, dhigh, dleft, dright):
    of_mask = lambda f: 12 + f // 2
    of_absorb = lambda f: 15
    y = (4, 8, NZ)
    x = (3, SLAB, NZ)
    pair = channel(lambda f: f, *x)
    mask_pair, absorb_pair = channel(lambda f: 6 + f // 4, *x), channel(lambda f: 7, *x)
    planes = pltpu.VMEM((2, TX + 6, TY + 8, NZ), F32)
    return pl.pallas_call(
        local_kernel,
        grid=(FIELDS,),
        in_specs=[
            fields(TX, TY, NZ), fields(*y), fields(*y), pair, pair,
            channel(lambda f: f // 2, TX, TY, NZ),
            channel(of_mask, *y), channel(of_mask, *y), mask_pair, mask_pair,
            fixed(TX, TY, NZ),
            channel(of_absorb, *y), channel(of_absorb, *y), absorb_pair, absorb_pair,
        ],
        out_specs=[fields(TX, TY, NZ)] * 2,
        out_shape=[shape(12, TX, TY, NZ)] * 2,
        scratch_shapes=[planes] * 5,
        compiler_params=params(),
        name="local",
    )(res, low, high, left, right, masks, dlow, dhigh, dleft, dright, absorb, dlow, dhigh, dleft, dright)


def own_place():
    return lax.axis_index("gx"), lax.axis_index("gy")


def sweep(index, p, q, blocks, chosen):
    total = None
    for j in range(NNZ):
        part = mm_nt(chosen(index[(p * GY + q) * NNZ + j]), blocks[j])
        total = part if total is None else total + part
    return total


def smem():
    return pl.BlockSpec(memory_space=pltpu.SMEM)


def tile_sweep_kernel(index, every, blocks, out):
    p, q = own_place()
    y = every[p * GY + q] - sweep(index, p, q, blocks, lambda t: every[t].astype(BF16))
    out[...] = jnp.broadcast_to(y.astype(BF16)[None], out.shape)


def tile_sweep(index, every, blocks):
    return pl.pallas_call(
        tile_sweep_kernel,
        in_specs=[smem()] + [whole()] * 2,
        out_specs=whole(),
        out_shape=shape(TILES, 8, 128, dtype=BF16),
        compiler_params=params(),
        name="tile_sweep",
    )(index, every, blocks)


def column_place(t):
    return (t % GY) * GX + t // GY


def column_sweep(index, y0, chosen, pairs, out):
    p, q = own_place()
    for k in range(GX // 2):
        for c in range(2):
            a = ((p // 2 + GX // 2 - k) % (GX // 2)) * 2 + (p % 2 + c) % 2
            y = y0[a * GY + q] - sweep(index, a, q, pairs[k].at[c], chosen)
            out[:, a] = jnp.broadcast_to(y.astype(BF16)[None], (GY, 8, 128))


def column_sweep_kernel(by_column, index, every, y0, b0, b1, b2, b3, out):
    place = column_place if by_column else lambda t: t
    column_sweep(index, y0, lambda t: every[place(t)], (b0, b1, b2, b3), out)


def column_call(by_column, index, every, y0, pairs):
    return pl.pallas_call(
        functools.partial(column_sweep_kernel, by_column),
        in_specs=[smem()] + [whole()] * 6,
        out_specs=whole(),
        out_shape=shape(GY, GX, 8, 128, dtype=BF16),
        compiler_params=params(),
        name="column_sweep",
    )(index, every, y0, *pairs)


def last_sweep_kernel(index, every, y0, b0, b1, b3, blow, bhigh, out):
    p, q = own_place()
    take = lambda t: every[column_place(t)]
    pw, pe = jnp.maximum(p - 1, 0), jnp.minimum(p + 1, GX - 1)
    ql, qr = jnp.maximum(q - 1, 0), jnp.minimum(q + 1, GY - 1)

    def put(i, a, b, rows):
        out[i] = y0[a * GY + b] - sweep(index, a, b, rows, take)

    put(0, p, q, b0.at[0])
    put(3, p, ql, blow)
    put(4, p, qr, bhigh)

    @pl.when(p % 2 == 0)
    def _():
        put(1, pw, q, b1.at[1])
        put(2, pe, q, b0.at[1])

    @pl.when(p % 2 == 1)
    def _():
        put(1, pw, q, b0.at[1])
        put(2, pe, q, b3.at[1])


def last_sweep(index, every, y0, pairs, blow, bhigh):
    return pl.pallas_call(
        last_sweep_kernel,
        in_specs=[smem()] + [whole()] * 7,
        out_specs=whole(),
        out_shape=shape(5, 8, 128),
        compiler_params=params(),
        name="last_sweep",
    )(index, every, y0, pairs[0], pairs[1], pairs[3], blow, bhigh)


def alphas(total):
    row = jnp.broadcast_to(total, (8, 128))
    sub, lane = iota((8, 128), 0), iota((8, 128), 1)

    def take(first_lane):
        return jnp.sum(jnp.where(lane == sub + first_lane, row, 0.0), axis=1, keepdims=True)

    energy = jnp.where(sub[:, :1] < FIELDS, take(16), 1.0)
    are = jnp.broadcast_to(take(0) / energy, (8, 128))
    aim = jnp.broadcast_to(take(8) / energy, (8, 128))
    return are, aim


def restart_kernel(index, every, before, b0, b1, b2, b3, out, y0, alpha):
    are, aim = alphas(jnp.sum(every[...], axis=0)[6:7])
    alpha[:8] = are
    alpha[8:] = aim
    sub, lane = iota((8, 128), 0), iota((8, 128), 1)
    are = jnp.where(sub < FIELDS, are, 0.0)
    aim = jnp.where(sub < FIELDS, jnp.where(lane < 64, -aim, aim), 0.0)

    def coarse(t, _):
        part = every[t]
        y0[t] = before[t] - (are * part + aim * pltpu.roll(part, 64, 1))

    lax.fori_loop(0, TILES, coarse, None, unroll=8)
    column_sweep(index, y0, lambda t: y0[t].astype(BF16), (b0, b1, b2, b3), out)


def restart(index, every, before, pairs):
    return pl.pallas_call(
        restart_kernel,
        in_specs=[smem()] + [whole()] * 6,
        out_specs=[whole()] * 3,
        out_shape=[shape(GY, GX, 8, 128, dtype=BF16), shape(TILES, 8, 128), shape(16, 128)],
        compiler_params=params(),
        name="restart",
    )(index, every, before, *pairs)


def image_kernel(last, ys, pe, elow, ehigh, eleft, eright, depth, masks, absorb, res, local, part,
                 *refs):
    if last:
        direction, image, pay, mats, rows, edge, sides, acc = refs
    else:
        direction, image, pay, ylo, yhi, mats, rows, edge, sides, acc = refs
    f = pl.program_id(0)
    sub8 = iota((8, NZ), 0)

    @pl.when(f == 0)
    def _():
        d = depth[...]
        lane = iota((8, NZ), 1)
        beside = jnp.where(lane == 0, 0.0, pltpu.roll(d, 1, 1))
        beside = beside + jnp.where(lane == NZ - 1, 0.0, pltpu.roll(d, NZ - 1, 1))
        hi, lo = split(depth_matrix(d))
        nhi, nlo = split(depth_matrix(beside))
        mats[0] = jnp.concatenate([hi, hi], axis=0)
        mats[1] = jnp.concatenate([nhi, nhi], axis=0)
        mats[2] = jnp.concatenate([lo, nlo], axis=0)
        rows[...] = jnp.concatenate([hi, lo], axis=0)
        acc[...] = jnp.zeros_like(acc)
        for i, slab in enumerate((eleft, eright)):
            sides[i] = slab[0, 0, :TY].astype(F32) + slab[0, 0, TY : 2 * TY].astype(F32)
        for x in range(TX):
            low = jnp.broadcast_to(ehigh[0, 0, x : x + 1, :], (8, 128))
            high = jnp.broadcast_to(elow[0, 0, x : x + 1, :], (8, 128))
            edge[0, x] = jnp.where(sub8 == 0, low, 0.0)
            edge[1, x] = jnp.where(sub8 == 7, high, 0.0)

    row = pl.ds(f, 1)
    one = pe[...] * ys[0, row, :]
    three = one.reshape(TX, TY, 128)
    west = (sides[0] * ys[1, row, :])[None]
    east = (sides[1] * ys[2, row, :])[None]
    sub = iota((TX, TY, 128), 1)
    near = jnp.concatenate([west, three[:-1]], axis=0) + jnp.concatenate([three[1:], east], axis=0)
    near = near + jnp.where(sub == 0, 0.0, pltpu.roll(three, 1, 1))
    near = near + jnp.where(sub == TY - 1, 0.0, pltpu.roll(three, TY - 1, 1))
    first_rows = near[:, :8] + edge[0] * ys[3, row, :]
    last_rows = near[:, TY - 8 :] + edge[1] * ys[4, row, :]
    near = jnp.concatenate([first_rows, near[:, 8 : TY - 8], last_rows], axis=1).reshape(CELLS, 128)
    ohi, olo = split(one)
    nhi, nlo = split(near)
    o = jnp.concatenate([ohi, olo], axis=1)
    n = jnp.concatenate([nhi, nlo], axis=1)
    fine = mm(o, mats[0]) + mm(ohi, mats[2, :128])
    beside = mm(n, mats[0]) + mm(o, mats[1]) + mm(jnp.concatenate([nhi, ohi], axis=1), mats[2])
    cre, cim = fine[:, :NZ].reshape(TX, TY, NZ), fine[:, NZ:].reshape(TX, TY, NZ)
    bre, bim = beside[:, :NZ].reshape(TX, TY, NZ), beside[:, NZ:].reshape(TX, TY, NZ)
    direction[0] = local[0] + cre
    direction[1] = local[1] + cim
    dre = 5.5 - masks[0].astype(F32)
    dim = absorb[...]
    ire = part[0] + (dre * cre - dim * cim - bre)
    iim = part[1] + (dre * cim + dim * cre - bim)
    image[0] = ire
    image[1] = iim
    rre, rim = res[0], res[1]

    def total(v):
        return jnp.sum(jnp.sum(v, axis=(0, 1)).reshape(1, NZ), axis=1, keepdims=True)

    lane1 = iota((1, 128), 1)
    dots = jnp.where(lane1 == f, total(ire * rre + iim * rim), 0.0)
    dots = dots + jnp.where(lane1 == f + 8, total(ire * rim - iim * rre), 0.0)
    dots = dots + jnp.where(lane1 == f + 16, total(ire * ire + iim * iim), 0.0)
    acc[6:7, :] = acc[6:7, :] + dots
    if not last:
        acc[row, :] = restrict_rows(ire, iim, pe[...], rows[...])
        for c, value in ((0, ire), (1, iim)):
            ylo[c] = pack_low(value)
            yhi[c] = pack_high(value)

    @pl.when(f == FIELDS - 1)
    def _():
        if last:
            pay[...] = jnp.broadcast_to(acc[6:7, :], pay.shape)
        else:
            pay[...] = jnp.broadcast_to(acc[...][None], pay.shape)


def image_call(last, ys, pe, dlow, dhigh, dleft, dright, depth, masks, absorb, res, local, part):
    edge_y = channel(lambda f: 16, 4, 8, NZ)
    edge_x = channel(lambda f: 8, 3, SLAB, NZ)
    cells = fields(TX, TY, NZ)
    pay = (TILES, 128) if last else (TILES, 8, 128)
    out_specs = [cells, cells, fixed(*pay)]
    out_shape = [(shape if last else far_shape)(12, TX, TY, NZ), shape(12, TX, TY, NZ), shape(*pay)]
    if not last:
        out_specs += [fields(4, 8, NZ)] * 2
        out_shape += [shape(12, 4, 8, NZ)] * 2
    return pl.pallas_call(
        functools.partial(image_kernel, last),
        grid=(FIELDS,),
        in_specs=[fixed(5, 8, 128)]
        + [fixed(CELLS, 128), edge_y, edge_y, edge_x, edge_x, fixed(8, NZ)]
        + [channel(lambda f: f // 2, TX, TY, NZ), fixed(TX, TY, NZ), cells, cells, cells],
        out_specs=out_specs,
        out_shape=out_shape,
        scratch_shapes=[
            pltpu.VMEM((3, 256, 256), BF16),
            pltpu.VMEM((256, 256), BF16),
            pltpu.VMEM((2, TX, 8, 128), F32),
            pltpu.VMEM((2, TY, 128), F32),
            pltpu.VMEM((8, 128), F32),
        ],
        compiler_params=params(),
        name="image",
    )(ys, pe, dlow, dhigh, dleft, dright, depth, masks, absorb, res, local, part)


def finish_kernel(every, alpha, dir1, dir2, res, img, solution, residual, two):
    f = pl.program_id(0)

    @pl.when(f == 0)
    def _():
        are, aim = alphas(jnp.sum(every[...], axis=0, keepdims=True))
        two[:8] = are
        two[8:] = aim

    are, aim = alpha[pl.ds(f, 1), :], alpha[pl.ds(f + 8, 1), :]
    bre, bim = two[pl.ds(f, 1), :], two[pl.ds(f + 8, 1), :]
    sre, sim = complex_times(are, aim, dir1[0], dir1[1])
    tre, tim = complex_times(bre, bim, dir2[0], dir2[1])
    solution[0] = sre + tre
    solution[1] = sim + tim
    pre, pim = complex_times(bre, bim, img[0], img[1])
    residual[0] = res[0] - pre
    residual[1] = res[1] - pim


def finish(every, alpha, dir1, dir2, res, img):
    cells = fields(TX, TY, NZ)
    return pl.pallas_call(
        finish_kernel,
        grid=(FIELDS,),
        in_specs=[fixed(TILES, 128), fixed(16, 128), cells, cells, cells, cells],
        out_specs=[cells, cells],
        out_shape=[shape(12, TX, TY, NZ)] * 2,
        scratch_shapes=[pltpu.VMEM((16, 128), F32)],
        compiler_params=params(),
        name="finish",
    )(every, alpha, dir1, dir2, res, img)


def down(value, axis):
    count = lax.axis_size(axis)
    return lax.ppermute(value, axis, [(i + 1, i) for i in range(count - 1)])


def up(value, axis):
    count = lax.axis_size(axis)
    return lax.ppermute(value, axis, [(i, i + 1) for i in range(count - 1)])


def gather(copies, axes=BOTH):
    return lax.all_to_all(copies, axes, 0, 0, tiled=True)


def swap_cores(value):
    return lax.ppermute(value, "gx", [(i, i ^ 1) for i in range(GX)])


def round_x(value, k):
    return lax.ppermute(value, "gx", [(i, (i + 2 * k) % GX) for i in range(GX)])


def after(value, *others):
    return lax.optimization_barrier((value, *others))[0]


def on_device(sources, masks, absorption, plane_basis, depth_basis, coupling_blocks, coupling_index):
    src = sources.reshape(12, TX, TY, NZ)
    blocks = coupling_blocks.reshape(NNZ, 128, 128)
    index = coupling_index.reshape(-1)

    y0b, pe, ylo, yhi = first(src, masks, absorption, plane_basis, depth_basis)
    all0 = gather(y0b)
    low0, high0 = down(ylo, "gy"), up(yhi, "gy")
    other = swap_cores(blocks)
    own_pair = jnp.stack([blocks, other])
    blow, bhigh = up(blocks, "gy"), down(blocks, "gy")
    y1b = tile_sweep(index, after(all0, other), blocks)
    all1 = gather(y1b)
    to_left, to_right = slabs(src, masks, absorption, after(pe, y1b), low0, high0)
    left0, right0 = up(to_right, "gx"), down(to_left, "gx")
    mine = after(own_pair, y1b)
    pairs = [own_pair] + [round_x(mine, k) for k in (1, 2, 3)]
    y2b = column_call(False, index, after(all1, left0, right0, blow, bhigh), all0, pairs)
    all2 = gather(y2b, "gy").reshape(TILES, 8, 128)
    local, part = local_solve(
        src, low0, high0, after(left0, all2), right0, masks, absorption, low0, high0, left0, right0
    )
    ys = last_sweep(index, after(all2, part), all0, pairs, blow, bhigh)
    dir1, img1, pay, ylo, yhi = image_call(
        False, ys, pe, low0, high0, left0, right0, depth_basis, masks, absorption, src, local, part
    )

    all3 = gather(pay)
    low1, high1 = down(ylo, "gy"), up(yhi, "gy")
    y1b, y0, alpha = restart(index, all3, all0, pairs)
    all1 = gather(y1b, "gy").reshape(TILES, 8, 128)
    res, low, high, to_left, to_right = update(src, img1, alpha, low0, high0, low1, high1)
    left, right = up(to_right, "gx"), down(to_left, "gx")
    y2b = column_call(True, index, after(all1, left, right), y0, pairs)
    all2 = gather(y2b, "gy").reshape(TILES, 8, 128)
    local, part = local_solve(res, low, high, after(left, all2), right, masks, absorption, low0, high0, left0, right0)
    ys = last_sweep(index, after(all2, part), y0, pairs, blow, bhigh)
    dir2, img2, pay = image_call(
        True, ys, pe, low0, high0, left0, right0, depth_basis, masks, absorption, res, local, part
    )
    all3 = gather(pay)
    solution, residual = finish(all3, alpha, dir1, dir2, res, img2)
    return solution.reshape(sources.shape), residual.reshape(sources.shape)


def solution(mesh):
    return jax.shard_map(
        on_device,
        mesh=mesh,
        in_specs=(
            P(None, None, None, "gx", "gy", None),
            P(None, "gx", "gy", None),
            P("gx", "gy", None),
            P(None, "gx", "gy"),
            P(),
            P("gx", "gy", None, None, None),
            P(),
        ),
        out_specs=(P(None, None, None, "gx", "gy", None), P(None, None, None, "gx", "gy", None)),
        check_vma=False,
    )
```

```python
import functools

import jax
import jax.numpy as jnp
from jax import lax
from jax.experimental import pallas as pl
from jax.experimental.pallas import tpu as pltpu
from jax.sharding import PartitionSpec as P

F32 = jnp.float32
BF16 = jnp.bfloat16
TX, TY, NZ = 8, 32, 128
CELLS = TX * TY
GX, GY = 8, 16
TILES = GX * GY
NNZ = 5
FIELDS = 6
VMEM = 12 * 1024 * 1024
EDGES = (25, 4, 16, NZ)
BOTH = ("gx", "gy")


def params(**more):
    return pltpu.CompilerParams(vmem_limit_bytes=VMEM, **more)


def iota(shape, dim):
    return lax.broadcasted_iota(jnp.int32, shape, dim)


def split(x):
    hi = x.astype(BF16)
    return hi, (x - hi.astype(F32)).astype(BF16)


def mm(a, b):
    return lax.dot_general(a, b, (((1,), (0,)), ((), ())), preferred_element_type=F32)


def mm_nt(a, b):
    return lax.dot_general(a, b, (((1,), (1,)), ((), ())), preferred_element_type=F32)


def depth_matrix(depth):
    tall = jnp.concatenate([depth] * 8, axis=0)
    none = jnp.zeros_like(tall)
    return jnp.concatenate(
        [jnp.concatenate([tall, none], axis=1), jnp.concatenate([none, tall], axis=1)], axis=0
    )


def restrict_rows(re, im, pe, rows):
    cells = jnp.concatenate([re.reshape(CELLS, NZ), im.reshape(CELLS, NZ)], axis=1)
    hi, lo = split(cells)
    both = mm_nt(hi, rows)
    part = both[:, :128] + both[:, 128:] + mm_nt(lo, rows[:128])
    return jnp.sum(pe * part, axis=0, keepdims=True)


def pack_low(cells):
    sub = iota((4, 8, NZ), 1)
    return jnp.where(sub < 4, cells[0:4, 0:8], pltpu.roll(cells[4:8, 0:8], 4, 1))


def pack_high(cells):
    sub = iota((4, 8, NZ), 1)
    return jnp.where(sub >= 4, cells[0:4, 24:32], pltpu.roll(cells[4:8, 24:32], 4, 1))


def halo_rows(low, high, x):
    sub = iota((8, NZ), 0)
    if x < 4:
        return jnp.where(sub < 4, low[x], high[x])
    return jnp.where(sub < 4, pltpu.roll(low[x - 4], 4, 0), pltpu.roll(high[x - 4], 4, 0))


def wide_plane(cells, low, high, x):
    return jnp.concatenate([cells[x], halo_rows(low, high, x)], axis=0)


def even_row():
    return lax.axis_index("gy") % 2 == 0


def by_pairs(to_last, to_next):
    even = even_row()
    return jnp.where(even, to_next, to_last), jnp.where(even, to_last, to_next)


def first_kernel(
    src_far, masks_far, absorb_far, plane_far, depth_far, blocks_far, y0b_far, pe, in_far, out_far,
    src, masks, absorb, plane, depth, blocks, y0b, inner, outer, rows, y0, sems,
):
    copies = []
    for f in range(FIELDS):
        two = pl.ds(2 * f, 2)
        copies.append(pltpu.make_async_copy(src_far.at[two], src.at[two], sems.at[f]))
    rest = ((masks_far, masks), (absorb_far, absorb), (plane_far, plane), (depth_far, depth), (blocks_far, blocks))
    for i, (there, here) in enumerate(rest):
        copies.append(pltpu.make_async_copy(there, here, sems.at[FIELDS + i]))
    for copy in copies[::-1]:
        copy.start()
    copies[FIELDS + 2].wait()
    copies[FIELDS + 3].wait()

    pick = (iota((8, 128), 1) // 8) % 8 == iota((8, 128), 0)
    pick = jnp.where(pick, 1.0, 0.0)
    picks = jnp.concatenate([pick] * 3, axis=0).astype(BF16)
    for x in range(TX):
        p = plane[:, x, :]
        hi = p.astype(BF16).astype(F32)
        mid = (p - hi).astype(BF16).astype(F32)
        low = p - hi - mid
        parts = jnp.concatenate([hi, mid, low], axis=0).astype(BF16)
        pe[x * TY : (x + 1) * TY, :] = lax.dot_general(
            parts, picks, (((0,), (0,)), ((), ())), preferred_element_type=F32
        )
    hi, lo = split(depth_matrix(depth[...]))
    rows[...] = jnp.concatenate([hi, lo], axis=0)
    y0[...] = jnp.zeros_like(y0)

    def edges(re, im):
        low = jnp.concatenate([pack_low(re), pack_low(im)], axis=1)
        high = jnp.concatenate([pack_high(re), pack_high(im)], axis=1)
        return by_pairs(low, high)

    def put(refs, at, values):
        for ref, value in zip(refs, values):
            hi, lo = split(value)
            ref[at[0]] = hi
            if len(at) > 1:
                ref[at[1]] = lo

    refs = (inner, outer)
    for f in range(FIELDS):
        copies[f].wait()
        re, im = src[2 * f], src[2 * f + 1]
        y0[f : f + 1, :] = restrict_rows(re, im, pe[...], rows[...])
        put(refs, (f, FIELDS + f), edges(re, im))
    y0b[...] = jnp.broadcast_to(y0[...][None], y0b.shape)
    results = [pltpu.make_async_copy(y0b, y0b_far, sems.at[FIELDS + 5])]
    results[0].start()
    copies[FIELDS].wait()
    copies[FIELDS + 1].wait()
    put(refs, (12,), edges(masks[0].astype(F32), masks[1].astype(F32)))
    put(refs, (13,), edges(masks[2].astype(F32), absorb[...]))
    copies[FIELDS + 4].wait()
    ends = by_pairs(pe[pl.ds(0, TX, stride=TY), :], pe[pl.ds(TY - 1, TX, stride=TY), :])
    for ref, end in zip(refs, ends):
        hi = end.astype(BF16).astype(F32)
        ref[14] = jnp.zeros((4, 16, NZ), BF16)
        ref[14, 0] = jnp.concatenate([hi, end - hi], axis=0).astype(BF16)
        for j in range(NNZ):
            ref[15 + 2 * j : 17 + 2 * j] = blocks[j].reshape(2, 4, 16, 128)
    results.append(pltpu.make_async_copy(inner, in_far, sems.at[FIELDS + 6]))
    results.append(pltpu.make_async_copy(outer, out_far, sems.at[FIELDS + 7]))
    results[1].start()
    results[2].start()
    for copy in results:
        copy.wait()


def fixed(*shape):
    return pl.BlockSpec(shape, lambda f: (0,) * len(shape))


def fields(*shape):
    return pl.BlockSpec((2,) + shape, lambda f: (f,) + (0,) * len(shape))


def whole():
    return pl.BlockSpec(memory_space=pltpu.VMEM)


def shape(*dims, dtype=F32):
    return jax.ShapeDtypeStruct(dims, dtype)


def far_shape(*dims, dtype=F32):
    return pltpu.HBM(dims, dtype)


def far(value):
    return pltpu.with_memory_space_constraint(value, pltpu.HBM)


def anywhere():
    return pl.BlockSpec(memory_space=pl.ANY)


def first(src, masks, absorb, plane, depth, blocks):
    return pl.pallas_call(
        first_kernel,
        in_specs=[anywhere()] * 6,
        out_specs=[anywhere(), whole(), anywhere(), anywhere()],
        out_shape=[far_shape(TILES, 8, 128), shape(CELLS, 128), far_shape(*EDGES, dtype=BF16), far_shape(*EDGES, dtype=BF16)],
        scratch_shapes=[
            pltpu.VMEM((12, TX, TY, NZ), F32),
            pltpu.VMEM((3, TX, TY, NZ), jnp.int32),
            pltpu.VMEM((TX, TY, NZ), F32),
            pltpu.VMEM((8, TX, TY), F32),
            pltpu.VMEM((8, NZ), F32),
            pltpu.VMEM((NNZ, 128, 128), BF16),
            pltpu.VMEM((TILES, 8, 128), F32),
            pltpu.VMEM(EDGES, BF16),
            pltpu.VMEM(EDGES, BF16),
            pltpu.VMEM((256, 256), BF16),
            pltpu.VMEM((8, 128), F32),
            pltpu.SemaphoreType.DMA((FIELDS + 8,)),
        ],
        compiler_params=params(),
        name="first",
    )(far(src), far(masks), far(absorb), far(plane), far(depth), far(blocks))


def anywhere():
    return pl.BlockSpec(memory_space=pl.ANY)


SLAB = 2 * (TY + 8)


def slab_plane(re, im, re_halo, im_halo):
    return jnp.concatenate([re, im, re_halo, im_halo], axis=0).astype(BF16)


def slab_part(slab, i, c):
    start = c * TY if isinstance(c, int) else pl.multiple_of(c * TY, TY)
    own = slab[i, pl.ds(start, TY), :].astype(F32)
    halo = slab[i, 2 * TY :, :].astype(F32)
    return jnp.concatenate([own, jnp.where(c == 1, halo[8:], halo[:8])], axis=0)


def own_core():
    return lax.axis_index("gx") % 2


def fill_sides(fill, core_out, chip_out):
    @pl.when(own_core() == 0)
    def _():
        fill(core_out, TX - 3)
        fill(chip_out, 0)

    @pl.when(own_core() == 1)
    def _():
        fill(core_out, 0)
        fill(chip_out, TX - 3)


def slabs_kernel(src, masks, absorb, pe, inner, outer, b0, b1, b2, b3, core_out, chip_out, low, high):
    even = even_row()
    for pair in range(8):
        sides = []
        for ref in (inner, outer):
            value = ref[pair].astype(F32) if pair < FIELDS else ref[FIELDS + pair].astype(F32)
            sides.append(value + ref[FIELDS + pair].astype(F32) if pair < FIELDS else value)
        for out, value in ((low, jnp.where(even, sides[0], sides[1])), (high, jnp.where(even, sides[1], sides[0]))):
            out[2 * pair] = value[:, :8]
            out[2 * pair + 1] = value[:, 8:]
    ends = [ref[14, 0].astype(F32) for ref in (inner, outer)]
    ends = [end[:8] + end[8:] for end in ends]
    for out, value in ((low, jnp.where(even, *ends)), (high, jnp.where(even, *ends[::-1]))):
        out[16] = jnp.zeros((4, 8, NZ), F32)
        out[16, 0] = value

    def halo(ch, x):
        return halo_rows(low[ch], high[ch], x)

    def fill(out, start):
        for i in range(3):
            x = start + i
            for f in range(FIELDS):
                a, b = 2 * f, 2 * f + 1
                out[3 * f + i] = slab_plane(src[a, x], src[b, x], halo(a, x), halo(b, x))
            out[18 + i] = slab_plane(masks[0, x].astype(F32), masks[1, x].astype(F32), halo(12, x), halo(13, x))
            out[21 + i] = slab_plane(masks[2, x].astype(F32), absorb[x], halo(14, x), halo(15, x))
        none = jnp.zeros((8, 128), F32)
        edge = pe[:TY] if start == 0 else pe[CELLS - TY :]
        hi = edge.astype(BF16).astype(F32)
        out[24] = slab_plane(hi, edge - hi, none, none)
        out[25] = jnp.zeros((SLAB, 128), BF16)
        out[26] = jnp.zeros((SLAB, 128), BF16)

    fill_sides(fill, core_out, chip_out)
    for k, rows in enumerate((b0, b1, b2, b3)):
        core_out[27 + 8 * k : 35 + 8 * k] = rows[...].reshape(8, SLAB, 128)


def slabs(src, masks, absorb, pe, inner, outer, rows):
    return pl.pallas_call(
        slabs_kernel,
        in_specs=[whole()] * 10,
        out_specs=[whole()] * 4,
        out_shape=[shape(59, SLAB, NZ, dtype=BF16), shape(27, SLAB, NZ, dtype=BF16)] + [shape(17, 4, 8, NZ)] * 2,
        compiler_params=params(),
        name="slabs",
    )(src, masks, absorb, pe, inner, outer, *rows)


def complex_times(are, aim, re, im):
    return are * re - aim * im, are * im + aim * re


def update_kernel(res, img, alpha, low0, high0, inner, outer, out, low, high, core_out, chip_out):
    even = even_row()
    for f in range(FIELDS):
        are = alpha[f : f + 1, :]
        aim = alpha[8 + f : 9 + f, :]
        a, b = 2 * f, 2 * f + 1
        pre, pim = complex_times(are, aim, img[a], img[b])
        out[a] = res[a] - pre
        out[b] = res[b] - pim
        pre, pim = complex_times(are, aim, *[jnp.where(even, inner[ch], outer[ch]) for ch in (a, b)])
        low[a] = low0[a] - pre
        low[b] = low0[b] - pim
        pre, pim = complex_times(are, aim, *[jnp.where(even, outer[ch], inner[ch]) for ch in (a, b)])
        high[a] = high0[a] - pre
        high[b] = high0[b] - pim

    def fill(slab, start):
        for f in range(FIELDS):
            a, b = 2 * f, 2 * f + 1
            for i in range(3):
                x = start + i
                halos = [halo_rows(low[ch], high[ch], x) for ch in (a, b)]
                slab[3 * f + i] = slab_plane(out[a, x], out[b, x], *halos)

    fill_sides(fill, core_out, chip_out)


def update(res, img, alpha, low0, high0, inner, outer):
    return pl.pallas_call(
        update_kernel,
        in_specs=[whole()] * 7,
        out_specs=[whole()] * 5,
        out_shape=[
            shape(12, TX, TY, NZ),
            shape(12, 4, 8, NZ),
            shape(12, 4, 8, NZ),
            shape(18, SLAB, NZ, dtype=BF16),
            shape(18, SLAB, NZ, dtype=BF16),
        ],
        compiler_params=params(),
        name="update",
    )(res, img, alpha, low0, high0, inner, outer)


def local_kernel(src, low, high, left, right, mask, mlow, mhigh, mleft, mright, absorb, alow, ahigh, aleft, aright,
                 local, image, inv, r, z1, z2, z3):
    lane = iota((TY + 8, NZ), 1)

    core = own_core()

    def plane(cells, lo, hi, by_core, by_chip, c, p):
        if 0 <= p < TX:
            return wide_plane(cells, lo, hi, p)
        i, by_chip_on = (p + 3, 0) if p < 0 else (p - TX, 1)
        return jnp.where(core == by_chip_on, slab_part(by_chip, i, c), slab_part(by_core, i, c))

    which = (pl.program_id(0) // 2) % 2
    for p in range(-3, TX + 3):
        i = p + 3
        if 0 <= p < TX:
            m = jnp.concatenate([mask[0, p].astype(F32), halo_rows(mlow[0], mhigh[0], p)], axis=0)
        else:
            m = plane(None, None, None, mleft, mright, which, p)
        dim = plane(absorb, alow[0], ahigh[0], aleft, aright, 1, p)
        dre = 5.5 - m
        inside = dim > 1.0
        scale = 1.0 / jnp.where(inside, dre * dre + dim * dim, 1.0)
        ire = jnp.where(inside, dre * scale, 0.0)
        iim = jnp.where(inside, -dim * scale, 0.0)
        inv[0, i] = ire
        inv[1, i] = iim
        re = plane(src[0], low[0], high[0], left, right, 0, p)
        im = plane(src[1], low[1], high[1], left, right, 1, p)
        r[0, i] = re
        r[1, i] = im
        z1[0, i], z1[1, i] = complex_times(ire, iim, re, im)

    def near(z, c, i):
        mid = z[c, i]
        total = z[c, i - 1] + z[c, i + 1]
        total = total + pltpu.roll(mid, 1, 0) + pltpu.roll(mid, TY + 7, 0)
        total = total + jnp.where(lane == 0, 0.0, pltpu.roll(mid, 1, 1))
        return total + jnp.where(lane == NZ - 1, 0.0, pltpu.roll(mid, NZ - 1, 1))

    for i in range(1, TX + 5):
        re = r[0, i] + near(z1, 0, i)
        im = r[1, i] + near(z1, 1, i)
        z2[0, i], z2[1, i] = complex_times(inv[0, i], inv[1, i], re, im)
    for i in range(2, TX + 4):
        re = r[0, i] + near(z2, 0, i)
        im = r[1, i] + near(z2, 1, i)
        zre, zim = complex_times(inv[0, i], inv[1, i], re, im)
        z3[0, i], z3[1, i] = zre, zim
        if 3 <= i < TX + 3:
            local[0, i - 3], local[1, i - 3] = zre[:TY], zim[:TY]
            image[0, i - 3], image[1, i - 3] = re[:TY], im[:TY]
    for i in range(3, TX + 3):
        for c in range(2):
            image[c, i - 3] = image[c, i - 3] - near(z3, c, i)[:TY]


def channel(offset, *dims):
    return pl.BlockSpec((1,) + dims, lambda f: (offset(f),) + (0,) * len(dims))


def slab_of(which):
    return pl.BlockSpec((3, SLAB, NZ), lambda f: (which(f), 0, 0))


def local_solve(res, low, high, left, right, masks, absorb, dlow, dhigh, dleft, dright):
    of_mask = lambda f: 12 + f // 2
    of_absorb = lambda f: 15
    y = (4, 8, NZ)
    pair, mask_pair, absorb_pair = slab_of(lambda f: f), slab_of(lambda f: 6 + f // 4), slab_of(lambda f: 7)
    planes = pltpu.VMEM((2, TX + 6, TY + 8, NZ), F32)
    return pl.pallas_call(
        local_kernel,
        grid=(FIELDS,),
        in_specs=[
            fields(TX, TY, NZ), fields(*y), fields(*y), pair, pair,
            channel(lambda f: f // 2, TX, TY, NZ),
            channel(of_mask, *y), channel(of_mask, *y), mask_pair, mask_pair,
            fixed(TX, TY, NZ),
            channel(of_absorb, *y), channel(of_absorb, *y), absorb_pair, absorb_pair,
        ],
        out_specs=[fields(TX, TY, NZ)] * 2,
        out_shape=[shape(12, TX, TY, NZ)] * 2,
        scratch_shapes=[planes] * 5,
        compiler_params=params(),
        name="local",
    )(res, low, high, left, right, masks, dlow, dhigh, dleft, dright, absorb, dlow, dhigh, dleft, dright)


def own_place():
    return lax.axis_index("gx"), lax.axis_index("gy")


def sweep(index, p, q, blocks, chosen):
    total = None
    for j in range(NNZ):
        part = mm_nt(chosen(index[(p * GY + q) * NNZ + j]), blocks[j])
        total = part if total is None else total + part
    return total


def smem():
    return pl.BlockSpec(memory_space=pltpu.SMEM)


def tile_sweep_kernel(index, every, blocks, out):
    p, q = own_place()
    y = every[p * GY + q] - sweep(index, p, q, blocks, lambda t: every[t].astype(BF16))
    out[...] = jnp.broadcast_to(y.astype(BF16)[None], out.shape)


def tile_sweep(index, every, blocks):
    return pl.pallas_call(
        tile_sweep_kernel,
        in_specs=[smem()] + [whole()] * 2,
        out_specs=whole(),
        out_shape=shape(TILES, 8, 128, dtype=BF16),
        compiler_params=params(),
        name="tile_sweep",
    )(index, every, blocks)


def column_place(t):
    return (t % GY) * GX + t // GY


def column_sweep(index, y0, chosen, rows, out):
    p, q = own_place()
    for i in range(GX):
        a = ((p // 2 + GX // 2 - i // 2) % (GX // 2)) * 2 + (p % 2 + i % 2) % 2
        y = y0[a * GY + q] - sweep(index, a, q, rows(i), chosen)
        out[:, a] = jnp.broadcast_to(y.astype(BF16)[None], (GY, 8, 128))


def packed_blocks(slab, k):
    rows = slab[8 * k : 8 * k + 8].reshape(NNZ * 128, 128)
    return [rows[128 * j : 128 * j + 128] for j in range(NNZ)]


def first_column_kernel(index, every, y0, b0, b1, b2, b3, by_core, out):
    own = (b0, b1, b2, b3)
    theirs = by_core.at[27:59]
    column_sweep(
        index, y0, lambda t: every[t], lambda i: packed_blocks(theirs, i // 2) if i % 2 else own[i // 2], out
    )


def first_column(index, every, y0, rows, by_core):
    return pl.pallas_call(
        first_column_kernel,
        in_specs=[smem()] + [whole()] * 7,
        out_specs=whole(),
        out_shape=shape(GY, GX, 8, 128, dtype=BF16),
        compiler_params=params(),
        name="column_sweep",
    )(index, every, y0, *rows, by_core)


def column_rows(own, theirs):
    return lambda i: packed_blocks(theirs, i // 2) if i % 2 else own.at[i // 2]


def column_sweep_kernel(index, every, y0, own, theirs, out):
    column_sweep(index, y0, lambda t: every[column_place(t)], column_rows(own, theirs), out)


def column_call(index, every, y0, own, theirs):
    return pl.pallas_call(
        column_sweep_kernel,
        in_specs=[smem()] + [whole()] * 4,
        out_specs=whole(),
        out_shape=shape(GY, GX, 8, 128, dtype=BF16),
        compiler_params=params(),
        name="column_sweep",
    )(index, every, y0, own, theirs)


def edge_blocks(edges):
    rows = edges[15:25].reshape(NNZ * 128, 128)
    return [rows[128 * j : 128 * j + 128] for j in range(NNZ)]


def last_sweep_kernel(index, every, y0, own, theirs, inner, outer, out):
    p, q = own_place()
    take = lambda t: every[column_place(t)]
    pw, pe = jnp.maximum(p - 1, 0), jnp.minimum(p + 1, GX - 1)
    ql, qr = jnp.maximum(q - 1, 0), jnp.minimum(q + 1, GY - 1)

    def put(i, a, b, rows):
        out[i] = y0[a * GY + b] - sweep(index, a, b, rows, take)

    put(0, p, q, own)

    @pl.when(q % 2 == 0)
    def _():
        put(3, p, ql, edge_blocks(outer))
        put(4, p, qr, edge_blocks(inner))

    @pl.when(q % 2 == 1)
    def _():
        put(3, p, ql, edge_blocks(inner))
        put(4, p, qr, edge_blocks(outer))

    @pl.when(p % 2 == 0)
    def _():
        put(1, pw, q, packed_blocks(theirs, 1))
        put(2, pe, q, packed_blocks(theirs, 0))

    @pl.when(p % 2 == 1)
    def _():
        put(1, pw, q, packed_blocks(theirs, 0))
        put(2, pe, q, packed_blocks(theirs, 3))


def first_last_kernel(index, every, y0, own, by_core, inner, outer, out):
    last_sweep_kernel(index, every, y0, own, by_core.at[27:59], inner, outer, out)


def later_last_kernel(index, every, y0, own, theirs, inner, outer, out):
    last_sweep_kernel(index, every, y0, own.at[0], theirs, inner, outer, out)


def last_sweep(kernel, index, every, y0, own, theirs, inner, outer):
    return pl.pallas_call(
        kernel,
        in_specs=[smem()] + [whole()] * 6,
        out_specs=whole(),
        out_shape=shape(5, 8, 128),
        compiler_params=params(),
        name="last_sweep",
    )(index, every, y0, own, theirs, inner, outer)


def alphas(total):
    row = jnp.broadcast_to(total, (8, 128))
    sub, lane = iota((8, 128), 0), iota((8, 128), 1)

    def take(first_lane):
        return jnp.sum(jnp.where(lane == sub + first_lane, row, 0.0), axis=1, keepdims=True)

    energy = jnp.where(sub[:, :1] < FIELDS, take(16), 1.0)
    are = jnp.broadcast_to(take(0) / energy, (8, 128))
    aim = jnp.broadcast_to(take(8) / energy, (8, 128))
    return are, aim


def restart_kernel(index, every, before, b0, b1, b2, b3, by_core, out, y0, alpha, own, theirs, sems):
    copies = [pltpu.make_async_copy(rows, own.at[k], sems.at[k]) for k, rows in enumerate((b0, b1, b2, b3))]
    copies.append(pltpu.make_async_copy(by_core.at[27:59], theirs, sems.at[4]))
    for copy in copies:
        copy.start()
    are, aim = alphas(jnp.sum(every[...], axis=0)[6:7])
    alpha[:8] = are
    alpha[8:] = aim
    sub, lane = iota((8, 128), 0), iota((8, 128), 1)
    are = jnp.where(sub < FIELDS, are, 0.0)
    aim = jnp.where(sub < FIELDS, jnp.where(lane < 64, -aim, aim), 0.0)

    def coarse(t, _):
        part = every[t]
        y0[t] = before[t] - (are * part + aim * pltpu.roll(part, 64, 1))

    lax.fori_loop(0, TILES, coarse, None, unroll=8)
    for copy in copies:
        copy.wait()
    column_sweep(index, y0, lambda t: y0[t].astype(BF16), column_rows(own, theirs), out)


def restart(index, every, before, rows, by_core):
    return pl.pallas_call(
        restart_kernel,
        in_specs=[smem()] + [whole()] * 2 + [anywhere()] * 5,
        out_specs=[whole()] * 5,
        out_shape=[
            shape(GY, GX, 8, 128, dtype=BF16),
            shape(TILES, 8, 128),
            shape(16, 128),
            shape(4, NNZ, 128, 128, dtype=BF16),
            shape(32, SLAB, 128, dtype=BF16),
        ],
        scratch_shapes=[pltpu.SemaphoreType.DMA((5,))],
        compiler_params=params(),
        name="restart",
    )(index, every, before, *[far(row) for row in rows], far(by_core))


def image_kernel(last, ys, pe, elow, ehigh, eleft, eright, depth, masks, absorb, res, local, part,
                 *refs):
    if last:
        direction, image, pay, mats, rows, edge, sides, acc = refs
    else:
        direction, image, pay_far, in_far, out_far, mats, rows, edge, sides, acc, pay, inner, outer, sems = refs
    f = pl.program_id(0)

    def sent(i):
        two = pl.ds(2 * i, 2)
        return (
            pltpu.make_async_copy(inner.at[two], in_far.at[two], sems.at[i]),
            pltpu.make_async_copy(outer.at[two], out_far.at[two], sems.at[FIELDS + i]),
        )

    sub8 = iota((8, NZ), 0)

    @pl.when(f == 0)
    def _():
        d = depth[...]
        lane = iota((8, NZ), 1)
        beside = jnp.where(lane == 0, 0.0, pltpu.roll(d, 1, 1))
        beside = beside + jnp.where(lane == NZ - 1, 0.0, pltpu.roll(d, NZ - 1, 1))
        hi, lo = split(depth_matrix(d))
        nhi, nlo = split(depth_matrix(beside))
        mats[0] = jnp.concatenate([hi, hi], axis=0)
        mats[1] = jnp.concatenate([nhi, nhi], axis=0)
        mats[2] = jnp.concatenate([lo, nlo], axis=0)
        rows[...] = jnp.concatenate([hi, lo], axis=0)
        acc[...] = jnp.zeros_like(acc)
        by_core, by_chip = [s[0, :TY].astype(F32) + s[0, TY : 2 * TY].astype(F32) for s in (eleft, eright)]
        sides[0] = jnp.where(own_core() == 0, by_chip, by_core)
        sides[1] = jnp.where(own_core() == 0, by_core, by_chip)
        for x in range(TX):
            low = jnp.broadcast_to(ehigh[0, 0, x : x + 1, :], (8, 128))
            high = jnp.broadcast_to(elow[0, 0, x : x + 1, :], (8, 128))
            edge[0, x] = jnp.where(sub8 == 0, low, 0.0)
            edge[1, x] = jnp.where(sub8 == 7, high, 0.0)

    row = pl.ds(f, 1)
    one = pe[...] * ys[0, row, :]
    three = one.reshape(TX, TY, 128)
    west = (sides[0] * ys[1, row, :])[None]
    east = (sides[1] * ys[2, row, :])[None]
    sub = iota((TX, TY, 128), 1)
    near = jnp.concatenate([west, three[:-1]], axis=0) + jnp.concatenate([three[1:], east], axis=0)
    near = near + jnp.where(sub == 0, 0.0, pltpu.roll(three, 1, 1))
    near = near + jnp.where(sub == TY - 1, 0.0, pltpu.roll(three, TY - 1, 1))
    first_rows = near[:, :8] + edge[0] * ys[3, row, :]
    last_rows = near[:, TY - 8 :] + edge[1] * ys[4, row, :]
    near = jnp.concatenate([first_rows, near[:, 8 : TY - 8], last_rows], axis=1).reshape(CELLS, 128)
    ohi, olo = split(one)
    nhi, nlo = split(near)
    o = jnp.concatenate([ohi, olo], axis=1)
    n = jnp.concatenate([nhi, nlo], axis=1)
    fine = mm(o, mats[0]) + mm(ohi, mats[2, :128])
    beside = mm(n, mats[0]) + mm(o, mats[1]) + mm(jnp.concatenate([nhi, ohi], axis=1), mats[2])
    cre, cim = fine[:, :NZ].reshape(TX, TY, NZ), fine[:, NZ:].reshape(TX, TY, NZ)
    bre, bim = beside[:, :NZ].reshape(TX, TY, NZ), beside[:, NZ:].reshape(TX, TY, NZ)
    direction[0] = local[0] + cre
    direction[1] = local[1] + cim
    dre = 5.5 - masks[0].astype(F32)
    dim = absorb[...]
    ire = part[0] + (dre * cre - dim * cim - bre)
    iim = part[1] + (dre * cim + dim * cre - bim)
    image[0] = ire
    image[1] = iim
    rre, rim = res[0], res[1]

    def total(v):
        return jnp.sum(jnp.sum(v, axis=(0, 1)).reshape(1, NZ), axis=1, keepdims=True)

    lane1 = iota((1, 128), 1)
    dots = jnp.where(lane1 == f, total(ire * rre + iim * rim), 0.0)
    dots = dots + jnp.where(lane1 == f + 8, total(ire * rim - iim * rre), 0.0)
    dots = dots + jnp.where(lane1 == f + 16, total(ire * ire + iim * iim), 0.0)
    acc[6:7, :] = acc[6:7, :] + dots
    if not last:
        acc[row, :] = restrict_rows(ire, iim, pe[...], rows[...])
        for c, value in ((0, ire), (1, iim)):
            inner[2 * f + c], outer[2 * f + c] = by_pairs(pack_low(value), pack_high(value))
        for copy in sent(f):
            copy.start()

    @pl.when(f == FIELDS - 1)
    def _():
        if last:
            pay[...] = jnp.broadcast_to(acc[6:7, :], pay.shape)
        else:
            pay[...] = jnp.broadcast_to(acc[...][None], pay.shape)
            copy = pltpu.make_async_copy(pay, pay_far, sems.at[2 * FIELDS])
            copy.start()
            for i in range(FIELDS):
                for other in sent(i):
                    other.wait()
            copy.wait()


def image_call(last, ys, pe, dlow, dhigh, dleft, dright, depth, masks, absorb, res, local, part):
    edge_y = channel(lambda f: 16, 4, 8, NZ)
    edge_x = slab_of(lambda f: 8)
    cells = fields(TX, TY, NZ)
    pay = (TILES, 128) if last else (TILES, 8, 128)
    out_specs = [cells, cells, fixed(*pay) if last else anywhere()]
    scratch = []
    out_shape = [(shape if last else far_shape)(12, TX, TY, NZ), shape(12, TX, TY, NZ), (shape if last else far_shape)(*pay)]
    if not last:
        out_specs += [anywhere()] * 2
        out_shape += [far_shape(12, 4, 8, NZ)] * 2
        scratch = [pltpu.VMEM(pay, F32)] + [pltpu.VMEM((12, 4, 8, NZ), F32)] * 2
        scratch.append(pltpu.SemaphoreType.DMA((2 * FIELDS + 1,)))
    return pl.pallas_call(
        functools.partial(image_kernel, last),
        grid=(FIELDS,),
        in_specs=[fixed(5, 8, 128)]
        + [fixed(CELLS, 128), edge_y, edge_y, edge_x, edge_x, fixed(8, NZ)]
        + [channel(lambda f: f // 2, TX, TY, NZ), fixed(TX, TY, NZ), cells, cells, cells],
        out_specs=out_specs,
        out_shape=out_shape,
        scratch_shapes=[
            pltpu.VMEM((3, 256, 256), BF16),
            pltpu.VMEM((256, 256), BF16),
            pltpu.VMEM((2, TX, 8, 128), F32),
            pltpu.VMEM((2, TY, 128), F32),
            pltpu.VMEM((8, 128), F32),
        ] + scratch,
        compiler_params=params(),
        name="image",
    )(ys, pe, dlow, dhigh, dleft, dright, depth, masks, absorb, res, local, part)


def finish_kernel(every, alpha, dir1, dir2, res, img, solution, residual, two):
    f = pl.program_id(0)

    @pl.when(f == 0)
    def _():
        are, aim = alphas(jnp.sum(every[...], axis=0, keepdims=True))
        two[:8] = are
        two[8:] = aim

    are, aim = alpha[pl.ds(f, 1), :], alpha[pl.ds(f + 8, 1), :]
    bre, bim = two[pl.ds(f, 1), :], two[pl.ds(f + 8, 1), :]
    sre, sim = complex_times(are, aim, dir1[0], dir1[1])
    tre, tim = complex_times(bre, bim, dir2[0], dir2[1])
    solution[0] = sre + tre
    solution[1] = sim + tim
    pre, pim = complex_times(bre, bim, img[0], img[1])
    residual[0] = res[0] - pre
    residual[1] = res[1] - pim


def finish(every, alpha, dir1, dir2, res, img):
    cells = fields(TX, TY, NZ)
    return pl.pallas_call(
        finish_kernel,
        grid=(FIELDS,),
        in_specs=[fixed(TILES, 128), fixed(16, 128), cells, cells, cells, cells],
        out_specs=[cells, cells],
        out_shape=[shape(12, TX, TY, NZ)] * 2,
        scratch_shapes=[pltpu.VMEM((16, 128), F32)],
        compiler_params=params(),
        name="finish",
    )(every, alpha, dir1, dir2, res, img)


def swap_pairs(value):
    return lax.ppermute(value, "gy", [(i, i ^ 1) for i in range(GY)])


def swap_between(value):
    ends = [(i, i + 1) for i in range(1, GY - 1, 2)]
    return lax.ppermute(value, "gy", ends + [(j, i) for i, j in ends])


def gather(copies, axes=BOTH):
    return lax.all_to_all(copies, axes, 0, 0, tiled=True)


def swap_cores(value):
    return lax.ppermute(value, "gx", [(i, i ^ 1) for i in range(GX)])


def swap_chips(value):
    ends = [(i, i + 1) for i in range(1, GX - 1, 2)]
    return lax.ppermute(value, "gx", ends + [(j, i) for i, j in ends])


def round_x(value, k):
    return lax.ppermute(value, "gx", [(i, (i + 2 * k) % GX) for i in range(GX)])


def after(value, *others):
    return lax.optimization_barrier((value, *others))[0]


def on_device(sources, masks, absorption, plane_basis, depth_basis, coupling_blocks, coupling_index):
    src = sources.reshape(12, TX, TY, NZ)
    blocks = coupling_blocks.reshape(NNZ, 128, 128)
    index = coupling_index.reshape(-1)

    y0b, pe, inner, outer = first(src, masks, absorption, plane_basis, depth_basis, blocks)
    all0 = gather(y0b)
    inner0, outer0 = swap_pairs(inner), swap_between(outer)
    rows = [blocks] + [round_x(blocks, k) for k in (1, 2, 3)]
    y1b = tile_sweep(index, all0, blocks)
    all1 = gather(y1b)
    for_core, for_chip, low0, high0 = slabs(src, masks, absorption, after(pe, y1b), inner0, outer0, rows)
    core0, chip0 = swap_cores(for_core), swap_chips(for_chip)
    y2b = first_column(index, after(all1, core0, chip0), all0, rows, core0)
    all2 = gather(y2b, "gy").reshape(TILES, 8, 128)
    local, part = local_solve(
        src, low0, high0, after(core0, all2), chip0, masks, absorption, low0, high0, core0, chip0
    )
    ys = last_sweep(first_last_kernel, index, after(all2, part), all0, blocks, core0, inner0, outer0)
    dir1, img1, pay, inner, outer = image_call(
        False, ys, pe, low0, high0, core0, chip0, depth_basis, masks, absorption, src, local, part
    )

    all3 = gather(pay)
    inner1, outer1 = swap_pairs(inner), swap_between(outer)
    y1b, y0, alpha, own, theirs = restart(index, all3, all0, rows, core0)
    all1 = gather(y1b, "gy").reshape(TILES, 8, 128)
    res, low, high, for_core, for_chip = update(src, img1, alpha, low0, high0, inner1, outer1)
    by_core, by_chip = swap_cores(for_core), swap_chips(for_chip)
    y2b = column_call(index, after(all1, by_core, by_chip), y0, own, theirs)
    all2 = gather(y2b, "gy").reshape(TILES, 8, 128)
    local, part = local_solve(res, low, high, after(by_core, all2), by_chip, masks, absorption, low0, high0, core0, chip0)
    ys = last_sweep(later_last_kernel, index, after(all2, part), y0, own, theirs, inner0, outer0)
    dir2, img2, pay = image_call(
        True, ys, pe, low0, high0, core0, chip0, depth_basis, masks, absorption, res, local, part
    )
    all3 = gather(pay)
    solution, residual = finish(all3, alpha, dir1, dir2, res, img2)
    return solution.reshape(sources.shape), residual.reshape(sources.shape)


def solution(mesh):
    return jax.shard_map(
        on_device,
        mesh=mesh,
        in_specs=(
            P(None, None, None, "gx", "gy", None),
            P(None, "gx", "gy", None),
            P("gx", "gy", None),
            P(None, "gx", "gy"),
            P(),
            P("gx", "gy", None, None, None),
            P(),
        ),
        out_specs=(P(None, None, None, "gx", "gy", None), P(None, None, None, "gx", "gy", None)),
        check_vma=False,
    )
```

```python
import functools

import jax
import jax.numpy as jnp
from jax import lax
from jax.experimental import pallas as pl
from jax.experimental.pallas import tpu as pltpu
from jax.sharding import PartitionSpec as P

F32 = jnp.float32
BF16 = jnp.bfloat16
TX, TY, NZ = 8, 32, 128
CELLS = TX * TY
GX, GY = 8, 16
TILES = GX * GY
NNZ = 5
FIELDS = 6
VMEM = 12 * 1024 * 1024
EDGES = (25, 4, 16, NZ)
BOTH = ("gx", "gy")


def params(**more):
    return pltpu.CompilerParams(vmem_limit_bytes=VMEM, **more)


def iota(shape, dim):
    return lax.broadcasted_iota(jnp.int32, shape, dim)


def split(x):
    hi = x.astype(BF16)
    return hi, (x - hi.astype(F32)).astype(BF16)


def mm(a, b):
    return lax.dot_general(a, b, (((1,), (0,)), ((), ())), preferred_element_type=F32)


def mm_nt(a, b):
    return lax.dot_general(a, b, (((1,), (1,)), ((), ())), preferred_element_type=F32)


def depth_matrix(depth):
    tall = jnp.concatenate([depth] * 8, axis=0)
    none = jnp.zeros_like(tall)
    return jnp.concatenate(
        [jnp.concatenate([tall, none], axis=1), jnp.concatenate([none, tall], axis=1)], axis=0
    )


def restrict_rows(re, im, pe, rows):
    cells = jnp.concatenate([re.reshape(CELLS, NZ), im.reshape(CELLS, NZ)], axis=1)
    hi, lo = split(cells)
    both = mm_nt(hi, rows)
    part = both[:, :128] + both[:, 128:] + mm_nt(lo, rows[:128])
    return jnp.sum(pe * part, axis=0, keepdims=True)


def pack_low(cells):
    sub = iota((4, 8, NZ), 1)
    return jnp.where(sub < 4, cells[0:4, 0:8], pltpu.roll(cells[4:8, 0:8], 4, 1))


def pack_high(cells):
    sub = iota((4, 8, NZ), 1)
    return jnp.where(sub >= 4, cells[0:4, 24:32], pltpu.roll(cells[4:8, 24:32], 4, 1))


def halo_rows(low, high, x):
    sub = iota((8, NZ), 0)
    if x < 4:
        return jnp.where(sub < 4, low[x], high[x])
    return jnp.where(sub < 4, pltpu.roll(low[x - 4], 4, 0), pltpu.roll(high[x - 4], 4, 0))


def wide_plane(cells, low, high, x):
    return jnp.concatenate([cells[x], halo_rows(low, high, x)], axis=0)


def even_row():
    return lax.axis_index("gy") % 2 == 0


def by_pairs(to_last, to_next):
    even = even_row()
    return jnp.where(even, to_next, to_last), jnp.where(even, to_last, to_next)


def first_kernel(
    src_far, masks_far, absorb_far, plane_far, depth_far, blocks_far, y0b_far, pe, in_far, out_far, y0_far,
    src, masks, absorb, plane, depth, blocks, y0b, inner, outer, rows, y0, sems,
):
    copies = []
    for f in range(FIELDS):
        two = pl.ds(2 * f, 2)
        copies.append(pltpu.make_async_copy(src_far.at[two], src.at[two], sems.at[f]))
    rest = ((masks_far, masks), (absorb_far, absorb), (plane_far, plane), (depth_far, depth), (blocks_far, blocks))
    for i, (there, here) in enumerate(rest):
        copies.append(pltpu.make_async_copy(there, here, sems.at[FIELDS + i]))
    for copy in copies[::-1]:
        copy.start()
    copies[FIELDS + 2].wait()
    copies[FIELDS + 3].wait()

    pick = (iota((8, 128), 1) // 8) % 8 == iota((8, 128), 0)
    pick = jnp.where(pick, 1.0, 0.0)
    picks = jnp.concatenate([pick] * 3, axis=0).astype(BF16)
    for x in range(TX):
        p = plane[:, x, :]
        hi = p.astype(BF16).astype(F32)
        mid = (p - hi).astype(BF16).astype(F32)
        low = p - hi - mid
        parts = jnp.concatenate([hi, mid, low], axis=0).astype(BF16)
        pe[x * TY : (x + 1) * TY, :] = lax.dot_general(
            parts, picks, (((0,), (0,)), ((), ())), preferred_element_type=F32
        )
    hi, lo = split(depth_matrix(depth[...]))
    rows[...] = jnp.concatenate([hi, lo], axis=0)
    y0[...] = jnp.zeros_like(y0)

    def edges(re, im):
        low = jnp.concatenate([pack_low(re), pack_low(im)], axis=1)
        high = jnp.concatenate([pack_high(re), pack_high(im)], axis=1)
        return by_pairs(low, high)

    def put(refs, at, values):
        for ref, value in zip(refs, values):
            hi, lo = split(value)
            ref[at[0]] = hi
            if len(at) > 1:
                ref[at[1]] = lo

    refs = (inner, outer)
    for f in range(FIELDS):
        copies[f].wait()
        re, im = src[2 * f], src[2 * f + 1]
        y0[f : f + 1, :] = restrict_rows(re, im, pe[...], rows[...])
        put(refs, (f, FIELDS + f), edges(re, im))
    y0b[...] = jnp.broadcast_to(y0[...].astype(BF16)[None], y0b.shape)
    results = [
        pltpu.make_async_copy(y0b, y0b_far, sems.at[FIELDS + 5]),
        pltpu.make_async_copy(y0, y0_far, sems.at[FIELDS + 8]),
    ]
    results[0].start()
    results[1].start()
    copies[FIELDS].wait()
    copies[FIELDS + 1].wait()
    put(refs, (12,), edges(masks[0].astype(F32), masks[1].astype(F32)))
    put(refs, (13,), edges(masks[2].astype(F32), absorb[...]))
    copies[FIELDS + 4].wait()
    ends = by_pairs(pe[pl.ds(0, TX, stride=TY), :], pe[pl.ds(TY - 1, TX, stride=TY), :])
    for ref, end in zip(refs, ends):
        hi = end.astype(BF16).astype(F32)
        ref[14] = jnp.zeros((4, 16, NZ), BF16)
        ref[14, 0] = jnp.concatenate([hi, end - hi], axis=0).astype(BF16)
        for j in range(NNZ):
            ref[15 + 2 * j : 17 + 2 * j] = blocks[j].reshape(2, 4, 16, 128)
    results.append(pltpu.make_async_copy(inner, in_far, sems.at[FIELDS + 6]))
    results.append(pltpu.make_async_copy(outer, out_far, sems.at[FIELDS + 7]))
    results[2].start()
    results[3].start()
    for copy in results:
        copy.wait()


def fixed(*shape):
    return pl.BlockSpec(shape, lambda f: (0,) * len(shape))


def fields(*shape):
    return pl.BlockSpec((2,) + shape, lambda f: (f,) + (0,) * len(shape))


def whole():
    return pl.BlockSpec(memory_space=pltpu.VMEM)


def shape(*dims, dtype=F32):
    return jax.ShapeDtypeStruct(dims, dtype)


def far_shape(*dims, dtype=F32):
    return pltpu.HBM(dims, dtype)


def far(value):
    return pltpu.with_memory_space_constraint(value, pltpu.HBM)


def anywhere():
    return pl.BlockSpec(memory_space=pl.ANY)


def first(src, masks, absorb, plane, depth, blocks):
    return pl.pallas_call(
        first_kernel,
        in_specs=[anywhere()] * 6,
        out_specs=[anywhere(), whole()] + [anywhere()] * 3,
        out_shape=[far_shape(TILES, 8, 128, dtype=BF16), shape(CELLS, 128)]
        + [far_shape(*EDGES, dtype=BF16)] * 2
        + [far_shape(8, 128)],
        scratch_shapes=[
            pltpu.VMEM((12, TX, TY, NZ), F32),
            pltpu.VMEM((3, TX, TY, NZ), jnp.int32),
            pltpu.VMEM((TX, TY, NZ), F32),
            pltpu.VMEM((8, TX, TY), F32),
            pltpu.VMEM((8, NZ), F32),
            pltpu.VMEM((NNZ, 128, 128), BF16),
            pltpu.VMEM((TILES, 8, 128), BF16),
            pltpu.VMEM(EDGES, BF16),
            pltpu.VMEM(EDGES, BF16),
            pltpu.VMEM((256, 256), BF16),
            pltpu.VMEM((8, 128), F32),
            pltpu.SemaphoreType.DMA((FIELDS + 9,)),
        ],
        compiler_params=params(),
        name="first",
    )(far(src), far(masks), far(absorb), far(plane), far(depth), far(blocks))


def anywhere():
    return pl.BlockSpec(memory_space=pl.ANY)


SLAB = 2 * (TY + 8)


def slab_plane(re, im, re_halo, im_halo):
    return jnp.concatenate([re, im, re_halo, im_halo], axis=0).astype(BF16)


def slab_part(slab, i, c):
    start = c * TY if isinstance(c, int) else pl.multiple_of(c * TY, TY)
    own = slab[i, pl.ds(start, TY), :].astype(F32)
    halo = slab[i, 2 * TY :, :].astype(F32)
    return jnp.concatenate([own, jnp.where(c == 1, halo[8:], halo[:8])], axis=0)


def own_core():
    return lax.axis_index("gx") % 2


def fill_sides(fill, core_out, chip_out):
    @pl.when(own_core() == 0)
    def _():
        fill(core_out, TX - 3)
        fill(chip_out, 0)

    @pl.when(own_core() == 1)
    def _():
        fill(core_out, 0)
        fill(chip_out, TX - 3)


def slabs_kernel(src, masks, absorb, pe, inner, outer, b0, b1, b2, b3, core_out, chip_out, low, high):
    even = even_row()
    for pair in range(8):
        sides = []
        for ref in (inner, outer):
            value = ref[pair].astype(F32) if pair < FIELDS else ref[FIELDS + pair].astype(F32)
            sides.append(value + ref[FIELDS + pair].astype(F32) if pair < FIELDS else value)
        for out, value in ((low, jnp.where(even, sides[0], sides[1])), (high, jnp.where(even, sides[1], sides[0]))):
            out[2 * pair] = value[:, :8]
            out[2 * pair + 1] = value[:, 8:]
    ends = [ref[14, 0].astype(F32) for ref in (inner, outer)]
    ends = [end[:8] + end[8:] for end in ends]
    for out, value in ((low, jnp.where(even, *ends)), (high, jnp.where(even, *ends[::-1]))):
        out[16] = jnp.zeros((4, 8, NZ), F32)
        out[16, 0] = value

    def halo(ch, x):
        return halo_rows(low[ch], high[ch], x)

    def fill(out, start):
        for i in range(3):
            x = start + i
            for f in range(FIELDS):
                a, b = 2 * f, 2 * f + 1
                out[3 * f + i] = slab_plane(src[a, x], src[b, x], halo(a, x), halo(b, x))
            out[18 + i] = slab_plane(masks[0, x].astype(F32), masks[1, x].astype(F32), halo(12, x), halo(13, x))
            out[21 + i] = slab_plane(masks[2, x].astype(F32), absorb[x], halo(14, x), halo(15, x))
        none = jnp.zeros((8, 128), F32)
        edge = pe[:TY] if start == 0 else pe[CELLS - TY :]
        hi = edge.astype(BF16).astype(F32)
        out[24] = slab_plane(hi, edge - hi, none, none)
        out[25] = jnp.zeros((SLAB, 128), BF16)
        out[26] = jnp.zeros((SLAB, 128), BF16)

    fill_sides(fill, core_out, chip_out)
    for k, rows in enumerate((b0, b1, b2, b3)):
        core_out[27 + 8 * k : 35 + 8 * k] = rows[...].reshape(8, SLAB, 128)


def slabs(src, masks, absorb, pe, inner, outer, rows):
    return pl.pallas_call(
        slabs_kernel,
        in_specs=[whole()] * 10,
        out_specs=[whole()] * 4,
        out_shape=[shape(59, SLAB, NZ, dtype=BF16), shape(27, SLAB, NZ, dtype=BF16)] + [shape(17, 4, 8, NZ)] * 2,
        compiler_params=params(),
        name="slabs",
    )(src, masks, absorb, pe, inner, outer, *rows)


def complex_times(are, aim, re, im):
    return are * re - aim * im, are * im + aim * re


def update_kernel(res, img, alpha, low0, high0, inner, outer, out, low, high, core_out, chip_out):
    even = even_row()
    for f in range(FIELDS):
        are = alpha[f : f + 1, :]
        aim = alpha[8 + f : 9 + f, :]
        a, b = 2 * f, 2 * f + 1
        pre, pim = complex_times(are, aim, img[a], img[b])
        out[a] = res[a] - pre
        out[b] = res[b] - pim
        pre, pim = complex_times(are, aim, *[jnp.where(even, inner[ch], outer[ch]) for ch in (a, b)])
        low[a] = low0[a] - pre
        low[b] = low0[b] - pim
        pre, pim = complex_times(are, aim, *[jnp.where(even, outer[ch], inner[ch]) for ch in (a, b)])
        high[a] = high0[a] - pre
        high[b] = high0[b] - pim

    def fill(slab, start):
        for f in range(FIELDS):
            a, b = 2 * f, 2 * f + 1
            for i in range(3):
                x = start + i
                halos = [halo_rows(low[ch], high[ch], x) for ch in (a, b)]
                slab[3 * f + i] = slab_plane(out[a, x], out[b, x], *halos)

    fill_sides(fill, core_out, chip_out)


def update(res, img, alpha, low0, high0, inner, outer):
    return pl.pallas_call(
        update_kernel,
        in_specs=[whole()] * 7,
        out_specs=[whole()] * 5,
        out_shape=[
            shape(12, TX, TY, NZ),
            shape(12, 4, 8, NZ),
            shape(12, 4, 8, NZ),
            shape(18, SLAB, NZ, dtype=BF16),
            shape(18, SLAB, NZ, dtype=BF16),
        ],
        compiler_params=params(),
        name="update",
    )(res, img, alpha, low0, high0, inner, outer)


def local_kernel(src, low, high, left, right, mask, mlow, mhigh, mleft, mright, absorb, alow, ahigh, aleft, aright,
                 local, image, inv, r, z1, z2, z3):
    lane = iota((TY + 8, NZ), 1)

    core = own_core()

    def plane(cells, lo, hi, by_core, by_chip, c, p):
        if 0 <= p < TX:
            return wide_plane(cells, lo, hi, p)
        i, by_chip_on = (p + 3, 0) if p < 0 else (p - TX, 1)
        return jnp.where(core == by_chip_on, slab_part(by_chip, i, c), slab_part(by_core, i, c))

    which = (pl.program_id(0) // 2) % 2
    for p in range(-3, TX + 3):
        i = p + 3
        if 0 <= p < TX:
            m = jnp.concatenate([mask[0, p].astype(F32), halo_rows(mlow[0], mhigh[0], p)], axis=0)
        else:
            m = plane(None, None, None, mleft, mright, which, p)
        dim = plane(absorb, alow[0], ahigh[0], aleft, aright, 1, p)
        dre = 5.5 - m
        inside = dim > 1.0
        scale = 1.0 / jnp.where(inside, dre * dre + dim * dim, 1.0)
        ire = jnp.where(inside, dre * scale, 0.0)
        iim = jnp.where(inside, -dim * scale, 0.0)
        inv[0, i] = ire
        inv[1, i] = iim
        re = plane(src[0], low[0], high[0], left, right, 0, p)
        im = plane(src[1], low[1], high[1], left, right, 1, p)
        r[0, i] = re
        r[1, i] = im
        z1[0, i], z1[1, i] = complex_times(ire, iim, re, im)

    def near(z, c, i):
        mid = z[c, i]
        total = z[c, i - 1] + z[c, i + 1]
        total = total + pltpu.roll(mid, 1, 0) + pltpu.roll(mid, TY + 7, 0)
        total = total + jnp.where(lane == 0, 0.0, pltpu.roll(mid, 1, 1))
        return total + jnp.where(lane == NZ - 1, 0.0, pltpu.roll(mid, NZ - 1, 1))

    for i in range(1, TX + 5):
        re = r[0, i] + near(z1, 0, i)
        im = r[1, i] + near(z1, 1, i)
        z2[0, i], z2[1, i] = complex_times(inv[0, i], inv[1, i], re, im)
    for i in range(2, TX + 4):
        re = r[0, i] + near(z2, 0, i)
        im = r[1, i] + near(z2, 1, i)
        zre, zim = complex_times(inv[0, i], inv[1, i], re, im)
        z3[0, i], z3[1, i] = zre, zim
        if 3 <= i < TX + 3:
            local[0, i - 3], local[1, i - 3] = zre[:TY], zim[:TY]
            image[0, i - 3], image[1, i - 3] = re[:TY], im[:TY]
    for i in range(3, TX + 3):
        for c in range(2):
            image[c, i - 3] = image[c, i - 3] - near(z3, c, i)[:TY]


def channel(offset, *dims):
    return pl.BlockSpec((1,) + dims, lambda f: (offset(f),) + (0,) * len(dims))


def slab_of(which):
    return pl.BlockSpec((3, SLAB, NZ), lambda f: (which(f), 0, 0))


def local_solve(res, low, high, left, right, masks, absorb, dlow, dhigh, dleft, dright):
    of_mask = lambda f: 12 + f // 2
    of_absorb = lambda f: 15
    y = (4, 8, NZ)
    pair, mask_pair, absorb_pair = slab_of(lambda f: f), slab_of(lambda f: 6 + f // 4), slab_of(lambda f: 7)
    planes = pltpu.VMEM((2, TX + 6, TY + 8, NZ), F32)
    return pl.pallas_call(
        local_kernel,
        grid=(FIELDS,),
        in_specs=[
            fields(TX, TY, NZ), fields(*y), fields(*y), pair, pair,
            channel(lambda f: f // 2, TX, TY, NZ),
            channel(of_mask, *y), channel(of_mask, *y), mask_pair, mask_pair,
            fixed(TX, TY, NZ),
            channel(of_absorb, *y), channel(of_absorb, *y), absorb_pair, absorb_pair,
        ],
        out_specs=[fields(TX, TY, NZ)] * 2,
        out_shape=[shape(12, TX, TY, NZ)] * 2,
        scratch_shapes=[planes] * 5,
        compiler_params=params(),
        name="local",
    )(res, low, high, left, right, masks, dlow, dhigh, dleft, dright, absorb, dlow, dhigh, dleft, dright)


def own_place():
    return lax.axis_index("gx"), lax.axis_index("gy")


def sweep(index, p, q, blocks, chosen):
    total = None
    for j in range(NNZ):
        part = mm_nt(chosen(index[(p * GY + q) * NNZ + j]), blocks[j])
        total = part if total is None else total + part
    return total


def smem():
    return pl.BlockSpec(memory_space=pltpu.SMEM)


def tile_sweep_kernel(index, every, y0, blocks, out):
    p, q = own_place()
    y = y0[...] - sweep(index, p, q, blocks, lambda t: every[t])
    out[...] = jnp.broadcast_to(y.astype(BF16)[None], out.shape)


def tile_sweep(index, every, y0, blocks):
    return pl.pallas_call(
        tile_sweep_kernel,
        in_specs=[smem()] + [whole()] * 3,
        out_specs=whole(),
        out_shape=shape(TILES, 8, 128, dtype=BF16),
        compiler_params=params(),
        name="tile_sweep",
    )(index, every, y0, blocks)


def column_place(t):
    return (t % GY) * GX + t // GY


def column_sweep(index, own, y0, chosen, rows, out):
    p, q = own_place()
    for i in range(GX):
        a = ((p // 2 + GX // 2 - i // 2) % (GX // 2)) * 2 + (p % 2 + i % 2) % 2
        y = (own if i == 0 else y0[a * GY + q].astype(F32)) - sweep(index, a, q, rows(i), chosen)
        out[:, a] = jnp.broadcast_to(y.astype(BF16)[None], (GY, 8, 128))


def packed_blocks(slab, k):
    rows = slab[8 * k : 8 * k + 8].reshape(NNZ * 128, 128)
    return [rows[128 * j : 128 * j + 128] for j in range(NNZ)]


def first_column_kernel(index, every, y0, y0_own, b0, b1, b2, b3, by_core, out):
    own = (b0, b1, b2, b3)
    theirs = by_core.at[27:59]
    column_sweep(
        index, y0_own[...], y0, lambda t: every[t], lambda i: packed_blocks(theirs, i // 2) if i % 2 else own[i // 2], out
    )


def first_column(index, every, y0, y0_own, rows, by_core):
    return pl.pallas_call(
        first_column_kernel,
        in_specs=[smem()] + [whole()] * 8,
        out_specs=whole(),
        out_shape=shape(GY, GX, 8, 128, dtype=BF16),
        compiler_params=params(),
        name="column_sweep",
    )(index, every, y0, y0_own, *rows, by_core)


def column_rows(own, theirs):
    return lambda i: packed_blocks(theirs, i // 2) if i % 2 else own.at[i // 2]


def column_sweep_kernel(index, every, y0, own, theirs, out):
    p, q = own_place()
    column_sweep(index, y0[p * GY + q], y0, lambda t: every[column_place(t)], column_rows(own, theirs), out)


def column_call(index, every, y0, own, theirs):
    return pl.pallas_call(
        column_sweep_kernel,
        in_specs=[smem()] + [whole()] * 4,
        out_specs=whole(),
        out_shape=shape(GY, GX, 8, 128, dtype=BF16),
        compiler_params=params(),
        name="column_sweep",
    )(index, every, y0, own, theirs)


def edge_blocks(edges):
    rows = edges[15:25].reshape(NNZ * 128, 128)
    return [rows[128 * j : 128 * j + 128] for j in range(NNZ)]


def last_sweep_kernel(index, every, y0, y0_own, own, theirs, inner, outer, out):
    p, q = own_place()
    take = lambda t: every[column_place(t)]
    pw, pe = jnp.maximum(p - 1, 0), jnp.minimum(p + 1, GX - 1)
    ql, qr = jnp.maximum(q - 1, 0), jnp.minimum(q + 1, GY - 1)

    def put(i, a, b, rows):
        out[i] = y0[a * GY + b].astype(F32) - sweep(index, a, b, rows, take)

    out[0] = y0_own - sweep(index, p, q, own, take)

    @pl.when(q % 2 == 0)
    def _():
        put(3, p, ql, edge_blocks(outer))
        put(4, p, qr, edge_blocks(inner))

    @pl.when(q % 2 == 1)
    def _():
        put(3, p, ql, edge_blocks(inner))
        put(4, p, qr, edge_blocks(outer))

    @pl.when(p % 2 == 0)
    def _():
        put(1, pw, q, packed_blocks(theirs, 1))
        put(2, pe, q, packed_blocks(theirs, 0))

    @pl.when(p % 2 == 1)
    def _():
        put(1, pw, q, packed_blocks(theirs, 0))
        put(2, pe, q, packed_blocks(theirs, 3))


def first_last_kernel(index, every, y0, own, by_core, inner, outer, y0_own, out):
    last_sweep_kernel(index, every, y0, y0_own[...], own, by_core.at[27:59], inner, outer, out)


def later_last_kernel(index, every, y0, own, theirs, inner, outer, out):
    p, q = own_place()
    last_sweep_kernel(index, every, y0, y0[p * GY + q], own.at[0], theirs, inner, outer, out)


def last_sweep(kernel, index, every, y0, own, theirs, inner, outer, *more):
    return pl.pallas_call(
        kernel,
        in_specs=[smem()] + [whole()] * (6 + len(more)),
        out_specs=whole(),
        out_shape=shape(5, 8, 128),
        compiler_params=params(),
        name="last_sweep",
    )(index, every, y0, own, theirs, inner, outer, *more)


def alphas(total):
    row = jnp.broadcast_to(total, (8, 128))
    sub, lane = iota((8, 128), 0), iota((8, 128), 1)

    def take(first_lane):
        return jnp.sum(jnp.where(lane == sub + first_lane, row, 0.0), axis=1, keepdims=True)

    energy = jnp.where(sub[:, :1] < FIELDS, take(16), 1.0)
    are = jnp.broadcast_to(take(0) / energy, (8, 128))
    aim = jnp.broadcast_to(take(8) / energy, (8, 128))
    return are, aim


def restart_kernel(
    index, every, before, y0_far, b0, b1, b2, b3, by_core, out, y0, alpha, own, theirs, mine, sems
):
    copies = [pltpu.make_async_copy(rows, own.at[k], sems.at[k]) for k, rows in enumerate((b0, b1, b2, b3))]
    copies.append(pltpu.make_async_copy(by_core.at[27:59], theirs, sems.at[4]))
    copies.append(pltpu.make_async_copy(y0_far, mine, sems.at[5]))
    for copy in copies[::-1]:
        copy.start()
    are, aim = alphas(jnp.sum(every[...], axis=0)[6:7])
    alpha[:8] = are
    alpha[8:] = aim
    sub, lane = iota((8, 128), 0), iota((8, 128), 1)
    are = jnp.where(sub < FIELDS, are, 0.0)
    aim = jnp.where(sub < FIELDS, jnp.where(lane < 64, -aim, aim), 0.0)

    def next_coarse(y, part):
        change = y - part
        return y - (are * change + aim * pltpu.roll(change, 64, 1))

    def coarse(t, _):
        y0[t] = next_coarse(before[t].astype(F32), every[t])

    lax.fori_loop(0, TILES, coarse, None, unroll=8)
    for copy in copies:
        copy.wait()
    p, q = own_place()
    exact = next_coarse(mine[...], every[p * GY + q])
    y0[p * GY + q] = exact
    column_sweep(index, exact, y0, lambda t: y0[t].astype(BF16), column_rows(own, theirs), out)


def restart(index, every, before, y0_own, rows, by_core):
    return pl.pallas_call(
        restart_kernel,
        in_specs=[smem()] + [whole()] * 2 + [anywhere()] * 6,
        out_specs=[whole()] * 5,
        out_shape=[
            shape(GY, GX, 8, 128, dtype=BF16),
            shape(TILES, 8, 128),
            shape(16, 128),
            shape(4, NNZ, 128, 128, dtype=BF16),
            shape(32, SLAB, 128, dtype=BF16),
        ],
        scratch_shapes=[pltpu.VMEM((8, 128), F32), pltpu.SemaphoreType.DMA((6,))],
        compiler_params=params(),
        name="restart",
    )(index, every, before, far(y0_own), *[far(row) for row in rows], far(by_core))


def image_kernel(last, ys, pe, elow, ehigh, by_core, by_chip, depth, masks, absorb, res, local, part, *refs):
    if last:
        direction, image, pay, mats, rows, edge, acc = refs
    else:
        (dir_far, img_far, pay_far, in_far, out_far, mats, rows, edge, acc,
         direction, image, pay, inner, outer, sems) = refs

    def sent(f):
        two = pl.ds(2 * f, 2)
        pairs = ((inner, in_far), (outer, out_far), (direction, dir_far), (image, img_far))
        return [pltpu.make_async_copy(a.at[two], b.at[two], sems.at[4 * f + i]) for i, (a, b) in enumerate(pairs)]

    sub8 = iota((8, NZ), 0)
    d = depth[...]
    lane = iota((8, NZ), 1)
    beside = jnp.where(lane == 0, 0.0, pltpu.roll(d, 1, 1))
    beside = beside + jnp.where(lane == NZ - 1, 0.0, pltpu.roll(d, NZ - 1, 1))
    hi, lo = split(depth_matrix(d))
    nhi, nlo = split(depth_matrix(beside))
    mats[0] = jnp.concatenate([hi, hi], axis=0)
    mats[1] = jnp.concatenate([nhi, nhi], axis=0)
    mats[2] = jnp.concatenate([lo, nlo], axis=0)
    rows[...] = jnp.concatenate([hi, lo], axis=0)
    core_side, chip_side = [s[24, :TY].astype(F32) + s[24, TY : 2 * TY].astype(F32) for s in (by_core, by_chip)]
    west_edge = jnp.where(own_core() == 0, chip_side, core_side)
    east_edge = jnp.where(own_core() == 0, core_side, chip_side)
    for x in range(TX):
        low = jnp.broadcast_to(ehigh[16, 0, x : x + 1, :], (8, 128))
        high = jnp.broadcast_to(elow[16, 0, x : x + 1, :], (8, 128))
        edge[0, x] = jnp.where(sub8 == 0, low, 0.0)
        edge[1, x] = jnp.where(sub8 == 7, high, 0.0)

    def total(v):
        return jnp.sum(jnp.sum(v, axis=(0, 1)).reshape(1, NZ), axis=1, keepdims=True)

    lane1 = iota((1, 128), 1)
    dots = jnp.zeros((1, 128), F32)
    for f in range(FIELDS):
        a, b, row = 2 * f, 2 * f + 1, slice(f, f + 1)
        one = pe[...] * ys[0, row, :]
        three = one.reshape(TX, TY, 128)
        west = (west_edge * ys[1, row, :])[None]
        east = (east_edge * ys[2, row, :])[None]
        sub = iota((TX, TY, 128), 1)
        near = jnp.concatenate([west, three[:-1]], axis=0) + jnp.concatenate([three[1:], east], axis=0)
        near = near + jnp.where(sub == 0, 0.0, pltpu.roll(three, 1, 1))
        near = near + jnp.where(sub == TY - 1, 0.0, pltpu.roll(three, TY - 1, 1))
        first_rows = near[:, :8] + edge[0] * ys[3, row, :]
        last_rows = near[:, TY - 8 :] + edge[1] * ys[4, row, :]
        near = jnp.concatenate([first_rows, near[:, 8 : TY - 8], last_rows], axis=1).reshape(CELLS, 128)
        ohi, olo = split(one)
        nhi, nlo = split(near)
        o = jnp.concatenate([ohi, olo], axis=1)
        n = jnp.concatenate([nhi, nlo], axis=1)
        fine = mm(o, mats[0]) + mm(ohi, mats[2, :128])
        beside = mm(n, mats[0]) + mm(o, mats[1]) + mm(jnp.concatenate([nhi, ohi], axis=1), mats[2])
        cre, cim = fine[:, :NZ].reshape(TX, TY, NZ), fine[:, NZ:].reshape(TX, TY, NZ)
        bre, bim = beside[:, :NZ].reshape(TX, TY, NZ), beside[:, NZ:].reshape(TX, TY, NZ)
        direction[a] = local[a] + cre
        direction[b] = local[b] + cim
        dre = 5.5 - masks[f // 2].astype(F32)
        dim = absorb[...]
        ire = part[a] + (dre * cre - dim * cim - bre)
        iim = part[b] + (dre * cim + dim * cre - bim)
        image[a] = ire
        image[b] = iim
        rre, rim = res[a], res[b]
        dots = dots + jnp.where(lane1 == f, total(ire * rre + iim * rim), 0.0)
        dots = dots + jnp.where(lane1 == f + 8, total(ire * rim - iim * rre), 0.0)
        dots = dots + jnp.where(lane1 == f + 16, total(ire * ire + iim * iim), 0.0)
        if not last:
            acc[row, :] = restrict_rows(rre - ire, rim - iim, pe[...], rows[...])
            for ch, value in ((a, ire), (b, iim)):
                inner[ch], outer[ch] = by_pairs(pack_low(value), pack_high(value))
            for copy in sent(f):
                copy.start()
    if last:
        pay[...] = jnp.broadcast_to(dots, pay.shape)
    else:
        acc[6:7, :] = dots
        acc[7:8, :] = jnp.zeros((1, 128), F32)
        pay[...] = jnp.broadcast_to(acc[...][None], pay.shape)
        copy = pltpu.make_async_copy(pay, pay_far, sems.at[4 * FIELDS])
        copy.start()
        for f in range(FIELDS):
            for other in sent(f):
                other.wait()
        copy.wait()


def image_call(last, ys, pe, dlow, dhigh, by_core, by_chip, depth, masks, absorb, res, local, part):
    cells = (12, TX, TY, NZ)
    scratch = [
        pltpu.VMEM((3, 256, 256), BF16),
        pltpu.VMEM((256, 256), BF16),
        pltpu.VMEM((2, TX, 8, 128), F32),
        pltpu.VMEM((8, 128), F32),
    ]
    if last:
        out_specs = [whole()] * 3
        out_shape = [shape(*cells), shape(*cells), shape(TILES, 128)]
    else:
        out_specs = [anywhere()] * 5
        out_shape = [far_shape(*cells), far_shape(*cells), far_shape(TILES, 8, 128)]
        out_shape += [far_shape(12, 4, 8, NZ)] * 2
        scratch += [pltpu.VMEM(cells, F32)] * 2 + [pltpu.VMEM((TILES, 8, 128), F32)]
        scratch += [pltpu.VMEM((12, 4, 8, NZ), F32)] * 2 + [pltpu.SemaphoreType.DMA((4 * FIELDS + 1,))]
    return pl.pallas_call(
        functools.partial(image_kernel, last),
        in_specs=[whole()] * 12,
        out_specs=out_specs,
        out_shape=out_shape,
        scratch_shapes=scratch,
        compiler_params=params(),
        name="image",
    )(ys, pe, dlow, dhigh, by_core, by_chip, depth, masks, absorb, res, local, part)


def finish_kernel(every, alpha, dir1, dir2, res, img, solution, residual, two):
    f = pl.program_id(0)

    @pl.when(f == 0)
    def _():
        are, aim = alphas(jnp.sum(every[...], axis=0, keepdims=True))
        two[:8] = are
        two[8:] = aim

    are, aim = alpha[pl.ds(f, 1), :], alpha[pl.ds(f + 8, 1), :]
    bre, bim = two[pl.ds(f, 1), :], two[pl.ds(f + 8, 1), :]
    sre, sim = complex_times(are, aim, dir1[0], dir1[1])
    tre, tim = complex_times(bre, bim, dir2[0], dir2[1])
    solution[0] = sre + tre
    solution[1] = sim + tim
    pre, pim = complex_times(bre, bim, img[0], img[1])
    residual[0] = res[0] - pre
    residual[1] = res[1] - pim


def finish(every, alpha, dir1, dir2, res, img):
    cells = fields(TX, TY, NZ)
    return pl.pallas_call(
        finish_kernel,
        grid=(FIELDS,),
        in_specs=[fixed(TILES, 128), fixed(16, 128), cells, cells, cells, cells],
        out_specs=[cells, cells],
        out_shape=[shape(12, TX, TY, NZ)] * 2,
        scratch_shapes=[pltpu.VMEM((16, 128), F32)],
        compiler_params=params(),
        name="finish",
    )(every, alpha, dir1, dir2, res, img)


def swap_pairs(value):
    return lax.ppermute(value, "gy", [(i, i ^ 1) for i in range(GY)])


def swap_between(value):
    ends = [(i, i + 1) for i in range(1, GY - 1, 2)]
    return lax.ppermute(value, "gy", ends + [(j, i) for i, j in ends])


def gather(copies, axes=BOTH):
    return lax.all_to_all(copies, axes, 0, 0, tiled=True)


def swap_cores(value):
    return lax.ppermute(value, "gx", [(i, i ^ 1) for i in range(GX)])


def swap_chips(value):
    ends = [(i, i + 1) for i in range(1, GX - 1, 2)]
    return lax.ppermute(value, "gx", ends + [(j, i) for i, j in ends])


def round_x(value, k):
    return lax.ppermute(value, "gx", [(i, (i + 2 * k) % GX) for i in range(GX)])


def after(value, *others):
    return lax.optimization_barrier((value, *others))[0]


def on_device(sources, masks, absorption, plane_basis, depth_basis, coupling_blocks, coupling_index):
    src = sources.reshape(12, TX, TY, NZ)
    blocks = coupling_blocks.reshape(NNZ, 128, 128)
    index = coupling_index.reshape(-1)

    y0b, pe, inner, outer, y0_own = first(src, masks, absorption, plane_basis, depth_basis, blocks)
    all0 = gather(y0b)
    inner0, outer0 = swap_pairs(inner), swap_between(outer)
    rows = [blocks] + [round_x(blocks, k) for k in (1, 2, 3)]
    y1b = tile_sweep(index, all0, y0_own, blocks)
    all1 = gather(after(y1b, *rows))
    for_core, for_chip, low0, high0 = slabs(src, masks, absorption, after(pe, all1), inner0, outer0, rows)
    core0, chip0 = swap_cores(for_core), swap_chips(for_chip)
    y2b = first_column(index, all1, all0, y0_own, rows, core0)
    all2 = gather(y2b, "gy").reshape(TILES, 8, 128)
    local, part = local_solve(
        src, low0, high0, after(core0, all2), chip0, masks, absorption, low0, high0, core0, chip0
    )
    ys = last_sweep(first_last_kernel, index, after(all2, part), all0, blocks, core0, inner0, outer0, y0_own)
    dir1, img1, pay, inner, outer = image_call(
        False, ys, pe, low0, high0, core0, chip0, depth_basis, masks, absorption, src, local, part
    )

    all3 = gather(pay)
    inner1, outer1 = swap_pairs(inner), swap_between(outer)
    y1b, y0, alpha, own, theirs = restart(index, all3, all0, y0_own, rows, core0)
    all1 = gather(y1b, "gy").reshape(TILES, 8, 128)
    res, low, high, for_core, for_chip = update(src, img1, alpha, low0, high0, inner1, outer1)
    by_core, by_chip = swap_cores(for_core), swap_chips(for_chip)
    y2b = column_call(index, after(all1, by_core, by_chip), y0, own, theirs)
    all2 = gather(y2b, "gy").reshape(TILES, 8, 128)
    local, part = local_solve(res, low, high, after(by_core, all2), by_chip, masks, absorption, low0, high0, core0, chip0)
    ys = last_sweep(later_last_kernel, index, after(all2, part), y0, own, theirs, inner0, outer0)
    dir2, img2, pay = image_call(
        True, ys, pe, low0, high0, core0, chip0, depth_basis, masks, absorption, res, local, part
    )
    all3 = gather(pay)
    solution, residual = finish(all3, alpha, dir1, dir2, res, img2)
    return solution.reshape(sources.shape), residual.reshape(sources.shape)


def solution(mesh):
    return jax.shard_map(
        on_device,
        mesh=mesh,
        in_specs=(
            P(None, None, None, "gx", "gy", None),
            P(None, "gx", "gy", None),
            P("gx", "gy", None),
            P(None, "gx", "gy"),
            P(),
            P("gx", "gy", None, None, None),
            P(),
        ),
        out_specs=(P(None, None, None, "gx", "gy", None), P(None, None, None, "gx", "gy", None)),
        check_vma=False,
    )
```

```python
import functools

import jax
import jax.numpy as jnp
from jax import lax
from jax.experimental import pallas as pl
from jax.experimental.pallas import tpu as pltpu
from jax.sharding import PartitionSpec as P

F32 = jnp.float32
BF16 = jnp.bfloat16
TX, TY, NZ = 8, 32, 128
CELLS = TX * TY
GX, GY = 8, 16
TILES = GX * GY
NNZ = 5
FIELDS = 6
VMEM = 12 * 1024 * 1024
EDGES = (25, 4, 16, NZ)
BOTH = ("gx", "gy")


def params(**more):
    return pltpu.CompilerParams(vmem_limit_bytes=VMEM, **more)


def iota(shape, dim):
    return lax.broadcasted_iota(jnp.int32, shape, dim)


def split(x):
    hi = x.astype(BF16)
    return hi, (x - hi.astype(F32)).astype(BF16)


def mm(a, b):
    return lax.dot_general(a, b, (((1,), (0,)), ((), ())), preferred_element_type=F32)


def mm_nt(a, b):
    return lax.dot_general(a, b, (((1,), (1,)), ((), ())), preferred_element_type=F32)


def depth_matrix(depth):
    tall = jnp.concatenate([depth] * 8, axis=0)
    none = jnp.zeros_like(tall)
    return jnp.concatenate(
        [jnp.concatenate([tall, none], axis=1), jnp.concatenate([none, tall], axis=1)], axis=0
    )


def restrict_rows(re, im, pe, rows):
    cells = jnp.concatenate([re.reshape(CELLS, NZ), im.reshape(CELLS, NZ)], axis=1)
    hi, lo = split(cells)
    both = mm_nt(hi, rows)
    part = both[:, :128] + both[:, 128:] + mm_nt(lo, rows[:128])
    return jnp.sum(pe * part, axis=0, keepdims=True)


def pack_low(cells):
    sub = iota((4, 8, NZ), 1)
    return jnp.where(sub < 4, cells[0:4, 0:8], pltpu.roll(cells[4:8, 0:8], 4, 1))


def pack_high(cells):
    sub = iota((4, 8, NZ), 1)
    return jnp.where(sub >= 4, cells[0:4, 24:32], pltpu.roll(cells[4:8, 24:32], 4, 1))


def halo_rows(low, high, x):
    sub = iota((8, NZ), 0)
    if x < 4:
        return jnp.where(sub < 4, low[x], high[x])
    return jnp.where(sub < 4, pltpu.roll(low[x - 4], 4, 0), pltpu.roll(high[x - 4], 4, 0))


def wide_plane(cells, low, high, x):
    return jnp.concatenate([cells[x], halo_rows(low, high, x)], axis=0)


def even_row():
    return lax.axis_index("gy") % 2 == 0


def by_pairs(to_last, to_next):
    even = even_row()
    return jnp.where(even, to_next, to_last), jnp.where(even, to_last, to_next)


def first_kernel(
    src_far, masks_far, absorb_far, plane_far, depth_far, blocks_far, y0b_far, pe, in_far, out_far, y0_far,
    src, masks, absorb, plane, depth, blocks, y0b, inner, outer, rows, y0, sems,
):
    copies = []
    for f in range(FIELDS):
        two = pl.ds(2 * f, 2)
        copies.append(pltpu.make_async_copy(src_far.at[two], src.at[two], sems.at[f]))
    rest = ((masks_far, masks), (absorb_far, absorb), (plane_far, plane), (depth_far, depth), (blocks_far, blocks))
    for i, (there, here) in enumerate(rest):
        copies.append(pltpu.make_async_copy(there, here, sems.at[FIELDS + i]))
    for copy in copies[::-1]:
        copy.start()
    copies[FIELDS + 2].wait()
    copies[FIELDS + 3].wait()

    pick = (iota((8, 128), 1) // 8) % 8 == iota((8, 128), 0)
    pick = jnp.where(pick, 1.0, 0.0)
    picks = jnp.concatenate([pick] * 3, axis=0).astype(BF16)
    for x in range(TX):
        p = plane[:, x, :]
        hi = p.astype(BF16).astype(F32)
        mid = (p - hi).astype(BF16).astype(F32)
        low = p - hi - mid
        parts = jnp.concatenate([hi, mid, low], axis=0).astype(BF16)
        pe[x * TY : (x + 1) * TY, :] = lax.dot_general(
            parts, picks, (((0,), (0,)), ((), ())), preferred_element_type=F32
        )
    hi, lo = split(depth_matrix(depth[...]))
    rows[...] = jnp.concatenate([hi, lo], axis=0)
    y0[...] = jnp.zeros_like(y0)

    def edges(re, im):
        low = jnp.concatenate([pack_low(re), pack_low(im)], axis=1)
        high = jnp.concatenate([pack_high(re), pack_high(im)], axis=1)
        return by_pairs(low, high)

    def put(refs, at, values):
        for ref, value in zip(refs, values):
            hi, lo = split(value)
            ref[at[0]] = hi
            if len(at) > 1:
                ref[at[1]] = lo

    refs = (inner, outer)
    for f in range(FIELDS):
        copies[f].wait()
        re, im = src[2 * f], src[2 * f + 1]
        y0[f : f + 1, :] = restrict_rows(re, im, pe[...], rows[...])
        put(refs, (f, FIELDS + f), edges(re, im))
    y0b[...] = jnp.broadcast_to(y0[...].astype(BF16)[None], y0b.shape)
    results = [
        pltpu.make_async_copy(y0b, y0b_far, sems.at[FIELDS + 5]),
        pltpu.make_async_copy(y0, y0_far, sems.at[FIELDS + 8]),
    ]
    results[0].start()
    results[1].start()
    copies[FIELDS].wait()
    copies[FIELDS + 1].wait()
    put(refs, (12,), edges(masks[0].astype(F32), masks[1].astype(F32)))
    put(refs, (13,), edges(masks[2].astype(F32), absorb[...]))
    copies[FIELDS + 4].wait()
    ends = by_pairs(pe[pl.ds(0, TX, stride=TY), :], pe[pl.ds(TY - 1, TX, stride=TY), :])
    for ref, end in zip(refs, ends):
        hi = end.astype(BF16).astype(F32)
        ref[14] = jnp.zeros((4, 16, NZ), BF16)
        ref[14, 0] = jnp.concatenate([hi, end - hi], axis=0).astype(BF16)
        for j in range(NNZ):
            ref[15 + 2 * j : 17 + 2 * j] = blocks[j].reshape(2, 4, 16, 128)
    results.append(pltpu.make_async_copy(inner, in_far, sems.at[FIELDS + 6]))
    results.append(pltpu.make_async_copy(outer, out_far, sems.at[FIELDS + 7]))
    results[2].start()
    results[3].start()
    for copy in results:
        copy.wait()


def fixed(*shape):
    return pl.BlockSpec(shape, lambda f: (0,) * len(shape))


def fields(*shape):
    return pl.BlockSpec((2,) + shape, lambda f: (f,) + (0,) * len(shape))


def whole():
    return pl.BlockSpec(memory_space=pltpu.VMEM)


def shape(*dims, dtype=F32):
    return jax.ShapeDtypeStruct(dims, dtype)


def far_shape(*dims, dtype=F32):
    return pltpu.HBM(dims, dtype)


def far(value):
    return pltpu.with_memory_space_constraint(value, pltpu.HBM)


def anywhere():
    return pl.BlockSpec(memory_space=pl.ANY)


def first(src, masks, absorb, plane, depth, blocks):
    return pl.pallas_call(
        first_kernel,
        in_specs=[anywhere()] * 6,
        out_specs=[anywhere(), whole()] + [anywhere()] * 3,
        out_shape=[far_shape(TILES, 8, 128, dtype=BF16), shape(CELLS, 128)]
        + [far_shape(*EDGES, dtype=BF16)] * 2
        + [far_shape(8, 128)],
        scratch_shapes=[
            pltpu.VMEM((12, TX, TY, NZ), F32),
            pltpu.VMEM((3, TX, TY, NZ), jnp.int32),
            pltpu.VMEM((TX, TY, NZ), F32),
            pltpu.VMEM((8, TX, TY), F32),
            pltpu.VMEM((8, NZ), F32),
            pltpu.VMEM((NNZ, 128, 128), BF16),
            pltpu.VMEM((TILES, 8, 128), BF16),
            pltpu.VMEM(EDGES, BF16),
            pltpu.VMEM(EDGES, BF16),
            pltpu.VMEM((256, 256), BF16),
            pltpu.VMEM((8, 128), F32),
            pltpu.SemaphoreType.DMA((FIELDS + 9,)),
        ],
        compiler_params=params(),
        name="first",
    )(far(src), far(masks), far(absorb), far(plane), far(depth), far(blocks))


def anywhere():
    return pl.BlockSpec(memory_space=pl.ANY)


SLAB = 2 * (TY + 8)


def slab_plane(re, im, re_halo, im_halo):
    return jnp.concatenate([re, im, re_halo, im_halo], axis=0).astype(BF16)


def slab_part(slab, i, c):
    start = c * TY if isinstance(c, int) else pl.multiple_of(c * TY, TY)
    own = slab[i, pl.ds(start, TY), :].astype(F32)
    halo = slab[i, 2 * TY :, :].astype(F32)
    return jnp.concatenate([own, jnp.where(c == 1, halo[8:], halo[:8])], axis=0)


def own_core():
    return lax.axis_index("gx") % 2


def fill_sides(fill, core_out, chip_out):
    @pl.when(own_core() == 0)
    def _():
        fill(core_out, TX - 3)
        fill(chip_out, 0)

    @pl.when(own_core() == 1)
    def _():
        fill(core_out, 0)
        fill(chip_out, TX - 3)


def slabs_kernel(src, masks, absorb, pe, inner, outer, b0, b1, b2, b3, core_out, chip_out, low, high):
    even = even_row()
    for pair in range(8):
        sides = []
        for ref in (inner, outer):
            value = ref[pair].astype(F32) if pair < FIELDS else ref[FIELDS + pair].astype(F32)
            sides.append(value + ref[FIELDS + pair].astype(F32) if pair < FIELDS else value)
        for out, value in ((low, jnp.where(even, sides[0], sides[1])), (high, jnp.where(even, sides[1], sides[0]))):
            out[2 * pair] = value[:, :8]
            out[2 * pair + 1] = value[:, 8:]
    ends = [ref[14, 0].astype(F32) for ref in (inner, outer)]
    ends = [end[:8] + end[8:] for end in ends]
    for out, value in ((low, jnp.where(even, *ends)), (high, jnp.where(even, *ends[::-1]))):
        out[16] = jnp.zeros((4, 8, NZ), F32)
        out[16, 0] = value

    def halo(ch, x):
        return halo_rows(low[ch], high[ch], x)

    def fill(out, start):
        for i in range(3):
            x = start + i
            for f in range(FIELDS):
                a, b = 2 * f, 2 * f + 1
                out[3 * f + i] = slab_plane(src[a, x], src[b, x], halo(a, x), halo(b, x))
            out[18 + i] = slab_plane(masks[0, x].astype(F32), masks[1, x].astype(F32), halo(12, x), halo(13, x))
            out[21 + i] = slab_plane(masks[2, x].astype(F32), absorb[x], halo(14, x), halo(15, x))
        none = jnp.zeros((8, 128), F32)
        edge = pe[:TY] if start == 0 else pe[CELLS - TY :]
        hi = edge.astype(BF16).astype(F32)
        out[24] = slab_plane(hi, edge - hi, none, none)
        out[25] = jnp.zeros((SLAB, 128), BF16)
        out[26] = jnp.zeros((SLAB, 128), BF16)

    fill_sides(fill, core_out, chip_out)
    for k, rows in enumerate((b0, b1, b2, b3)):
        core_out[27 + 8 * k : 35 + 8 * k] = rows[...].reshape(8, SLAB, 128)


def slabs(src, masks, absorb, pe, inner, outer, rows):
    return pl.pallas_call(
        slabs_kernel,
        in_specs=[whole()] * 10,
        out_specs=[whole()] * 4,
        out_shape=[shape(59, SLAB, NZ, dtype=BF16), shape(27, SLAB, NZ, dtype=BF16)] + [shape(17, 4, 8, NZ)] * 2,
        compiler_params=params(),
        name="slabs",
    )(src, masks, absorb, pe, inner, outer, *rows)


def complex_times(are, aim, re, im):
    return are * re - aim * im, are * im + aim * re


def update_kernel(res, img, alpha, low0, high0, inner, outer, out, low, high, core_out, chip_out):
    even = even_row()
    for f in range(FIELDS):
        are = alpha[f : f + 1, :]
        aim = alpha[8 + f : 9 + f, :]
        a, b = 2 * f, 2 * f + 1
        pre, pim = complex_times(are, aim, img[a], img[b])
        out[a] = res[a] - pre
        out[b] = res[b] - pim
        pre, pim = complex_times(are, aim, *[jnp.where(even, inner[ch], outer[ch]) for ch in (a, b)])
        low[a] = low0[a] - pre
        low[b] = low0[b] - pim
        pre, pim = complex_times(are, aim, *[jnp.where(even, outer[ch], inner[ch]) for ch in (a, b)])
        high[a] = high0[a] - pre
        high[b] = high0[b] - pim

    def fill(slab, start):
        for f in range(FIELDS):
            a, b = 2 * f, 2 * f + 1
            for i in range(3):
                x = start + i
                halos = [halo_rows(low[ch], high[ch], x) for ch in (a, b)]
                slab[3 * f + i] = slab_plane(out[a, x], out[b, x], *halos)

    fill_sides(fill, core_out, chip_out)


def update(res, img, alpha, low0, high0, inner, outer):
    return pl.pallas_call(
        update_kernel,
        in_specs=[whole()] * 7,
        out_specs=[whole()] * 5,
        out_shape=[
            shape(12, TX, TY, NZ),
            shape(12, 4, 8, NZ),
            shape(12, 4, 8, NZ),
            shape(18, SLAB, NZ, dtype=BF16),
            shape(18, SLAB, NZ, dtype=BF16),
        ],
        compiler_params=params(),
        name="update",
    )(res, img, alpha, low0, high0, inner, outer)


def local_kernel(src, low, high, left, right, mask, mlow, mhigh, mleft, mright, absorb, alow, ahigh, aleft, aright,
                 local, image, inv, r, z1, z2, z3):
    lane = iota((TY + 8, NZ), 1)

    core = own_core()

    def plane(cells, lo, hi, by_core, by_chip, c, p):
        if 0 <= p < TX:
            return wide_plane(cells, lo, hi, p)
        i, by_chip_on = (p + 3, 0) if p < 0 else (p - TX, 1)
        return jnp.where(core == by_chip_on, slab_part(by_chip, i, c), slab_part(by_core, i, c))

    which = (pl.program_id(0) // 2) % 2
    for p in range(-3, TX + 3):
        i = p + 3
        if 0 <= p < TX:
            m = jnp.concatenate([mask[0, p].astype(F32), halo_rows(mlow[0], mhigh[0], p)], axis=0)
        else:
            m = plane(None, None, None, mleft, mright, which, p)
        dim = plane(absorb, alow[0], ahigh[0], aleft, aright, 1, p)
        dre = 5.5 - m
        inside = dim > 1.0
        scale = 1.0 / jnp.where(inside, dre * dre + dim * dim, 1.0)
        ire = jnp.where(inside, dre * scale, 0.0)
        iim = jnp.where(inside, -dim * scale, 0.0)
        inv[0, i] = ire
        inv[1, i] = iim
        re = plane(src[0], low[0], high[0], left, right, 0, p)
        im = plane(src[1], low[1], high[1], left, right, 1, p)
        r[0, i] = re
        r[1, i] = im
        z1[0, i], z1[1, i] = complex_times(ire, iim, re, im)

    def near(z, c, i):
        mid = z[c, i]
        total = z[c, i - 1] + z[c, i + 1]
        total = total + pltpu.roll(mid, 1, 0) + pltpu.roll(mid, TY + 7, 0)
        total = total + jnp.where(lane == 0, 0.0, pltpu.roll(mid, 1, 1))
        return total + jnp.where(lane == NZ - 1, 0.0, pltpu.roll(mid, NZ - 1, 1))

    for i in range(1, TX + 5):
        re = r[0, i] + near(z1, 0, i)
        im = r[1, i] + near(z1, 1, i)
        z2[0, i], z2[1, i] = complex_times(inv[0, i], inv[1, i], re, im)
    for i in range(2, TX + 4):
        re = r[0, i] + near(z2, 0, i)
        im = r[1, i] + near(z2, 1, i)
        zre, zim = complex_times(inv[0, i], inv[1, i], re, im)
        z3[0, i], z3[1, i] = zre, zim
        if 3 <= i < TX + 3:
            local[0, i - 3], local[1, i - 3] = zre[:TY], zim[:TY]
            image[0, i - 3], image[1, i - 3] = re[:TY], im[:TY]
    for i in range(3, TX + 3):
        for c in range(2):
            image[c, i - 3] = image[c, i - 3] - near(z3, c, i)[:TY]


def channel(offset, *dims):
    return pl.BlockSpec((1,) + dims, lambda f: (offset(f),) + (0,) * len(dims))


def slab_of(which):
    return pl.BlockSpec((3, SLAB, NZ), lambda f: (which(f), 0, 0))


def local_solve(res, low, high, left, right, masks, absorb, dlow, dhigh, dleft, dright):
    of_mask = lambda f: 12 + f // 2
    of_absorb = lambda f: 15
    y = (4, 8, NZ)
    pair, mask_pair, absorb_pair = slab_of(lambda f: f), slab_of(lambda f: 6 + f // 4), slab_of(lambda f: 7)
    planes = pltpu.VMEM((2, TX + 6, TY + 8, NZ), F32)
    return pl.pallas_call(
        local_kernel,
        grid=(FIELDS,),
        in_specs=[
            fields(TX, TY, NZ), fields(*y), fields(*y), pair, pair,
            channel(lambda f: f // 2, TX, TY, NZ),
            channel(of_mask, *y), channel(of_mask, *y), mask_pair, mask_pair,
            fixed(TX, TY, NZ),
            channel(of_absorb, *y), channel(of_absorb, *y), absorb_pair, absorb_pair,
        ],
        out_specs=[fields(TX, TY, NZ)] * 2,
        out_shape=[shape(12, TX, TY, NZ)] * 2,
        scratch_shapes=[planes] * 5,
        compiler_params=params(),
        name="local",
    )(res, low, high, left, right, masks, dlow, dhigh, dleft, dright, absorb, dlow, dhigh, dleft, dright)


def own_place():
    return lax.axis_index("gx"), lax.axis_index("gy")


def sweep(index, p, q, blocks, chosen):
    total = None
    for j in range(NNZ):
        part = mm_nt(chosen(index[(p * GY + q) * NNZ + j]), blocks[j])
        total = part if total is None else total + part
    return total


def smem():
    return pl.BlockSpec(memory_space=pltpu.SMEM)


def tile_sweep_kernel(index, every, y0, blocks, out):
    p, q = own_place()
    y = y0[...] - sweep(index, p, q, blocks, lambda t: every[t])
    out[...] = jnp.broadcast_to(y.astype(BF16)[None], out.shape)


def tile_sweep(index, every, y0, blocks):
    return pl.pallas_call(
        tile_sweep_kernel,
        in_specs=[smem()] + [whole()] * 3,
        out_specs=whole(),
        out_shape=shape(TILES, 8, 128, dtype=BF16),
        compiler_params=params(),
        name="tile_sweep",
    )(index, every, y0, blocks)


def column_place(t):
    return (t % GY) * GX + t // GY


def column_sweep(index, own, y0, chosen, rows, out):
    p, q = own_place()
    for i in range(GX):
        a = ((p // 2 + GX // 2 - i // 2) % (GX // 2)) * 2 + (p % 2 + i % 2) % 2
        y = (own if i == 0 else y0[a * GY + q].astype(F32)) - sweep(index, a, q, rows(i), chosen)
        out[:, a] = jnp.broadcast_to(y.astype(BF16)[None], (GY, 8, 128))


def packed_blocks(slab, k):
    rows = slab[8 * k : 8 * k + 8].reshape(NNZ * 128, 128)
    return [rows[128 * j : 128 * j + 128] for j in range(NNZ)]


def first_column_kernel(index, every, y0, y0_own, b0, b1, b2, b3, by_core, out):
    own = (b0, b1, b2, b3)
    theirs = by_core.at[27:59]
    column_sweep(
        index, y0_own[...], y0, lambda t: every[t], lambda i: packed_blocks(theirs, i // 2) if i % 2 else own[i // 2], out
    )


def first_column(index, every, y0, y0_own, rows, by_core):
    return pl.pallas_call(
        first_column_kernel,
        in_specs=[smem()] + [whole()] * 8,
        out_specs=whole(),
        out_shape=shape(GY, GX, 8, 128, dtype=BF16),
        compiler_params=params(),
        name="column_sweep",
    )(index, every, y0, y0_own, *rows, by_core)


def column_rows(own, theirs):
    return lambda i: packed_blocks(theirs, i // 2) if i % 2 else own.at[i // 2]


def column_sweep_kernel(index, every, y0, own, theirs, out):
    p, q = own_place()
    column_sweep(index, y0[p * GY + q], y0, lambda t: every[column_place(t)], column_rows(own, theirs), out)


def column_call(index, every, y0, own, theirs):
    return pl.pallas_call(
        column_sweep_kernel,
        in_specs=[smem()] + [whole()] * 4,
        out_specs=whole(),
        out_shape=shape(GY, GX, 8, 128, dtype=BF16),
        compiler_params=params(),
        name="column_sweep",
    )(index, every, y0, own, theirs)


def edge_blocks(edges):
    rows = edges[15:25].reshape(NNZ * 128, 128)
    return [rows[128 * j : 128 * j + 128] for j in range(NNZ)]


def last_sweep_kernel(index, every, y0, y0_own, own, theirs, inner, outer, out):
    p, q = own_place()
    take = lambda t: every[column_place(t)]
    pw, pe = jnp.maximum(p - 1, 0), jnp.minimum(p + 1, GX - 1)
    ql, qr = jnp.maximum(q - 1, 0), jnp.minimum(q + 1, GY - 1)

    def put(i, a, b, rows):
        out[i] = y0[a * GY + b].astype(F32) - sweep(index, a, b, rows, take)

    out[0] = y0_own - sweep(index, p, q, own, take)

    @pl.when(q % 2 == 0)
    def _():
        put(3, p, ql, edge_blocks(outer))
        put(4, p, qr, edge_blocks(inner))

    @pl.when(q % 2 == 1)
    def _():
        put(3, p, ql, edge_blocks(inner))
        put(4, p, qr, edge_blocks(outer))

    @pl.when(p % 2 == 0)
    def _():
        put(1, pw, q, packed_blocks(theirs, 1))
        put(2, pe, q, packed_blocks(theirs, 0))

    @pl.when(p % 2 == 1)
    def _():
        put(1, pw, q, packed_blocks(theirs, 0))
        put(2, pe, q, packed_blocks(theirs, 3))


def first_last_kernel(index, every, y0, own, by_core, inner, outer, y0_own, out):
    last_sweep_kernel(index, every, y0, y0_own[...], own, by_core.at[27:59], inner, outer, out)


def later_last_kernel(index, every, y0, own, theirs, inner, outer, out):
    p, q = own_place()
    last_sweep_kernel(index, every, y0, y0[p * GY + q], own.at[0], theirs, inner, outer, out)


def last_sweep(kernel, index, every, y0, own, theirs, inner, outer, *more):
    return pl.pallas_call(
        kernel,
        in_specs=[smem()] + [whole()] * (6 + len(more)),
        out_specs=whole(),
        out_shape=shape(5, 8, 128),
        compiler_params=params(),
        name="last_sweep",
    )(index, every, y0, own, theirs, inner, outer, *more)


def alphas(total):
    row = jnp.broadcast_to(total, (8, 128))
    sub, lane = iota((8, 128), 0), iota((8, 128), 1)

    def take(first_lane):
        return jnp.sum(jnp.where(lane == sub + first_lane, row, 0.0), axis=1, keepdims=True)

    energy = jnp.where(sub[:, :1] < FIELDS, take(16), 1.0)
    are = jnp.broadcast_to(take(0) / energy, (8, 128))
    aim = jnp.broadcast_to(take(8) / energy, (8, 128))
    return are, aim


def restart_kernel(
    index, every, before, y0_far, b0, b1, b2, b3, by_core, out, y0, alpha, own, theirs, mine, sems
):
    copies = [pltpu.make_async_copy(rows, own.at[k], sems.at[k]) for k, rows in enumerate((b0, b1, b2, b3))]
    copies.append(pltpu.make_async_copy(by_core.at[27:59], theirs, sems.at[4]))
    copies.append(pltpu.make_async_copy(y0_far, mine, sems.at[5]))
    for copy in copies[::-1]:
        copy.start()
    parts = every[...].reshape(8, 16, 8, 128)
    parts = [parts[i] for i in range(8)]
    while len(parts) > 1:
        parts = [x + y for x, y in zip(parts[::2], parts[1::2])]
    are, aim = alphas(jnp.sum(parts[0], axis=0)[6:7])
    alpha[:8] = are
    alpha[8:] = aim
    sub, lane = iota((8, 128), 0), iota((8, 128), 1)
    are = jnp.where(sub < FIELDS, are, 0.0)
    aim = jnp.where(sub < FIELDS, jnp.where(lane < 64, -aim, aim), 0.0)

    def next_coarse(y, part):
        change = y - part
        return y - (are * change + aim * pltpu.roll(change, 64, 1))

    for t in range(TILES):
        y0[t] = next_coarse(before[t].astype(F32), every[t])
    for copy in copies:
        copy.wait()
    p, q = own_place()
    exact = next_coarse(mine[...], every[p * GY + q])
    y0[p * GY + q] = exact
    column_sweep(index, exact, y0, lambda t: y0[t].astype(BF16), column_rows(own, theirs), out)


def restart(index, every, before, y0_own, rows, by_core):
    return pl.pallas_call(
        restart_kernel,
        in_specs=[smem()] + [whole()] * 2 + [anywhere()] * 6,
        out_specs=[whole()] * 5,
        out_shape=[
            shape(GY, GX, 8, 128, dtype=BF16),
            shape(TILES, 8, 128),
            shape(16, 128),
            shape(4, NNZ, 128, 128, dtype=BF16),
            shape(32, SLAB, 128, dtype=BF16),
        ],
        scratch_shapes=[pltpu.VMEM((8, 128), F32), pltpu.SemaphoreType.DMA((6,))],
        compiler_params=params(),
        name="restart",
    )(index, every, before, far(y0_own), *[far(row) for row in rows], far(by_core))


def image_kernel(last, ys, pe, elow, ehigh, by_core, by_chip, depth, masks, absorb, res, local, part, *refs):
    if last:
        direction, image, pay, mats, rows, edge, acc = refs
    else:
        (dir_far, img_far, pay_far, in_far, out_far, mats, rows, edge, acc,
         direction, image, pay, inner, outer, sems) = refs

    def sent(f):
        two = pl.ds(2 * f, 2)
        pairs = ((inner, in_far), (outer, out_far), (direction, dir_far), (image, img_far))
        return [pltpu.make_async_copy(a.at[two], b.at[two], sems.at[4 * f + i]) for i, (a, b) in enumerate(pairs)]

    sub8 = iota((8, NZ), 0)
    d = depth[...]
    lane = iota((8, NZ), 1)
    beside = jnp.where(lane == 0, 0.0, pltpu.roll(d, 1, 1))
    beside = beside + jnp.where(lane == NZ - 1, 0.0, pltpu.roll(d, NZ - 1, 1))
    hi, lo = split(depth_matrix(d))
    nhi, nlo = split(depth_matrix(beside))
    mats[0] = jnp.concatenate([hi, hi], axis=0)
    mats[1] = jnp.concatenate([nhi, nhi], axis=0)
    mats[2] = jnp.concatenate([lo, nlo], axis=0)
    rows[...] = jnp.concatenate([hi, lo], axis=0)
    core_side, chip_side = [s[24, :TY].astype(F32) + s[24, TY : 2 * TY].astype(F32) for s in (by_core, by_chip)]
    west_edge = jnp.where(own_core() == 0, chip_side, core_side)
    east_edge = jnp.where(own_core() == 0, core_side, chip_side)
    for x in range(TX):
        low = jnp.broadcast_to(ehigh[16, 0, x : x + 1, :], (8, 128))
        high = jnp.broadcast_to(elow[16, 0, x : x + 1, :], (8, 128))
        edge[0, x] = jnp.where(sub8 == 0, low, 0.0)
        edge[1, x] = jnp.where(sub8 == 7, high, 0.0)

    def total(v):
        return jnp.sum(jnp.sum(v, axis=(0, 1)).reshape(1, NZ), axis=1, keepdims=True)

    lane1 = iota((1, 128), 1)
    dots = jnp.zeros((1, 128), F32)
    for f in range(FIELDS):
        a, b, row = 2 * f, 2 * f + 1, slice(f, f + 1)
        one = pe[...] * ys[0, row, :]
        three = one.reshape(TX, TY, 128)
        west = (west_edge * ys[1, row, :])[None]
        east = (east_edge * ys[2, row, :])[None]
        sub = iota((TX, TY, 128), 1)
        near = jnp.concatenate([west, three[:-1]], axis=0) + jnp.concatenate([three[1:], east], axis=0)
        near = near + jnp.where(sub == 0, 0.0, pltpu.roll(three, 1, 1))
        near = near + jnp.where(sub == TY - 1, 0.0, pltpu.roll(three, TY - 1, 1))
        first_rows = near[:, :8] + edge[0] * ys[3, row, :]
        last_rows = near[:, TY - 8 :] + edge[1] * ys[4, row, :]
        near = jnp.concatenate([first_rows, near[:, 8 : TY - 8], last_rows], axis=1).reshape(CELLS, 128)
        ohi, olo = split(one)
        nhi, nlo = split(near)
        o = jnp.concatenate([ohi, olo], axis=1)
        n = jnp.concatenate([nhi, nlo], axis=1)
        fine = mm(o, mats[0]) + mm(ohi, mats[2, :128])
        beside = mm(n, mats[0]) + mm(o, mats[1]) + mm(jnp.concatenate([nhi, ohi], axis=1), mats[2])
        cre, cim = fine[:, :NZ].reshape(TX, TY, NZ), fine[:, NZ:].reshape(TX, TY, NZ)
        bre, bim = beside[:, :NZ].reshape(TX, TY, NZ), beside[:, NZ:].reshape(TX, TY, NZ)
        direction[a] = local[a] + cre
        direction[b] = local[b] + cim
        dre = 5.5 - masks[f // 2].astype(F32)
        dim = absorb[...]
        ire = part[a] + (dre * cre - dim * cim - bre)
        iim = part[b] + (dre * cim + dim * cre - bim)
        image[a] = ire
        image[b] = iim
        rre, rim = res[a], res[b]
        dots = dots + jnp.where(lane1 == f, total(ire * rre + iim * rim), 0.0)
        dots = dots + jnp.where(lane1 == f + 8, total(ire * rim - iim * rre), 0.0)
        dots = dots + jnp.where(lane1 == f + 16, total(ire * ire + iim * iim), 0.0)
        if not last:
            acc[row, :] = restrict_rows(rre - ire, rim - iim, pe[...], rows[...])
            for ch, value in ((a, ire), (b, iim)):
                inner[ch], outer[ch] = by_pairs(pack_low(value), pack_high(value))
            for copy in sent(f):
                copy.start()
    if last:
        pay[...] = jnp.broadcast_to(dots, pay.shape)
    else:
        acc[6:7, :] = dots
        acc[7:8, :] = jnp.zeros((1, 128), F32)
        pay[...] = jnp.broadcast_to(acc[...][None], pay.shape)
        copy = pltpu.make_async_copy(pay, pay_far, sems.at[4 * FIELDS])
        copy.start()
        for f in range(FIELDS):
            for other in sent(f):
                other.wait()
        copy.wait()


def image_call(last, ys, pe, dlow, dhigh, by_core, by_chip, depth, masks, absorb, res, local, part):
    cells = (12, TX, TY, NZ)
    scratch = [
        pltpu.VMEM((3, 256, 256), BF16),
        pltpu.VMEM((256, 256), BF16),
        pltpu.VMEM((2, TX, 8, 128), F32),
        pltpu.VMEM((8, 128), F32),
    ]
    if last:
        out_specs = [whole()] * 3
        out_shape = [shape(*cells), shape(*cells), shape(TILES, 128)]
    else:
        out_specs = [anywhere()] * 5
        out_shape = [far_shape(*cells), far_shape(*cells), far_shape(TILES, 8, 128)]
        out_shape += [far_shape(12, 4, 8, NZ)] * 2
        scratch += [pltpu.VMEM(cells, F32)] * 2 + [pltpu.VMEM((TILES, 8, 128), F32)]
        scratch += [pltpu.VMEM((12, 4, 8, NZ), F32)] * 2 + [pltpu.SemaphoreType.DMA((4 * FIELDS + 1,))]
    return pl.pallas_call(
        functools.partial(image_kernel, last),
        in_specs=[whole()] * 12,
        out_specs=out_specs,
        out_shape=out_shape,
        scratch_shapes=scratch,
        compiler_params=params(),
        name="image",
    )(ys, pe, dlow, dhigh, by_core, by_chip, depth, masks, absorb, res, local, part)


def finish_kernel(every, alpha, dir1, dir2, res, img, sol_far, res_far, sol, left, sems):
    are, aim = alpha[:8], alpha[8:]
    bre, bim = alphas(jnp.sum(every[...], axis=0, keepdims=True))
    copies = []
    for f in range(FIELDS):
        a, b, row = 2 * f, 2 * f + 1, slice(f, f + 1)
        sre, sim = complex_times(are[row], aim[row], dir1[a], dir1[b])
        tre, tim = complex_times(bre[row], bim[row], dir2[a], dir2[b])
        sol[a] = sre + tre
        sol[b] = sim + tim
        pre, pim = complex_times(bre[row], bim[row], img[a], img[b])
        left[a] = res[a] - pre
        left[b] = res[b] - pim
        two = pl.ds(a, 2)
        for i, (here, there) in enumerate(((sol, sol_far), (left, res_far))):
            copies.append(pltpu.make_async_copy(here.at[two], there.at[two], sems.at[2 * f + i]))
            copies[-1].start()
    for copy in copies:
        copy.wait()


def finish(every, alpha, dir1, dir2, res, img):
    cells = (12, TX, TY, NZ)
    return pl.pallas_call(
        finish_kernel,
        in_specs=[whole()] * 6,
        out_specs=[anywhere()] * 2,
        out_shape=[far_shape(*cells)] * 2,
        scratch_shapes=[pltpu.VMEM(cells, F32)] * 2 + [pltpu.SemaphoreType.DMA((2 * FIELDS,))],
        compiler_params=params(),
        name="finish",
    )(every, alpha, dir1, dir2, res, img)


def swap_pairs(value):
    return lax.ppermute(value, "gy", [(i, i ^ 1) for i in range(GY)])


def swap_between(value):
    ends = [(i, i + 1) for i in range(1, GY - 1, 2)]
    return lax.ppermute(value, "gy", ends + [(j, i) for i, j in ends])


def gather(copies, axes=BOTH):
    return lax.all_to_all(copies, axes, 0, 0, tiled=True)


def swap_cores(value):
    return lax.ppermute(value, "gx", [(i, i ^ 1) for i in range(GX)])


def swap_chips(value):
    ends = [(i, i + 1) for i in range(1, GX - 1, 2)]
    return lax.ppermute(value, "gx", ends + [(j, i) for i, j in ends])


def round_x(value, k):
    return lax.ppermute(value, "gx", [(i, (i + 2 * k) % GX) for i in range(GX)])


def after(value, *others):
    return lax.optimization_barrier((value, *others))[0]


def on_device(sources, masks, absorption, plane_basis, depth_basis, coupling_blocks, coupling_index):
    src = sources.reshape(12, TX, TY, NZ)
    blocks = coupling_blocks.reshape(NNZ, 128, 128)
    index = coupling_index.reshape(-1)

    y0b, pe, inner, outer, y0_own = first(src, masks, absorption, plane_basis, depth_basis, blocks)
    all0 = gather(y0b)
    inner0, outer0 = swap_pairs(inner), swap_between(outer)
    rows = [blocks] + [round_x(blocks, k) for k in (1, 2, 3)]
    y1b = tile_sweep(index, all0, y0_own, blocks)
    all1 = gather(after(y1b, *rows))
    for_core, for_chip, low0, high0 = slabs(src, masks, absorption, after(pe, all1), inner0, outer0, rows)
    core0, chip0 = swap_cores(for_core), swap_chips(for_chip)
    y2b = first_column(index, all1, all0, y0_own, rows, core0)
    all2 = gather(y2b, "gy").reshape(TILES, 8, 128)
    local, part = local_solve(
        src, low0, high0, after(core0, all2), chip0, masks, absorption, low0, high0, core0, chip0
    )
    ys = last_sweep(first_last_kernel, index, after(all2, part), all0, blocks, core0, inner0, outer0, y0_own)
    dir1, img1, pay, inner, outer = image_call(
        False, ys, pe, low0, high0, core0, chip0, depth_basis, masks, absorption, src, local, part
    )

    all3 = gather(pay)
    inner1, outer1 = swap_pairs(inner), swap_between(outer)
    y1b, y0, alpha, own, theirs = restart(index, all3, all0, y0_own, rows, core0)
    all1 = gather(y1b, "gy").reshape(TILES, 8, 128)
    res, low, high, for_core, for_chip = update(src, img1, alpha, low0, high0, inner1, outer1)
    by_core, by_chip = swap_cores(for_core), swap_chips(for_chip)
    y2b = column_call(index, after(all1, by_core, by_chip), y0, own, theirs)
    all2 = gather(y2b, "gy").reshape(TILES, 8, 128)
    local, part = local_solve(res, low, high, after(by_core, all2), by_chip, masks, absorption, low0, high0, core0, chip0)
    ys = last_sweep(later_last_kernel, index, after(all2, part), y0, own, theirs, inner0, outer0)
    dir2, img2, pay = image_call(
        True, ys, pe, low0, high0, core0, chip0, depth_basis, masks, absorption, res, local, part
    )
    all3 = gather(pay)
    solution, residual = finish(all3, alpha, dir1, dir2, res, img2)
    return solution.reshape(sources.shape), residual.reshape(sources.shape)


def solution(mesh):
    return jax.shard_map(
        on_device,
        mesh=mesh,
        in_specs=(
            P(None, None, None, "gx", "gy", None),
            P(None, "gx", "gy", None),
            P("gx", "gy", None),
            P(None, "gx", "gy"),
            P(),
            P("gx", "gy", None, None, None),
            P(),
        ),
        out_specs=(P(None, None, None, "gx", "gy", None), P(None, None, None, "gx", "gy", None)),
        check_vma=False,
    )
```

```python
import functools

import jax
import jax.numpy as jnp
from jax import lax
from jax.experimental import pallas as pl
from jax.experimental.pallas import tpu as pltpu
from jax.sharding import PartitionSpec as P

F32 = jnp.float32
BF16 = jnp.bfloat16
TX, TY, NZ = 8, 32, 128
CELLS = TX * TY
GX, GY = 8, 16
TILES = GX * GY
NNZ = 5
FIELDS = 6
VMEM = 12 * 1024 * 1024
EDGES = (25, 4, 16, NZ)
BOTH = ("gx", "gy")


def params(**more):
    return pltpu.CompilerParams(vmem_limit_bytes=VMEM, **more)


def iota(shape, dim):
    return lax.broadcasted_iota(jnp.int32, shape, dim)


def split(x):
    hi = x.astype(BF16)
    return hi, (x - hi.astype(F32)).astype(BF16)


def mm(a, b):
    return lax.dot_general(a, b, (((1,), (0,)), ((), ())), preferred_element_type=F32)


def mm_nt(a, b):
    return lax.dot_general(a, b, (((1,), (1,)), ((), ())), preferred_element_type=F32)


def depth_matrix(depth):
    tall = jnp.concatenate([depth] * 8, axis=0)
    none = jnp.zeros_like(tall)
    return jnp.concatenate(
        [jnp.concatenate([tall, none], axis=1), jnp.concatenate([none, tall], axis=1)], axis=0
    )


def restrict_rows(re, im, pe, rows):
    cells = jnp.concatenate([re.reshape(CELLS, NZ), im.reshape(CELLS, NZ)], axis=1)
    hi, lo = split(cells)
    both = mm_nt(hi, rows)
    part = both[:, :128] + both[:, 128:] + mm_nt(lo, rows[:128])
    return jnp.sum(pe * part, axis=0, keepdims=True)


def pack_low(cells):
    sub = iota((4, 8, NZ), 1)
    return jnp.where(sub < 4, cells[0:4, 0:8], pltpu.roll(cells[4:8, 0:8], 4, 1))


def pack_high(cells):
    sub = iota((4, 8, NZ), 1)
    return jnp.where(sub >= 4, cells[0:4, 24:32], pltpu.roll(cells[4:8, 24:32], 4, 1))


def halo_rows(low, high, x):
    sub = iota((8, NZ), 0)
    if x < 4:
        return jnp.where(sub < 4, low[x], high[x])
    return jnp.where(sub < 4, pltpu.roll(low[x - 4], 4, 0), pltpu.roll(high[x - 4], 4, 0))


def wide_plane(cells, low, high, x):
    return jnp.concatenate([cells[x], halo_rows(low, high, x)], axis=0)


def even_row():
    return lax.axis_index("gy") % 2 == 0


def by_pairs(to_last, to_next):
    even = even_row()
    return jnp.where(even, to_next, to_last), jnp.where(even, to_last, to_next)


def first_kernel(
    src_far, masks_far, absorb_far, plane_far, depth_far, blocks_far, y0b_far, pe, in_far, out_far, y0_far,
    src, masks, absorb, plane, depth, blocks, y0b, inner, outer, rows, y0, sems,
):
    copies = []
    for f in range(FIELDS):
        two = pl.ds(2 * f, 2)
        copies.append(pltpu.make_async_copy(src_far.at[two], src.at[two], sems.at[f]))
    rest = ((masks_far, masks), (absorb_far, absorb), (plane_far, plane), (depth_far, depth), (blocks_far, blocks))
    for i, (there, here) in enumerate(rest):
        copies.append(pltpu.make_async_copy(there, here, sems.at[FIELDS + i]))
    for copy in copies[::-1]:
        copy.start()
    copies[FIELDS + 2].wait()
    copies[FIELDS + 3].wait()

    pick = (iota((8, 128), 1) // 8) % 8 == iota((8, 128), 0)
    pick = jnp.where(pick, 1.0, 0.0)
    picks = jnp.concatenate([pick] * 3, axis=0).astype(BF16)
    for x in range(TX):
        p = plane[:, x, :]
        hi = p.astype(BF16).astype(F32)
        mid = (p - hi).astype(BF16).astype(F32)
        low = p - hi - mid
        parts = jnp.concatenate([hi, mid, low], axis=0).astype(BF16)
        pe[x * TY : (x + 1) * TY, :] = lax.dot_general(
            parts, picks, (((0,), (0,)), ((), ())), preferred_element_type=F32
        )
    hi, lo = split(depth_matrix(depth[...]))
    rows[...] = jnp.concatenate([hi, lo], axis=0)
    y0[...] = jnp.zeros_like(y0)

    def edges(re, im):
        low = jnp.concatenate([pack_low(re), pack_low(im)], axis=1)
        high = jnp.concatenate([pack_high(re), pack_high(im)], axis=1)
        return by_pairs(low, high)

    def put(refs, at, values):
        for ref, value in zip(refs, values):
            hi, lo = split(value)
            ref[at[0]] = hi
            if len(at) > 1:
                ref[at[1]] = lo

    refs = (inner, outer)
    for f in range(FIELDS):
        copies[f].wait()
        re, im = src[2 * f], src[2 * f + 1]
        y0[f : f + 1, :] = restrict_rows(re, im, pe[...], rows[...])
        put(refs, (f, FIELDS + f), edges(re, im))
    y0b[...] = jnp.broadcast_to(y0[...].astype(BF16)[None], y0b.shape)
    results = [
        pltpu.make_async_copy(y0b, y0b_far, sems.at[FIELDS + 5]),
        pltpu.make_async_copy(y0, y0_far, sems.at[FIELDS + 8]),
    ]
    results[0].start()
    results[1].start()
    copies[FIELDS].wait()
    copies[FIELDS + 1].wait()
    put(refs, (12,), edges(masks[0].astype(F32), masks[1].astype(F32)))
    put(refs, (13,), edges(masks[2].astype(F32), absorb[...]))
    copies[FIELDS + 4].wait()
    ends = by_pairs(pe[pl.ds(0, TX, stride=TY), :], pe[pl.ds(TY - 1, TX, stride=TY), :])
    for ref, end in zip(refs, ends):
        hi = end.astype(BF16).astype(F32)
        ref[14] = jnp.zeros((4, 16, NZ), BF16)
        ref[14, 0] = jnp.concatenate([hi, end - hi], axis=0).astype(BF16)
        for j in range(NNZ):
            ref[15 + 2 * j : 17 + 2 * j] = blocks[j].reshape(2, 4, 16, 128)
    results.append(pltpu.make_async_copy(inner, in_far, sems.at[FIELDS + 6]))
    results.append(pltpu.make_async_copy(outer, out_far, sems.at[FIELDS + 7]))
    results[2].start()
    results[3].start()
    for copy in results:
        copy.wait()


def fixed(*shape):
    return pl.BlockSpec(shape, lambda f: (0,) * len(shape))


def fields(*shape):
    return pl.BlockSpec((2,) + shape, lambda f: (f,) + (0,) * len(shape))


def whole():
    return pl.BlockSpec(memory_space=pltpu.VMEM)


def shape(*dims, dtype=F32):
    return jax.ShapeDtypeStruct(dims, dtype)


def far_shape(*dims, dtype=F32):
    return pltpu.HBM(dims, dtype)


def far(value):
    return pltpu.with_memory_space_constraint(value, pltpu.HBM)


def anywhere():
    return pl.BlockSpec(memory_space=pl.ANY)


def first(src, masks, absorb, plane, depth, blocks):
    return pl.pallas_call(
        first_kernel,
        in_specs=[anywhere()] * 6,
        out_specs=[anywhere(), whole()] + [anywhere()] * 3,
        out_shape=[far_shape(TILES, 8, 128, dtype=BF16), shape(CELLS, 128)]
        + [far_shape(*EDGES, dtype=BF16)] * 2
        + [far_shape(8, 128)],
        scratch_shapes=[
            pltpu.VMEM((12, TX, TY, NZ), F32),
            pltpu.VMEM((3, TX, TY, NZ), jnp.int32),
            pltpu.VMEM((TX, TY, NZ), F32),
            pltpu.VMEM((8, TX, TY), F32),
            pltpu.VMEM((8, NZ), F32),
            pltpu.VMEM((NNZ, 128, 128), BF16),
            pltpu.VMEM((TILES, 8, 128), BF16),
            pltpu.VMEM(EDGES, BF16),
            pltpu.VMEM(EDGES, BF16),
            pltpu.VMEM((256, 256), BF16),
            pltpu.VMEM((8, 128), F32),
            pltpu.SemaphoreType.DMA((FIELDS + 9,)),
        ],
        compiler_params=params(),
        name="first",
    )(far(src), far(masks), far(absorb), far(plane), far(depth), far(blocks))


def anywhere():
    return pl.BlockSpec(memory_space=pl.ANY)


SLAB = 2 * (TY + 8)


def slab_plane(re, im, re_halo, im_halo):
    return jnp.concatenate([re, im, re_halo, im_halo], axis=0).astype(BF16)


def slab_part(slab, i, c):
    start = c * TY if isinstance(c, int) else pl.multiple_of(c * TY, TY)
    own = slab[i, pl.ds(start, TY), :].astype(F32)
    halo = slab[i, 2 * TY :, :].astype(F32)
    return jnp.concatenate([own, jnp.where(c == 1, halo[8:], halo[:8])], axis=0)


def own_core():
    return lax.axis_index("gx") % 2


def fill_sides(fill, core_out, chip_out):
    @pl.when(own_core() == 0)
    def _():
        fill(core_out, TX - 3)
        fill(chip_out, 0)

    @pl.when(own_core() == 1)
    def _():
        fill(core_out, 0)
        fill(chip_out, TX - 3)


def slabs_kernel(src, masks, absorb, pe, inner, outer, b0, b1, b2, b3, core_out, chip_out, low, high):
    even = even_row()
    for pair in range(8):
        sides = []
        for ref in (inner, outer):
            value = ref[pair].astype(F32) if pair < FIELDS else ref[FIELDS + pair].astype(F32)
            sides.append(value + ref[FIELDS + pair].astype(F32) if pair < FIELDS else value)
        for out, value in ((low, jnp.where(even, sides[0], sides[1])), (high, jnp.where(even, sides[1], sides[0]))):
            out[2 * pair] = value[:, :8]
            out[2 * pair + 1] = value[:, 8:]
    ends = [ref[14, 0].astype(F32) for ref in (inner, outer)]
    ends = [end[:8] + end[8:] for end in ends]
    for out, value in ((low, jnp.where(even, *ends)), (high, jnp.where(even, *ends[::-1]))):
        out[16] = jnp.zeros((4, 8, NZ), F32)
        out[16, 0] = value

    def halo(ch, x):
        return halo_rows(low[ch], high[ch], x)

    def fill(out, start):
        for i in range(3):
            x = start + i
            for f in range(FIELDS):
                a, b = 2 * f, 2 * f + 1
                out[3 * f + i] = slab_plane(src[a, x], src[b, x], halo(a, x), halo(b, x))
            out[18 + i] = slab_plane(masks[0, x].astype(F32), masks[1, x].astype(F32), halo(12, x), halo(13, x))
            out[21 + i] = slab_plane(masks[2, x].astype(F32), absorb[x], halo(14, x), halo(15, x))
        none = jnp.zeros((8, 128), F32)
        edge = pe[:TY] if start == 0 else pe[CELLS - TY :]
        hi = edge.astype(BF16).astype(F32)
        out[24] = slab_plane(hi, edge - hi, none, none)
        out[25] = jnp.zeros((SLAB, 128), BF16)
        out[26] = jnp.zeros((SLAB, 128), BF16)

    fill_sides(fill, core_out, chip_out)
    for k, rows in enumerate((b0, b1, b2, b3)):
        core_out[27 + 8 * k : 35 + 8 * k] = rows[...].reshape(8, SLAB, 128)


def slabs(src, masks, absorb, pe, inner, outer, rows):
    return pl.pallas_call(
        slabs_kernel,
        in_specs=[whole()] * 10,
        out_specs=[whole()] * 4,
        out_shape=[shape(59, SLAB, NZ, dtype=BF16), shape(27, SLAB, NZ, dtype=BF16)] + [shape(17, 4, 8, NZ)] * 2,
        compiler_params=params(),
        name="slabs",
    )(src, masks, absorb, pe, inner, outer, *rows)


def complex_times(are, aim, re, im):
    return are * re - aim * im, are * im + aim * re


def update_kernel(res, img, alpha, low0, high0, inner, outer, out, low, high, core_out, chip_out):
    even = even_row()
    for f in range(FIELDS):
        are = alpha[f : f + 1, :]
        aim = alpha[8 + f : 9 + f, :]
        a, b = 2 * f, 2 * f + 1
        pre, pim = complex_times(are, aim, img[a], img[b])
        out[a] = res[a] - pre
        out[b] = res[b] - pim
        pre, pim = complex_times(are, aim, *[jnp.where(even, inner[ch], outer[ch]) for ch in (a, b)])
        low[a] = low0[a] - pre
        low[b] = low0[b] - pim
        pre, pim = complex_times(are, aim, *[jnp.where(even, outer[ch], inner[ch]) for ch in (a, b)])
        high[a] = high0[a] - pre
        high[b] = high0[b] - pim

    def fill(slab, start):
        for f in range(FIELDS):
            a, b = 2 * f, 2 * f + 1
            for i in range(3):
                x = start + i
                halos = [halo_rows(low[ch], high[ch], x) for ch in (a, b)]
                slab[3 * f + i] = slab_plane(out[a, x], out[b, x], *halos)

    fill_sides(fill, core_out, chip_out)


def update(res, img, alpha, low0, high0, inner, outer):
    return pl.pallas_call(
        update_kernel,
        in_specs=[whole()] * 7,
        out_specs=[whole()] * 5,
        out_shape=[
            shape(12, TX, TY, NZ),
            shape(12, 4, 8, NZ),
            shape(12, 4, 8, NZ),
            shape(18, SLAB, NZ, dtype=BF16),
            shape(18, SLAB, NZ, dtype=BF16),
        ],
        compiler_params=params(),
        name="update",
    )(res, img, alpha, low0, high0, inner, outer)


def local_kernel(src, low, high, left, right, mask, mlow, mhigh, mleft, mright, absorb, alow, ahigh, aleft, aright,
                 local, image, inv, r, z1, z2, z3):
    lane = iota((TY + 8, NZ), 1)

    core = own_core()

    def plane(cells, lo, hi, by_core, by_chip, c, p):
        if 0 <= p < TX:
            return wide_plane(cells, lo, hi, p)
        i, by_chip_on = (p + 3, 0) if p < 0 else (p - TX, 1)
        return jnp.where(core == by_chip_on, slab_part(by_chip, i, c), slab_part(by_core, i, c))

    which = pl.program_id(0) % 2
    for p in range(-3, TX + 3):
        i = p + 3
        if 0 <= p < TX:
            m = jnp.concatenate([mask[0, p].astype(F32), halo_rows(mlow[0], mhigh[0], p)], axis=0)
        else:
            m = plane(None, None, None, mleft, mright, which, p)
        dim = plane(absorb, alow[0], ahigh[0], aleft, aright, 1, p)
        dre = 5.5 - m
        inside = dim > 1.0
        scale = 1.0 / jnp.where(inside, dre * dre + dim * dim, 1.0)
        inv[0, i] = jnp.where(inside, dre * scale, 0.0)
        inv[1, i] = jnp.where(inside, -dim * scale, 0.0)

    def near(z, c, i):
        mid = z[c, i]
        total = z[c, i - 1] + z[c, i + 1]
        total = total + pltpu.roll(mid, 1, 0) + pltpu.roll(mid, TY + 7, 0)
        total = total + jnp.where(lane == 0, 0.0, pltpu.roll(mid, 1, 1))
        return total + jnp.where(lane == NZ - 1, 0.0, pltpu.roll(mid, NZ - 1, 1))

    for s in range(2):
        u, w = 2 * s, 2 * s + 1
        sides = left.at[3 * s : 3 * s + 3], right.at[3 * s : 3 * s + 3]
        for p in range(-3, TX + 3):
            i = p + 3
            re = plane(src[u], low[u], high[u], *sides, 0, p)
            im = plane(src[w], low[w], high[w], *sides, 1, p)
            r[0, i] = re
            r[1, i] = im
            z1[0, i], z1[1, i] = complex_times(inv[0, i], inv[1, i], re, im)
        for i in range(1, TX + 5):
            re = r[0, i] + near(z1, 0, i)
            im = r[1, i] + near(z1, 1, i)
            z2[0, i], z2[1, i] = complex_times(inv[0, i], inv[1, i], re, im)
        for i in range(2, TX + 4):
            re = r[0, i] + near(z2, 0, i)
            im = r[1, i] + near(z2, 1, i)
            zre, zim = complex_times(inv[0, i], inv[1, i], re, im)
            z3[0, i], z3[1, i] = zre, zim
            if 3 <= i < TX + 3:
                local[u, i - 3], local[w, i - 3] = zre[:TY], zim[:TY]
                image[u, i - 3], image[w, i - 3] = re[:TY], im[:TY]
        for i in range(3, TX + 3):
            for c in range(2):
                image[u + c, i - 3] = image[u + c, i - 3] - near(z3, c, i)[:TY]


def channel(offset, *dims):
    return pl.BlockSpec((1,) + dims, lambda f: (offset(f),) + (0,) * len(dims))


def slab_of(which):
    return pl.BlockSpec((3, SLAB, NZ), lambda f: (which(f), 0, 0))


def four(*shape):
    return pl.BlockSpec((4,) + shape, lambda f: (f,) + (0,) * len(shape))


def local_solve(res, low, high, left, right, masks, absorb, dlow, dhigh, dleft, dright):
    of_mask = lambda f: 12 + f
    of_absorb = lambda f: 15
    y = (4, 8, NZ)
    pair = pl.BlockSpec((6, SLAB, NZ), lambda f: (f, 0, 0))
    mask_pair, absorb_pair = slab_of(lambda f: 6 + f // 2), slab_of(lambda f: 7)
    planes = pltpu.VMEM((2, TX + 6, TY + 8, NZ), F32)
    return pl.pallas_call(
        local_kernel,
        grid=(3,),
        in_specs=[
            four(TX, TY, NZ), four(*y), four(*y), pair, pair,
            channel(lambda f: f, TX, TY, NZ),
            channel(of_mask, *y), channel(of_mask, *y), mask_pair, mask_pair,
            fixed(TX, TY, NZ),
            channel(of_absorb, *y), channel(of_absorb, *y), absorb_pair, absorb_pair,
        ],
        out_specs=[four(TX, TY, NZ)] * 2,
        out_shape=[shape(12, TX, TY, NZ)] * 2,
        scratch_shapes=[planes] * 5,
        compiler_params=params(),
        name="local",
    )(res, low, high, left, right, masks, dlow, dhigh, dleft, dright, absorb, dlow, dhigh, dleft, dright)


def own_place():
    return lax.axis_index("gx"), lax.axis_index("gy")


def sweep(index, p, q, blocks, chosen):
    total = None
    for j in range(NNZ):
        part = mm_nt(chosen(index[(p * GY + q) * NNZ + j]), blocks[j])
        total = part if total is None else total + part
    return total


def smem():
    return pl.BlockSpec(memory_space=pltpu.SMEM)


def tile_sweep_kernel(index, every, y0, blocks, out):
    p, q = own_place()
    y = y0[...] - sweep(index, p, q, blocks, lambda t: every[t])
    out[...] = jnp.broadcast_to(y.astype(BF16)[None], out.shape)


def tile_sweep(index, every, y0, blocks):
    return pl.pallas_call(
        tile_sweep_kernel,
        in_specs=[smem()] + [whole()] * 3,
        out_specs=whole(),
        out_shape=shape(TILES, 8, 128, dtype=BF16),
        compiler_params=params(),
        name="tile_sweep",
    )(index, every, y0, blocks)


def column_place(t):
    return (t % GY) * GX + t // GY


def column_sweep(index, own, y0, chosen, rows, out):
    p, q = own_place()
    for i in range(GX):
        a = ((p // 2 + GX // 2 - i // 2) % (GX // 2)) * 2 + (p % 2 + i % 2) % 2
        y = (own if i == 0 else y0[a * GY + q].astype(F32)) - sweep(index, a, q, rows(i), chosen)
        out[:, a] = jnp.broadcast_to(y.astype(BF16)[None], (GY, 8, 128))


def packed_blocks(slab, k):
    rows = slab[8 * k : 8 * k + 8].reshape(NNZ * 128, 128)
    return [rows[128 * j : 128 * j + 128] for j in range(NNZ)]


def first_column_kernel(index, every, y0, y0_own, b0, b1, b2, b3, by_core, out):
    own = (b0, b1, b2, b3)
    theirs = by_core.at[27:59]
    column_sweep(
        index, y0_own[...], y0, lambda t: every[t], lambda i: packed_blocks(theirs, i // 2) if i % 2 else own[i // 2], out
    )


def first_column(index, every, y0, y0_own, rows, by_core):
    return pl.pallas_call(
        first_column_kernel,
        in_specs=[smem()] + [whole()] * 8,
        out_specs=whole(),
        out_shape=shape(GY, GX, 8, 128, dtype=BF16),
        compiler_params=params(),
        name="column_sweep",
    )(index, every, y0, y0_own, *rows, by_core)


def column_rows(own, theirs):
    return lambda i: packed_blocks(theirs, i // 2) if i % 2 else own.at[i // 2]


def column_sweep_kernel(index, every, y0, own, theirs, out):
    p, q = own_place()
    column_sweep(index, y0[p * GY + q], y0, lambda t: every[column_place(t)], column_rows(own, theirs), out)


def column_call(index, every, y0, own, theirs):
    return pl.pallas_call(
        column_sweep_kernel,
        in_specs=[smem()] + [whole()] * 4,
        out_specs=whole(),
        out_shape=shape(GY, GX, 8, 128, dtype=BF16),
        compiler_params=params(),
        name="column_sweep",
    )(index, every, y0, own, theirs)


def edge_blocks(edges):
    rows = edges[15:25].reshape(NNZ * 128, 128)
    return [rows[128 * j : 128 * j + 128] for j in range(NNZ)]


def last_sweep_kernel(index, every, y0, y0_own, own, theirs, inner, outer, out):
    p, q = own_place()
    take = lambda t: every[column_place(t)]
    pw, pe = jnp.maximum(p - 1, 0), jnp.minimum(p + 1, GX - 1)
    ql, qr = jnp.maximum(q - 1, 0), jnp.minimum(q + 1, GY - 1)

    def put(i, a, b, rows):
        out[i] = y0[a * GY + b].astype(F32) - sweep(index, a, b, rows, take)

    out[0] = y0_own - sweep(index, p, q, own, take)

    @pl.when(q % 2 == 0)
    def _():
        put(3, p, ql, edge_blocks(outer))
        put(4, p, qr, edge_blocks(inner))

    @pl.when(q % 2 == 1)
    def _():
        put(3, p, ql, edge_blocks(inner))
        put(4, p, qr, edge_blocks(outer))

    @pl.when(p % 2 == 0)
    def _():
        put(1, pw, q, packed_blocks(theirs, 1))
        put(2, pe, q, packed_blocks(theirs, 0))

    @pl.when(p % 2 == 1)
    def _():
        put(1, pw, q, packed_blocks(theirs, 0))
        put(2, pe, q, packed_blocks(theirs, 3))


def first_last_kernel(index, every, y0, own, by_core, inner, outer, y0_own, out):
    last_sweep_kernel(index, every, y0, y0_own[...], own, by_core.at[27:59], inner, outer, out)


def later_last_kernel(index, every, y0, own, theirs, inner, outer, out):
    p, q = own_place()
    last_sweep_kernel(index, every, y0, y0[p * GY + q], own.at[0], theirs, inner, outer, out)


def last_sweep(kernel, index, every, y0, own, theirs, inner, outer, *more):
    return pl.pallas_call(
        kernel,
        in_specs=[smem()] + [whole()] * (6 + len(more)),
        out_specs=whole(),
        out_shape=shape(5, 8, 128),
        compiler_params=params(),
        name="last_sweep",
    )(index, every, y0, own, theirs, inner, outer, *more)


def alphas(total):
    row = jnp.broadcast_to(total, (8, 128))
    sub, lane = iota((8, 128), 0), iota((8, 128), 1)

    def take(first_lane):
        return jnp.sum(jnp.where(lane == sub + first_lane, row, 0.0), axis=1, keepdims=True)

    energy = jnp.where(sub[:, :1] < FIELDS, take(16), 1.0)
    are = jnp.broadcast_to(take(0) / energy, (8, 128))
    aim = jnp.broadcast_to(take(8) / energy, (8, 128))
    return are, aim


def restart_kernel(
    index, every, before, y0_far, b0, b1, b2, b3, by_core, out, y0, alpha, own, theirs, mine, sems
):
    copies = [pltpu.make_async_copy(rows, own.at[k], sems.at[k]) for k, rows in enumerate((b0, b1, b2, b3))]
    copies.append(pltpu.make_async_copy(by_core.at[27:59], theirs, sems.at[4]))
    copies.append(pltpu.make_async_copy(y0_far, mine, sems.at[5]))
    for copy in copies[::-1]:
        copy.start()
    parts = every[...].reshape(8, 16, 8, 128)
    parts = [parts[i] for i in range(8)]
    while len(parts) > 1:
        parts = [x + y for x, y in zip(parts[::2], parts[1::2])]
    are, aim = alphas(jnp.sum(parts[0], axis=0)[6:7])
    alpha[:8] = are
    alpha[8:] = aim
    sub, lane = iota((8, 128), 0), iota((8, 128), 1)
    are = jnp.where(sub < FIELDS, are, 0.0)
    aim = jnp.where(sub < FIELDS, jnp.where(lane < 64, -aim, aim), 0.0)

    def next_coarse(y, part):
        change = y - part
        return y - (are * change + aim * pltpu.roll(change, 64, 1))

    for t in range(TILES):
        y0[t] = next_coarse(before[t].astype(F32), every[t])
    for copy in copies:
        copy.wait()
    p, q = own_place()
    exact = next_coarse(mine[...], every[p * GY + q])
    y0[p * GY + q] = exact
    column_sweep(index, exact, y0, lambda t: y0[t].astype(BF16), column_rows(own, theirs), out)


def restart(index, every, before, y0_own, rows, by_core):
    return pl.pallas_call(
        restart_kernel,
        in_specs=[smem()] + [whole()] * 2 + [anywhere()] * 6,
        out_specs=[whole()] * 5,
        out_shape=[
            shape(GY, GX, 8, 128, dtype=BF16),
            shape(TILES, 8, 128),
            shape(16, 128),
            shape(4, NNZ, 128, 128, dtype=BF16),
            shape(32, SLAB, 128, dtype=BF16),
        ],
        scratch_shapes=[pltpu.VMEM((8, 128), F32), pltpu.SemaphoreType.DMA((6,))],
        compiler_params=params(),
        name="restart",
    )(index, every, before, far(y0_own), *[far(row) for row in rows], far(by_core))


def image_kernel(last, ys, pe, elow, ehigh, by_core, by_chip, depth, masks, absorb, res, local, part, *refs):
    if last:
        direction, image, pay, mats, rows, edge, acc = refs
    else:
        (dir_far, img_far, pay_far, in_far, out_far, mats, rows, edge, acc,
         direction, image, pay, inner, outer, sems) = refs

    def sent(f):
        two = pl.ds(2 * f, 2)
        pairs = ((inner, in_far), (outer, out_far), (direction, dir_far), (image, img_far))
        return [pltpu.make_async_copy(a.at[two], b.at[two], sems.at[4 * f + i]) for i, (a, b) in enumerate(pairs)]

    sub8 = iota((8, NZ), 0)
    d = depth[...]
    lane = iota((8, NZ), 1)
    beside = jnp.where(lane == 0, 0.0, pltpu.roll(d, 1, 1))
    beside = beside + jnp.where(lane == NZ - 1, 0.0, pltpu.roll(d, NZ - 1, 1))
    hi, lo = split(depth_matrix(d))
    nhi, nlo = split(depth_matrix(beside))
    mats[0] = jnp.concatenate([hi, hi], axis=0)
    mats[1] = jnp.concatenate([nhi, nhi], axis=0)
    mats[2] = jnp.concatenate([lo, nlo], axis=0)
    rows[...] = jnp.concatenate([hi, lo], axis=0)
    core_side, chip_side = [s[24, :TY].astype(F32) + s[24, TY : 2 * TY].astype(F32) for s in (by_core, by_chip)]
    west_edge = jnp.where(own_core() == 0, chip_side, core_side)
    east_edge = jnp.where(own_core() == 0, core_side, chip_side)
    for x in range(TX):
        low = jnp.broadcast_to(ehigh[16, 0, x : x + 1, :], (8, 128))
        high = jnp.broadcast_to(elow[16, 0, x : x + 1, :], (8, 128))
        edge[0, x] = jnp.where(sub8 == 0, low, 0.0)
        edge[1, x] = jnp.where(sub8 == 7, high, 0.0)

    def total(v):
        return jnp.sum(jnp.sum(v, axis=(0, 1)).reshape(1, NZ), axis=1, keepdims=True)

    lane1 = iota((1, 128), 1)
    dots = jnp.zeros((1, 128), F32)
    for f in range(FIELDS):
        a, b, row = 2 * f, 2 * f + 1, slice(f, f + 1)
        one = pe[...] * ys[0, row, :]
        three = one.reshape(TX, TY, 128)
        west = (west_edge * ys[1, row, :])[None]
        east = (east_edge * ys[2, row, :])[None]
        sub = iota((TX, TY, 128), 1)
        near = jnp.concatenate([west, three[:-1]], axis=0) + jnp.concatenate([three[1:], east], axis=0)
        near = near + jnp.where(sub == 0, 0.0, pltpu.roll(three, 1, 1))
        near = near + jnp.where(sub == TY - 1, 0.0, pltpu.roll(three, TY - 1, 1))
        first_rows = near[:, :8] + edge[0] * ys[3, row, :]
        last_rows = near[:, TY - 8 :] + edge[1] * ys[4, row, :]
        near = jnp.concatenate([first_rows, near[:, 8 : TY - 8], last_rows], axis=1).reshape(CELLS, 128)
        ohi, olo = split(one)
        nhi, nlo = split(near)
        o = jnp.concatenate([ohi, olo], axis=1)
        n = jnp.concatenate([nhi, nlo], axis=1)
        fine = mm(o, mats[0]) + mm(ohi, mats[2, :128])
        beside = mm(n, mats[0]) + mm(o, mats[1]) + mm(jnp.concatenate([nhi, ohi], axis=1), mats[2])
        cre, cim = fine[:, :NZ].reshape(TX, TY, NZ), fine[:, NZ:].reshape(TX, TY, NZ)
        bre, bim = beside[:, :NZ].reshape(TX, TY, NZ), beside[:, NZ:].reshape(TX, TY, NZ)
        direction[a] = local[a] + cre
        direction[b] = local[b] + cim
        dre = 5.5 - masks[f // 2].astype(F32)
        dim = absorb[...]
        ire = part[a] + (dre * cre - dim * cim - bre)
        iim = part[b] + (dre * cim + dim * cre - bim)
        image[a] = ire
        image[b] = iim
        rre, rim = res[a], res[b]
        dots = dots + jnp.where(lane1 == f, total(ire * rre + iim * rim), 0.0)
        dots = dots + jnp.where(lane1 == f + 8, total(ire * rim - iim * rre), 0.0)
        dots = dots + jnp.where(lane1 == f + 16, total(ire * ire + iim * iim), 0.0)
        if not last:
            acc[row, :] = restrict_rows(rre - ire, rim - iim, pe[...], rows[...])
            for ch, value in ((a, ire), (b, iim)):
                inner[ch], outer[ch] = by_pairs(pack_low(value), pack_high(value))
            for copy in sent(f):
                copy.start()
    if last:
        pay[...] = jnp.broadcast_to(dots, pay.shape)
    else:
        acc[6:7, :] = dots
        acc[7:8, :] = jnp.zeros((1, 128), F32)
        pay[...] = jnp.broadcast_to(acc[...][None], pay.shape)
        copy = pltpu.make_async_copy(pay, pay_far, sems.at[4 * FIELDS])
        copy.start()
        for f in range(FIELDS):
            for other in sent(f):
                other.wait()
        copy.wait()


def image_call(last, ys, pe, dlow, dhigh, by_core, by_chip, depth, masks, absorb, res, local, part):
    cells = (12, TX, TY, NZ)
    scratch = [
        pltpu.VMEM((3, 256, 256), BF16),
        pltpu.VMEM((256, 256), BF16),
        pltpu.VMEM((2, TX, 8, 128), F32),
        pltpu.VMEM((8, 128), F32),
    ]
    if last:
        out_specs = [whole()] * 3
        out_shape = [shape(*cells), shape(*cells), shape(TILES, 128)]
    else:
        out_specs = [anywhere()] * 5
        out_shape = [far_shape(*cells), far_shape(*cells), far_shape(TILES, 8, 128)]
        out_shape += [far_shape(12, 4, 8, NZ)] * 2
        scratch += [pltpu.VMEM(cells, F32)] * 2 + [pltpu.VMEM((TILES, 8, 128), F32)]
        scratch += [pltpu.VMEM((12, 4, 8, NZ), F32)] * 2 + [pltpu.SemaphoreType.DMA((4 * FIELDS + 1,))]
    return pl.pallas_call(
        functools.partial(image_kernel, last),
        in_specs=[whole()] * 12,
        out_specs=out_specs,
        out_shape=out_shape,
        scratch_shapes=scratch,
        compiler_params=params(),
        name="image",
    )(ys, pe, dlow, dhigh, by_core, by_chip, depth, masks, absorb, res, local, part)


def finish_kernel(every, alpha, dir1, dir2, res, img, sol_far, res_far, sol, left, sems):
    are, aim = alpha[:8], alpha[8:]
    bre, bim = alphas(jnp.sum(every[...], axis=0, keepdims=True))
    copies = []
    for f in range(FIELDS):
        a, b, row = 2 * f, 2 * f + 1, slice(f, f + 1)
        sre, sim = complex_times(are[row], aim[row], dir1[a], dir1[b])
        tre, tim = complex_times(bre[row], bim[row], dir2[a], dir2[b])
        sol[a] = sre + tre
        sol[b] = sim + tim
        pre, pim = complex_times(bre[row], bim[row], img[a], img[b])
        left[a] = res[a] - pre
        left[b] = res[b] - pim
        two = pl.ds(a, 2)
        for i, (here, there) in enumerate(((sol, sol_far), (left, res_far))):
            copies.append(pltpu.make_async_copy(here.at[two], there.at[two], sems.at[2 * f + i]))
            copies[-1].start()
    for copy in copies:
        copy.wait()


def finish(every, alpha, dir1, dir2, res, img):
    cells = (12, TX, TY, NZ)
    return pl.pallas_call(
        finish_kernel,
        in_specs=[whole()] * 6,
        out_specs=[anywhere()] * 2,
        out_shape=[far_shape(*cells)] * 2,
        scratch_shapes=[pltpu.VMEM(cells, F32)] * 2 + [pltpu.SemaphoreType.DMA((2 * FIELDS,))],
        compiler_params=params(),
        name="finish",
    )(every, alpha, dir1, dir2, res, img)


def swap_pairs(value):
    return lax.ppermute(value, "gy", [(i, i ^ 1) for i in range(GY)])


def swap_between(value):
    ends = [(i, i + 1) for i in range(1, GY - 1, 2)]
    return lax.ppermute(value, "gy", ends + [(j, i) for i, j in ends])


def gather(copies, axes=BOTH):
    return lax.all_to_all(copies, axes, 0, 0, tiled=True)


def swap_cores(value):
    return lax.ppermute(value, "gx", [(i, i ^ 1) for i in range(GX)])


def swap_chips(value):
    ends = [(i, i + 1) for i in range(1, GX - 1, 2)]
    return lax.ppermute(value, "gx", ends + [(j, i) for i, j in ends])


def round_x(value, k):
    return lax.ppermute(value, "gx", [(i, (i + 2 * k) % GX) for i in range(GX)])


def after(value, *others):
    return lax.optimization_barrier((value, *others))[0]


def on_device(sources, masks, absorption, plane_basis, depth_basis, coupling_blocks, coupling_index):
    src = sources.reshape(12, TX, TY, NZ)
    blocks = coupling_blocks.reshape(NNZ, 128, 128)
    index = coupling_index.reshape(-1)

    y0b, pe, inner, outer, y0_own = first(src, masks, absorption, plane_basis, depth_basis, blocks)
    all0 = gather(y0b)
    inner0, outer0 = swap_pairs(inner), swap_between(outer)
    rows = [blocks] + [round_x(blocks, k) for k in (1, 2, 3)]
    y1b = tile_sweep(index, all0, y0_own, blocks)
    all1 = gather(after(y1b, *rows))
    for_core, for_chip, low0, high0 = slabs(src, masks, absorption, after(pe, all1), inner0, outer0, rows)
    core0, chip0 = swap_cores(for_core), swap_chips(for_chip)
    y2b = first_column(index, all1, all0, y0_own, rows, core0)
    all2 = gather(y2b, "gy").reshape(TILES, 8, 128)
    local, part = local_solve(
        src, low0, high0, after(core0, all2), chip0, masks, absorption, low0, high0, core0, chip0
    )
    ys = last_sweep(first_last_kernel, index, after(all2, part), all0, blocks, core0, inner0, outer0, y0_own)
    dir1, img1, pay, inner, outer = image_call(
        False, ys, pe, low0, high0, core0, chip0, depth_basis, masks, absorption, src, local, part
    )

    all3 = gather(pay)
    inner1, outer1 = swap_pairs(inner), swap_between(outer)
    y1b, y0, alpha, own, theirs = restart(index, all3, all0, y0_own, rows, core0)
    all1 = gather(y1b, "gy").reshape(TILES, 8, 128)
    res, low, high, for_core, for_chip = update(src, img1, alpha, low0, high0, inner1, outer1)
    by_core, by_chip = swap_cores(for_core), swap_chips(for_chip)
    y2b = column_call(index, after(all1, by_core, by_chip), y0, own, theirs)
    all2 = gather(y2b, "gy").reshape(TILES, 8, 128)
    local, part = local_solve(res, low, high, after(by_core, all2), by_chip, masks, absorption, low0, high0, core0, chip0)
    ys = last_sweep(later_last_kernel, index, after(all2, part), y0, own, theirs, inner0, outer0)
    dir2, img2, pay = image_call(
        True, ys, pe, low0, high0, core0, chip0, depth_basis, masks, absorption, res, local, part
    )
    all3 = gather(pay)
    solution, residual = finish(all3, alpha, dir1, dir2, res, img2)
    return solution.reshape(sources.shape), residual.reshape(sources.shape)


def solution(mesh):
    return jax.shard_map(
        on_device,
        mesh=mesh,
        in_specs=(
            P(None, None, None, "gx", "gy", None),
            P(None, "gx", "gy", None),
            P("gx", "gy", None),
            P(None, "gx", "gy"),
            P(),
            P("gx", "gy", None, None, None),
            P(),
        ),
        out_specs=(P(None, None, None, "gx", "gy", None), P(None, None, None, "gx", "gy", None)),
        check_vma=False,
    )
```
